512 devices in a mesh: dp: 32 (over z, y_lo), tensor: 16 (over y_hi, x, core).
Axes of the slice: x: 4, y: 8 (y_hi: 2, y_lo: 4; y = y_hi * 4 + y_lo), z: 8, core: 2. Of those that a mesh axis runs over, the one named last changes fastest.
Arguments:
- states: bfloat16 [8192, 8192], P('dp'), may hold values from -6 to 6
- query_weight: bfloat16 [8192, 4096], P('tensor', 'dp'), may hold values from -0.0625 to 0.0625
- key_matrix: bfloat16 [8192, 512], P('tensor', 'dp'), may hold values from -0.0625 to 0.0625
- value_matrix: bfloat16 [8192, 512], P('tensor', 'dp'), may hold values from -0.0625 to 0.0625
- block_mask: int32 [128, 4], P('dp'), may hold values from 0 to 1, as said below
- risk_weight: float32 [128], P('dp'), may hold values from -1 to 1
- upstream: bfloat16 [8192, 4096], P('dp', 'tensor'), may hold values from -1.5 to 1.5
Outputs:
- attn_out: bfloat16 [8192, 4096], P('dp', 'tensor')
- grad_query: float32 [8192, 4096], P('dp', 'tensor')
The draws below stay inside these ranges and needn't reach their ends.
Inputs may be any that keep to these rules, and one draw needn't show every extreme that they name: `block_mask`: within each group of 4 blocks, row b is 1 exactly at the blocks on the path from the root of b's tree to b, b included; every ancestor has a lower index than its descendants.
All inputs are finite; a program needn't handle non-finite values.
Results may differ from the reference program's by a relative error of at most 0.03.
Values may be sent and summed in bfloat16 or wider, within the bound.
No kernel may reach another device: no remote copies, remote signals or barrier semaphores. Data moves between devices by JAX's collectives and lax.ppermute only.
A program may use at most 128 MiB of HBM per device.

```python
import math
import jax
import jax.numpy as jnp
import numpy as np
from jax import lax

MODEL_DIMENSION = 8192
LOCAL_QUERY_HEADS = 32
LOCAL_KEY_HEADS = 4
HEAD_DIMENSION = 128
BS = 64
TOK_DEV = 256
TOKENS = 8192


def draw_block_mask(key, part):
    key = jax.random.fold_in(key, 7)
    blocks_dev = TOK_DEV // BS
    groups = TOKENS // TOK_DEV
    raw = jax.random.randint(key, (groups, blocks_dev), 0, 1048576)
    order = jnp.arange(blocks_dev, dtype=jnp.int32)
    parents = raw % (order[None, :] + 1) - 1
    ancestry = jnp.zeros((groups, blocks_dev, blocks_dev), jnp.int32)
    for level in range(blocks_dev):
        parent_now = parents[:, level]
        safe_parent = jnp.maximum(parent_now, 0)
        parent_rows = jnp.take_along_axis(ancestry, safe_parent[:, None, None], axis=1)[:, 0, :]
        parent_rows = jnp.where(parent_now[:, None] >= 0, parent_rows, 0)
        own_row = (order == level).astype(jnp.int32)[None, :] + parent_rows
        ancestry = ancestry.at[:, level, :].set(own_row)
    return ancestry.reshape(groups * blocks_dev, blocks_dev).astype(jnp.int32)


def strengthened(result, rng, source, target, blocks, factor):
    owner, partner = [(jnp.arange(result.shape[dim]) // (result.shape[dim] // blocks)).reshape([-1 if axis == dim else 1 for axis in range(result.ndim)]) for dim in (source, target)]
    chosen = jax.random.permutation(rng, blocks)[partner]
    strong = (owner == chosen) | (owner == (partner + blocks // 2) % blocks)
    return jnp.where(strong, factor * result, result)


def block_scale(own_key, extent, cuts, low, largest):
    loudness = 1.0
    for dim, parts in cuts:
        steps = jax.random.uniform(jax.random.fold_in(jax.random.fold_in(own_key, 6), dim), (parts,), jnp.float32, low / len(cuts), largest / len(cuts))
        loudness = loudness * jnp.repeat(jnp.exp(steps), extent[dim] // parts).reshape((-1,) + (1,) * (len(extent) - 1 - dim))
    return loudness


def scatter_about(stream_key, extent, width, bound, shards=(), held_as=jnp.bfloat16):
    entries = width * jax.random.normal(stream_key, extent, jnp.float32)
    if shards:
        entries = entries * block_scale(stream_key, extent, shards, -0.22, 0.18)
    return jnp.clip(entries, -bound, bound).astype(held_as)


def noise_with(rng, extent, width, bound, cuts, heavy, held_as=jnp.bfloat16):
    values = width * jax.random.normal(rng, extent, jnp.float32)
    if cuts:
        values = values * block_scale(rng, extent, cuts, -0.22, 0.18)
    return jnp.clip(strengthened(values, jax.random.fold_in(rng, 3), *heavy), -bound, bound).astype(held_as)


def setup_inputs(seed: int = 0) -> dict:
    key_list = jax.random.split(jax.random.key(seed), 8)
    return {
        "states": noise_with(key_list[0], (TOKENS, MODEL_DIMENSION), 1.0, 6.0, ((0, 32),), (0, 1, 32, 2.75)),
        "query_weight": scatter_about(key_list[1], (MODEL_DIMENSION, LOCAL_QUERY_HEADS * HEAD_DIMENSION), MODEL_DIMENSION ** -0.5, 0.0625, ((0, 16), (1, 32))),
        "key_matrix": scatter_about(key_list[2], (MODEL_DIMENSION, LOCAL_KEY_HEADS * HEAD_DIMENSION), MODEL_DIMENSION ** -0.5, 0.0625, ((0, 16), (1, 32))),
        "value_matrix": scatter_about(key_list[3], (MODEL_DIMENSION, LOCAL_KEY_HEADS * HEAD_DIMENSION), MODEL_DIMENSION ** -0.5, 0.0625, ((0, 16), (1, 32))),
        "block_mask": draw_block_mask(jax.random.fold_in(key_list[7], 71), 0),
        "risk_weight": jnp.clip(jax.random.uniform(key_list[5], (TOKENS // BS,), jnp.float32, -1.0, 1.0) * block_scale(key_list[5], (TOKENS // BS,), ((0, 32),), -0.4, 0.0), -1.0, 1.0),
        "upstream": scatter_about(key_list[6], (TOKENS, LOCAL_QUERY_HEADS * HEAD_DIMENSION), 0.25, 1.5, ((0, 32), (1, 16))),
    }


def apply_rotary(vector, cosine_lookup, sine_lookup):
    halves = vector.shape[-1] // 2
    first_half = vector[..., :halves]
    second_half = vector[..., halves:]
    return vector * cosine_lookup + jnp.concatenate([-second_half, first_half], axis=-1) * sine_lookup

def unrotate(vector, cosine_lookup, sine_lookup):
    halves = vector.shape[-1] // 2
    first_half = vector[..., :halves]
    second_half = vector[..., halves:]
    return vector * cosine_lookup + jnp.concatenate([second_half, -first_half], axis=-1) * sine_lookup

def device_step(states, query_weight, key_matrix, value_matrix, mask_rows, risk_rows, upstream):
    sequence_length = states.shape[0]
    heads_per_group = LOCAL_QUERY_HEADS // LOCAL_KEY_HEADS
    scaling = 1.0 / math.sqrt(HEAD_DIMENSION)
    q_lin = jnp.dot(states, query_weight, preferred_element_type=jnp.float32)
    key_linear = jnp.dot(states, key_matrix, preferred_element_type=jnp.float32)
    value_linear = jnp.dot(states, value_matrix, preferred_element_type=jnp.float32)
    depths = lax.optimization_barrier(jnp.sum(mask_rows, axis=1)) - 1
    offsets = jnp.arange(BS, dtype=jnp.int32)
    places = (depths[:, None] * BS + offsets[None, :]).reshape(sequence_length)
    frequency = jnp.exp(-math.log(1000000.0) * jnp.arange(HEAD_DIMENSION // 2, dtype=jnp.float32) * 2.0 / HEAD_DIMENSION)
    angles = places.astype(jnp.float32)[:, None] * frequency[None, :]
    cosine_lookup = jnp.concatenate([jnp.cos(angles), jnp.cos(angles)], axis=-1)[:, None, :]
    sine_lookup = jnp.concatenate([jnp.sin(angles), jnp.sin(angles)], axis=-1)[:, None, :]
    queries = (apply_rotary(q_lin.reshape(sequence_length, LOCAL_QUERY_HEADS, HEAD_DIMENSION), cosine_lookup, sine_lookup) * scaling).astype(jnp.bfloat16)
    rotated_keys = apply_rotary(key_linear.reshape(sequence_length, LOCAL_KEY_HEADS, HEAD_DIMENSION), cosine_lookup, sine_lookup).astype(jnp.bfloat16)
    projected_values = value_linear.reshape(sequence_length, LOCAL_KEY_HEADS, HEAD_DIMENSION).astype(jnp.bfloat16)
    head_map = np.arange(LOCAL_QUERY_HEADS) // heads_per_group
    key_heads = rotated_keys[:, head_map].astype(jnp.float32)
    value_heads = projected_values[:, head_map].astype(jnp.float32)
    scores = jnp.einsum('qhd,khd->hqk', queries.astype(jnp.float32), key_heads)
    position = jnp.arange(sequence_length, dtype=jnp.int32)
    blocks = position // BS
    wide_mask = jnp.repeat(jnp.repeat(mask_rows, BS, axis=0), BS, axis=1) > 0
    visible = wide_mask & ((blocks[:, None] != blocks[None, :]) | (position[:, None] >= position[None, :]))
    raised = jnp.exp(jnp.where(visible[None], scores, -jnp.inf))
    attend = raised / lax.optimization_barrier(jnp.sum(raised, axis=-1, keepdims=True))
    attend_b = attend.astype(jnp.bfloat16)
    mixed = jnp.einsum('hqk,khd->qhd', attend_b.astype(jnp.float32), value_heads)
    attn_out = mixed.reshape(sequence_length, LOCAL_QUERY_HEADS * HEAD_DIMENSION).astype(jnp.bfloat16)
    token_risk = jnp.repeat(risk_rows, BS)
    weighted = (upstream.astype(jnp.float32) * token_risk[:, None]).astype(jnp.bfloat16).reshape(sequence_length, LOCAL_QUERY_HEADS, HEAD_DIMENSION)
    pressure = jnp.einsum('qhd,khd->hqk', weighted.astype(jnp.float32), value_heads)
    centre = lax.optimization_barrier(jnp.sum(attend * pressure, axis=-1, keepdims=True))
    slope = (attend * (pressure - centre)).astype(jnp.bfloat16)
    dq_rot = jnp.einsum('hqk,khd->qhd', slope.astype(jnp.float32), key_heads) * scaling
    dq_rows = unrotate(dq_rot, cosine_lookup, sine_lookup).reshape(sequence_length, LOCAL_QUERY_HEADS * HEAD_DIMENSION).astype(jnp.bfloat16)
    partial_value = jnp.dot(states.T, dq_rows, preferred_element_type=jnp.float32)
    return (attn_out, partial_value)

def reference(states, query_weight, key_matrix, value_matrix, block_mask, risk_weight, upstream):
    groups = TOKENS // TOK_DEV
    blocks_dev = TOK_DEV // BS
    state_groups = states.reshape(groups, TOK_DEV, MODEL_DIMENSION)
    mask_groups = block_mask.reshape(groups, blocks_dev, blocks_dev)
    risk_groups = risk_weight.reshape(groups, blocks_dev)
    up_groups = upstream.reshape(groups, TOK_DEV, LOCAL_QUERY_HEADS * HEAD_DIMENSION)

    def one_group(total, inputs):
        group_states, group_mask, group_risk, group_up = inputs
        attn_out, partial_value = device_step(group_states, query_weight, key_matrix, value_matrix, group_mask, group_risk, group_up)
        rounded = lax.optimization_barrier(partial_value.astype(jnp.bfloat16))
        return (total + rounded.astype(jnp.float32), attn_out)
    start_total = jnp.zeros((MODEL_DIMENSION, LOCAL_QUERY_HEADS * HEAD_DIMENSION), jnp.float32)
    grad_query, outputs = lax.scan(one_group, start_total, (state_groups, mask_groups, risk_groups, up_groups))
    return (outputs.reshape(TOKENS, LOCAL_QUERY_HEADS * HEAD_DIMENSION), grad_query)
```

```python
import math

import jax
import jax.numpy as jnp
from jax import lax
from jax.experimental import pallas as pl
from jax.experimental.pallas import tpu as pltpu
from jax.sharding import Mesh
from jax.sharding import PartitionSpec as P

HEAD = 128
BS = 64
TOK = 256
AXES = ("z", "yl", "yh", "xh", "xb", "c")
SIZES = (8, 4, 2, 2, 2, 2)
F32 = jnp.float32
BF16 = jnp.bfloat16
VMEM_LIMIT = 48 * 1024 * 1024


def params():
    return pltpu.CompilerParams(vmem_limit_bytes=VMEM_LIMIT)


def home_pairs(turn):
    pairs = []
    for z in range(8):
        for yl in range(4):
            for t in range(16):
                half = (yl % 2) ^ turn
                block = 2 * t + half
                owner = (4 * z + yl) // 2
                pairs.append(((4 * z + yl) * 16 + t, block * 16 + owner))
    return pairs


def swap(value, axis, size, offset):
    return lax.ppermute(value, axis, [(i, i ^ offset) for i in range(size)])


def cut_kernel(where_ref, states_ref, one_ref, two_ref, three_ref, sems):
    core, lane = where_ref[0], where_ref[1]
    copies = []
    for number, out in enumerate((one_ref, two_ref, three_ref)):
        other = lane ^ (number + 1)
        for part in range(4):
            start = pl.multiple_of((4 * core + part) * 1024 + other * 256, 256)
            copies.append(
                pltpu.make_async_copy(
                    states_ref.at[:, pl.ds(start, 256)],
                    out.at[:, pl.ds(256 * part, 256)],
                    sems.at[number * 4 + part],
                )
            )
    for copy in copies:
        copy.start()
    for copy in copies:
        copy.wait()


def cut(where, states):
    shape = jax.ShapeDtypeStruct((TOK, 1024), BF16)
    return pl.pallas_call(
        cut_kernel,
        out_shape=(shape,) * 3,
        in_specs=[pl.BlockSpec(memory_space=pltpu.SMEM), pl.BlockSpec(memory_space=pl.ANY)],
        out_specs=(pl.BlockSpec(memory_space=pl.ANY),) * 3,
        scratch_shapes=[pltpu.SemaphoreType.DMA((12,))],
        compiler_params=params(),
        name="cut_states",
    )(where, states)


def z_block(step, where):
    return 4 * (where[0] ^ (step // 4)) + step % 4


def token_specs():
    own = pl.BlockSpec((TOK, 256), lambda i, w: (0, 4 * z_block(i, w) + w[1]))
    near = [pl.BlockSpec((TOK, 256), lambda i, w: (0, jnp.minimum(i, 3)))] * 3
    far = pl.BlockSpec((3, TOK, 256), lambda i, w: (0, 0, jnp.maximum(i - 4, 0)))
    return [own, *near, far]


def project_kernel(where_ref, own, n1, n2, n3, far, weights, own_out, o1, o2, o3, q_acc, kv_acc):
    step = pl.program_id(0)

    @pl.when(step == 0)
    def _():
        q_acc[...] = jnp.zeros_like(q_acc)
        kv_acc[...] = jnp.zeros_like(kv_acc)

    w_q = jnp.concatenate([weights[0, 0, :256, :], weights[0, 1, :256, :]], axis=1)
    w_kv = []
    for chunk in range(2):
        base = 256 + 32 * chunk
        w_kv.append(
            jnp.concatenate(
                [
                    weights[0, 0, base : base + 16, :],
                    weights[0, 1, base : base + 16, :],
                    weights[0, 0, base + 16 : base + 32, :],
                    weights[0, 1, base + 16 : base + 32, :],
                ],
                axis=0,
            )
        )
    w_kv = jnp.concatenate(w_kv, axis=1)

    def add(tokens):
        for j, x in enumerate(tokens):
            rows = pl.ds(j * TOK, TOK)
            q_acc[rows, :] += jnp.dot(x, w_q, preferred_element_type=F32)
            kv_acc[rows, :] += lax.dot_general(
                x, w_kv, (((1,), (1,)), ((), ())), preferred_element_type=F32
            )

    @pl.when(step < 4)
    def _():
        add((own[...], n1[...], n2[...], n3[...]))

    @pl.when(step >= 4)
    def _():
        add((own[...], far[0], far[1], far[2]))

    @pl.when(step == 7)
    def _():
        for j, out in enumerate((own_out, o1, o2, o3)):
            rows = pl.ds(j * TOK, TOK)
            out[:256, :] = q_acc[rows, :].astype(out.dtype)
            out[256:, :] = kv_acc[rows, :].T.astype(out.dtype)


def project(where, states, near, far, weights):
    full = pl.BlockSpec((320, 256), lambda i, w: (0, 0))
    return pl.pallas_call(
        project_kernel,
        out_shape=(
            jax.ShapeDtypeStruct((320, 256), F32),
            jax.ShapeDtypeStruct((320, 256), BF16),
            jax.ShapeDtypeStruct((320, 256), BF16),
            jax.ShapeDtypeStruct((320, 256), BF16),
        ),
        grid_spec=pltpu.PrefetchScalarGridSpec(
            num_scalar_prefetch=1,
            grid=(8,),
            in_specs=[
                *token_specs(),
                pl.BlockSpec((1, 2, 320, 128), lambda i, w: (z_block(i, w), 0, 0, 0)),
            ],
            out_specs=[full] * 4,
            scratch_shapes=[pltpu.VMEM((4 * TOK, 256), F32), pltpu.VMEM((4 * TOK, 64), F32)],
        ),
        compiler_params=params(),
        name="project",
    )(where, states, *near, far, weights)


def attend_kernel(
    q0, q1, q2, q3, kv, visible, weighted, cos_q, sin_q, cos_k, sin_k, attn_out, dq_out
):
    scaling = 1.0 / math.sqrt(HEAD)
    k_lin = jnp.concatenate([kv[s, :32, :] for s in range(4)], axis=0)
    values = jnp.concatenate([kv[s, 32:, :] for s in range(4)], axis=0).astype(BF16)
    k1, k2 = k_lin[:64], k_lin[64:]
    ck, sk = cos_k[...], sin_k[...]
    keys = jnp.concatenate([k1 * ck - k2 * sk, k2 * ck + k1 * sk], axis=0).astype(BF16)
    seen = visible[...] > 0
    cq, sq = cos_q[...], sin_q[...]
    for head in range(2):
        cols = pl.ds(head * HEAD, HEAD)
        q_lin = q0[:256, cols]
        for part in (q1, q2, q3):
            q_lin = q_lin + part[:256, cols].astype(F32)
        queries = ((q_lin * cq + pltpu.roll(q_lin, 64, 1) * sq) * scaling).astype(BF16)
        scores = jnp.dot(queries, keys, preferred_element_type=F32)
        raised = jnp.where(seen, jnp.exp(scores), 0.0)
        attend = raised / jnp.sum(raised, axis=1, keepdims=True)
        mixed = lax.dot_general(
            attend.astype(BF16), values, (((1,), (1,)), ((), ())), preferred_element_type=F32
        )
        attn_out[:, cols] = mixed.astype(BF16)
        pressure = jnp.dot(weighted[:, cols], values, preferred_element_type=F32)
        centre = jnp.sum(attend * pressure, axis=1, keepdims=True)
        slope = (attend * (pressure - centre)).astype(BF16)
        dq_rot = (
            lax.dot_general(slope, keys, (((1,), (1,)), ((), ())), preferred_element_type=F32)
            * scaling
        )
        dq = dq_rot * cq - pltpu.roll(dq_rot, 64, 1) * sq
        dq_out[cols, :] = dq.T.astype(BF16)


def attend(parts, kv, visible, weighted, tables):
    return pl.pallas_call(
        attend_kernel,
        out_shape=(
            jax.ShapeDtypeStruct((TOK, 256), BF16),
            jax.ShapeDtypeStruct((256, TOK), BF16),
        ),
        compiler_params=params(),
        name="attend",
    )(*parts, kv, visible, weighted, *tables)


def gradient_kernel(where_ref, own, n1, n2, n3, far, d0, d1, d2, d3, out):
    step = pl.program_id(0)

    def term(tokens):
        total = None
        for x, d in zip(tokens, (d0, d1, d2, d3)):
            product = jnp.dot(d[...], x, preferred_element_type=F32)
            total = product if total is None else total + product
        out[0] = total.astype(BF16)

    @pl.when(step < 4)
    def _():
        term((own[...], n1[...], n2[...], n3[...]))

    @pl.when(step >= 4)
    def _():
        term((own[...], far[0], far[1], far[2]))


def gradient(where, states, near, far, slopes):
    whole = pl.BlockSpec((256, TOK), lambda i, w: (0, 0))
    return pl.pallas_call(
        gradient_kernel,
        out_shape=jax.ShapeDtypeStruct((8, 256, 256), BF16),
        grid_spec=pltpu.PrefetchScalarGridSpec(
            num_scalar_prefetch=1,
            grid=(8,),
            in_specs=[*token_specs(), *[whole] * 4],
            out_specs=pl.BlockSpec((1, 256, 256), lambda i, w: (z_block(i, w), 0, 0)),
        ),
        compiler_params=params(),
        name="gradient",
    )(where, states, *near, far, *slopes)


def total_kernel(terms, out):
    total = terms[0].astype(F32)
    for z in range(1, 8):
        total = total + terms[z].astype(F32)
    out[...] = total.T


def add_up(terms):
    return pl.pallas_call(
        total_kernel,
        out_shape=jax.ShapeDtypeStruct((256, 256), F32),
        compiler_params=params(),
        name="add_up",
    )(terms)


def shards(states, query_weight, key_matrix, value_matrix, block_mask, risk_weight, upstream):
    core = lax.axis_index("c")
    lane = lax.axis_index("yl")
    where = jnp.stack([core, lane]).astype(jnp.int32)

    key_t, value_t = key_matrix.T, value_matrix.T
    halves = []
    for half in range(2):
        a, b, e = 256 * half, 256 * half + 128, 256 * half + 256
        halves.append(
            jnp.concatenate(
                [
                    query_weight[a:e],
                    key_t[:, a:b],
                    value_t[:, a:b],
                    key_t[:, b:e],
                    value_t[:, b:e],
                ],
                axis=0,
            )
        )
    even = lane % 2 == 0
    first = jnp.where(even, halves[0], halves[1])
    second = jnp.where(even, halves[1], halves[0])
    first = lax.ppermute(first, AXES, home_pairs(0))
    second = lax.ppermute(second, AXES, home_pairs(1))

    outgoing = cut(where, states)
    near = [swap(outgoing[j - 1], "yl", 4, j) for j in (1, 2, 3)]

    piece = jnp.stack([jnp.where(even, first, second), jnp.where(even, second, first)])
    weights = lax.all_to_all(
        jnp.broadcast_to(piece[None], (8,) + piece.shape), "z", split_axis=0, concat_axis=0
    )
    far = swap(jnp.stack(near), "c", 2, 1)

    parts = project(where, states, near, far, weights)
    parts = (parts[0], *[swap(parts[j], "yl", 4, j) for j in (1, 2, 3)])
    kv = parts[0][256:]
    for part in parts[1:]:
        kv = kv + part[256:].astype(F32)
    kv = lax.all_gather(kv, ("xb", "c"), axis=0, tiled=False)

    depths = jnp.sum(block_mask, axis=1) - 1
    places = (depths[:, None] * BS + jnp.arange(BS, dtype=jnp.int32)[None, :]).reshape(TOK)
    frequency = jnp.exp(
        -math.log(1000000.0) * jnp.arange(HEAD // 2, dtype=F32) * 2.0 / HEAD
    )
    angles = places.astype(F32)[:, None] * frequency[None, :]
    cosine, sine = jnp.cos(angles), jnp.sin(angles)
    tables = (
        jnp.concatenate([cosine, cosine], axis=1),
        jnp.concatenate([-sine, sine], axis=1),
        cosine.T,
        sine.T,
    )
    position = jnp.arange(TOK, dtype=jnp.int32)
    blocks = position // BS
    wide_mask = jnp.repeat(jnp.repeat(block_mask, BS, axis=0), BS, axis=1) > 0
    visible = wide_mask & (
        (blocks[:, None] != blocks[None, :]) | (position[:, None] >= position[None, :])
    )
    visible = visible.astype(F32)
    weighted = (upstream.astype(F32) * jnp.repeat(risk_weight, BS)[:, None]).astype(BF16)

    attn_out, dq = attend(parts, kv, visible, weighted, tables)
    slopes = (dq, *[swap(dq, "yl", 4, j) for j in (1, 2, 3)])
    terms = gradient(where, states, near, far, slopes)
    terms = lax.all_to_all(terms, "z", split_axis=0, concat_axis=0)
    return attn_out, add_up(terms)


def solution(mesh):
    fine = Mesh(mesh.devices.reshape(SIZES), AXES)
    dp, tensor = ("z", "yl"), ("yh", "xh", "xb", "c")
    in_specs = (
        P(dp, None),
        P(tensor, dp),
        P(tensor, dp),
        P(tensor, dp),
        P(dp, None),
        P(dp),
        P(dp, tensor),
    )
    out_specs = (P(dp, tensor), P(dp, tensor))
    return jax.shard_map(shards, mesh=fine, in_specs=in_specs, out_specs=out_specs, check_vma=False)
```

```python
import math

import jax
import jax.numpy as jnp
from jax import lax
from jax.experimental import pallas as pl
from jax.experimental.pallas import tpu as pltpu
from jax.sharding import Mesh
from jax.sharding import PartitionSpec as P

HEAD = 128
BS = 64
TOK = 256
AXES = ("zh", "zb", "yu", "yb", "yh", "xh", "xb", "c")
SIZES = (4, 2, 2, 2, 2, 2, 2, 2)
GROUP = ("zb", "yb")
OTHERS = ("zh", "yu")
F32 = jnp.float32
BF16 = jnp.bfloat16
VMEM_LIMIT = 48 * 1024 * 1024


def params():
    return pltpu.CompilerParams(vmem_limit_bytes=VMEM_LIMIT)


def home_pairs(turn):
    pairs = []
    for d in range(32):
        for t in range(16):
            half = (d % 2) ^ turn
            pairs.append((d * 16 + t, (2 * t + half) * 16 + d // 2))
    return pairs


def swap(value, offset):
    return lax.ppermute(value, GROUP, [(i, i ^ offset) for i in range(4)])


def swap_core(value):
    return lax.ppermute(value, "c", [(0, 1), (1, 0)])


def block_of(part, core):
    return 4 * (core ^ (part // 4)) + part % 4


def cut_kernel(where_ref, states_ref, own_ref, one_ref, two_ref, three_ref, sems):
    core, place = where_ref[0], where_ref[1]
    copies = []
    for number, out in enumerate((own_ref, one_ref, two_ref, three_ref)):
        other = place ^ number
        for part in range(8 if number == 0 else 4):
            block = block_of(part, core)
            start = (block // 2) * 2048 + (block % 2) * 512 + (other // 2) * 1024 + (other % 2) * 256
            copies.append(
                pltpu.make_async_copy(
                    states_ref.at[:, pl.ds(pl.multiple_of(start, 256), 256)],
                    out.at[:, pl.ds(256 * part, 256)],
                    sems.at[len(copies)],
                )
            )
    for copy in copies:
        copy.start()
    for copy in copies:
        copy.wait()


def cut(where, states):
    part = jax.ShapeDtypeStruct((TOK, 1024), BF16)
    return pl.pallas_call(
        cut_kernel,
        out_shape=(jax.ShapeDtypeStruct((TOK, 2048), BF16), part, part, part),
        in_specs=[pl.BlockSpec(memory_space=pltpu.SMEM), pl.BlockSpec(memory_space=pl.ANY)],
        out_specs=(pl.BlockSpec(memory_space=pl.ANY),) * 4,
        scratch_shapes=[pltpu.SemaphoreType.DMA((20,))],
        compiler_params=params(),
        name="cut_states",
    )(where, states)


def pack_kernel(where_ref, query, key_t, value_t, first, second):
    odd = where_ref[1] % 2
    for turn, out in enumerate((first, second)):
        half = odd ^ turn
        out[:256, :] = query[pl.ds(pl.multiple_of(256 * half, 256), 256), :]
        for chunk in range(2):
            lanes = pl.ds(pl.multiple_of(256 * half + 128 * chunk, 128), 128)
            base = 256 + 32 * chunk
            out[base : base + 16, :] = key_t[:, lanes]
            out[base + 16 : base + 32, :] = value_t[:, lanes]


def pack(where, query, key_t, value_t):
    part = jax.ShapeDtypeStruct((320, 128), BF16)
    vmem = pl.BlockSpec(memory_space=pltpu.VMEM)
    return pl.pallas_call(
        pack_kernel,
        out_shape=(part, part),
        in_specs=[pl.BlockSpec(memory_space=pltpu.SMEM), vmem, vmem, vmem],
        compiler_params=params(),
        name="pack_weights",
    )(where, query, key_t, value_t)


def copies_kernel(where_ref, first, second, out):
    odd = where_ref[1] % 2
    for device in range(8):
        out[device, odd] = first[...]
        out[device, 1 - odd] = second[...]


def copies(where, first, second):
    vmem = pl.BlockSpec(memory_space=pltpu.VMEM)
    return pl.pallas_call(
        copies_kernel,
        out_shape=jax.ShapeDtypeStruct((8, 2, 320, 128), BF16),
        in_specs=[pl.BlockSpec(memory_space=pltpu.SMEM), vmem, vmem],
        compiler_params=params(),
        name="weight_copies",
    )(where, first, second)


def project_kernel(
    where_ref, own, n1, n2, n3, f1, f2, f3, weights, own_out, o1, o2, o3, w_q, w_kv
):
    core = where_ref[0]
    for part in range(8):
        block = block_of(part, core)
        for head in range(2):
            rows, cols = pl.ds(256 * part, 256), pl.ds(HEAD * head, HEAD)
            w_q[rows, cols] = weights[block, head, :256, :]
            for chunk in range(2):
                lanes = pl.ds(256 * part + 128 * chunk, 128)
                base = 256 + 32 * chunk
                w_kv[16 * head : 16 * head + 16, lanes] = weights[block, head, base : base + 16, :]
                w_kv[32 + 16 * head : 48 + 16 * head, lanes] = weights[
                    block, head, base + 16 : base + 32, :
                ]

    def product(x, rows):
        q = jnp.dot(x, w_q[rows, :], preferred_element_type=F32)
        kv = lax.dot_general(
            x, w_kv[:, rows], (((1,), (1,)), ((), ())), preferred_element_type=F32
        )
        return q, kv

    low, high = pl.ds(0, 1024), pl.ds(1024, 1024)
    pieces = (
        (own[:, low], own[:, high]),
        (n1[...], f1[...]),
        (n2[...], f2[...]),
        (n3[...], f3[...]),
    )
    for (near, far), out in zip(pieces, (own_out, o1, o2, o3)):
        q_near, kv_near = product(near, low)
        q_far, kv_far = product(far, high)
        out[:256, :] = (q_near + q_far).astype(out.dtype)
        out[256:, :] = (kv_near + kv_far).T.astype(out.dtype)


def project(where, own, near, far, weights):
    part = jax.ShapeDtypeStruct((320, 256), BF16)
    return pl.pallas_call(
        project_kernel,
        out_shape=(jax.ShapeDtypeStruct((320, 256), F32), part, part, part),
        in_specs=[pl.BlockSpec(memory_space=pltpu.SMEM)]
        + [pl.BlockSpec(memory_space=pltpu.VMEM)] * 8,
        scratch_shapes=[pltpu.VMEM((2048, 256), BF16), pltpu.VMEM((64, 2048), BF16)],
        compiler_params=params(),
        name="project",
    )(where, own, *near, *far, weights)


def attend_kernel(
    q0, q1, q2, q3, kv, visible, weighted, cos_q, sin_q, cos_k, sin_k, attn_out, dq_out
):
    scaling = 1.0 / math.sqrt(HEAD)
    k_lin = jnp.concatenate([kv[s, :32, :] for s in range(4)], axis=0)
    values = jnp.concatenate([kv[s, 32:, :] for s in range(4)], axis=0).astype(BF16)
    k1, k2 = k_lin[:64], k_lin[64:]
    ck, sk = cos_k[...], sin_k[...]
    keys = jnp.concatenate([k1 * ck - k2 * sk, k2 * ck + k1 * sk], axis=0).astype(BF16)
    seen = visible[...] > 0
    cq, sq = cos_q[...], sin_q[...]
    for head in range(2):
        cols = pl.ds(head * HEAD, HEAD)
        q_lin = q0[:256, cols]
        for part in (q1, q2, q3):
            q_lin = q_lin + part[:256, cols].astype(F32)
        queries = ((q_lin * cq + pltpu.roll(q_lin, 64, 1) * sq) * scaling).astype(BF16)
        scores = jnp.dot(queries, keys, preferred_element_type=F32)
        raised = jnp.where(seen, jnp.exp(scores), 0.0)
        attend = raised / jnp.sum(raised, axis=1, keepdims=True)
        mixed = lax.dot_general(
            attend.astype(BF16), values, (((1,), (1,)), ((), ())), preferred_element_type=F32
        )
        attn_out[:, cols] = mixed.astype(BF16)
        pressure = jnp.dot(weighted[:, cols], values, preferred_element_type=F32)
        centre = jnp.sum(attend * pressure, axis=1, keepdims=True)
        slope = (attend * (pressure - centre)).astype(BF16)
        dq_rot = (
            lax.dot_general(slope, keys, (((1,), (1,)), ((), ())), preferred_element_type=F32)
            * scaling
        )
        dq = dq_rot * cq - pltpu.roll(dq_rot, 64, 1) * sq
        dq_out[cols, :] = dq.T.astype(BF16)


def attend(parts, kv, visible, weighted, tables):
    return pl.pallas_call(
        attend_kernel,
        out_shape=(
            jax.ShapeDtypeStruct((TOK, 256), BF16),
            jax.ShapeDtypeStruct((256, TOK), BF16),
        ),
        compiler_params=params(),
        name="attend",
    )(*parts, kv, visible, weighted, *tables)


def gradient_kernel(where_ref, own, n1, n2, n3, f1, f2, f3, d0, d1, d2, d3, out):
    core = where_ref[0]
    for part in range(8):
        near = part < 4
        cols = pl.ds(256 * (part % 4), 256)
        tokens = (own[:, pl.ds(256 * part, 256)],) + tuple(
            x[:, cols] for x in ((n1, n2, n3) if near else (f1, f2, f3))
        )
        total = None
        for x, d in zip(tokens, (d0, d1, d2, d3)):
            term = jnp.dot(d[...], x, preferred_element_type=F32)
            total = term if total is None else total + term
        out[block_of(part, core)] = total.astype(BF16)


def gradient(where, own, near, far, slopes):
    return pl.pallas_call(
        gradient_kernel,
        out_shape=jax.ShapeDtypeStruct((8, 256, 256), BF16),
        in_specs=[pl.BlockSpec(memory_space=pltpu.SMEM)]
        + [pl.BlockSpec(memory_space=pltpu.VMEM)] * 11,
        compiler_params=params(),
        name="gradient",
    )(where, own, *near, *far, *slopes)


def total_kernel(terms, out):
    total = terms[0].astype(F32)
    for block in range(1, 8):
        total = total + terms[block].astype(F32)
    out[...] = total.T


def add_up(terms):
    return pl.pallas_call(
        total_kernel,
        out_shape=jax.ShapeDtypeStruct((256, 256), F32),
        compiler_params=params(),
        name="add_up",
    )(terms)


def shards(states, query_weight, key_matrix, value_matrix, block_mask, risk_weight, upstream):
    core = lax.axis_index("c")
    place = 2 * lax.axis_index("zb") + lax.axis_index("yb")
    where = jnp.stack([core, place]).astype(jnp.int32)

    own, *outgoing = cut(where, states)
    near = [swap(outgoing[j - 1], j) for j in (1, 2, 3)]
    far = [swap_core(x) for x in near]

    query_weight, _ = lax.optimization_barrier((query_weight, outgoing))
    first, second = pack(where, query_weight, key_matrix.T, value_matrix.T)
    first = lax.ppermute(first, AXES, home_pairs(0))
    second = lax.ppermute(second, AXES, home_pairs(1))
    weights = lax.all_to_all(
        copies(where, first, second), OTHERS, split_axis=0, concat_axis=0
    )

    parts = project(where, own, near, far, weights)
    parts = (parts[0], *[swap(parts[j], j) for j in (1, 2, 3)])
    kv = parts[0][256:]
    for part in parts[1:]:
        kv = kv + part[256:].astype(F32)
    kv = lax.all_gather(kv, ("xb", "c"), axis=0, tiled=False)

    depths = jnp.sum(block_mask, axis=1) - 1
    places = (depths[:, None] * BS + jnp.arange(BS, dtype=jnp.int32)[None, :]).reshape(TOK)
    frequency = jnp.exp(
        -math.log(1000000.0) * jnp.arange(HEAD // 2, dtype=F32) * 2.0 / HEAD
    )
    angles = places.astype(F32)[:, None] * frequency[None, :]
    cosine, sine = jnp.cos(angles), jnp.sin(angles)
    tables = (
        jnp.concatenate([cosine, cosine], axis=1),
        jnp.concatenate([-sine, sine], axis=1),
        cosine.T,
        sine.T,
    )
    position = jnp.arange(TOK, dtype=jnp.int32)
    blocks = position // BS
    wide_mask = jnp.repeat(jnp.repeat(block_mask, BS, axis=0), BS, axis=1) > 0
    visible = wide_mask & (
        (blocks[:, None] != blocks[None, :]) | (position[:, None] >= position[None, :])
    )
    visible = visible.astype(F32)
    weighted = (upstream.astype(F32) * jnp.repeat(risk_weight, BS)[:, None]).astype(BF16)

    attn_out, dq = attend(parts, kv, visible, weighted, tables)
    slopes = (dq, *[swap(dq, j) for j in (1, 2, 3)])
    terms = gradient(where, own, near, far, slopes)
    terms = lax.all_to_all(terms, OTHERS, split_axis=0, concat_axis=0)
    return attn_out, add_up(terms)


def solution(mesh):
    fine = Mesh(mesh.devices.reshape(SIZES), AXES)
    dp, tensor = AXES[:4], AXES[4:]
    in_specs = (
        P(dp, None),
        P(tensor, dp),
        P(tensor, dp),
        P(tensor, dp),
        P(dp, None),
        P(dp),
        P(dp, tensor),
    )
    out_specs = (P(dp, tensor), P(dp, tensor))
    return jax.shard_map(shards, mesh=fine, in_specs=in_specs, out_specs=out_specs, check_vma=False)
```

```python
import math

import jax
import jax.numpy as jnp
from jax import lax
from jax.experimental import pallas as pl
from jax.experimental.pallas import tpu as pltpu
from jax.sharding import Mesh
from jax.sharding import PartitionSpec as P

HEAD = 128
BS = 64
TOK = 256
AXES = ("zh", "zb", "yu", "yb", "yh", "xh", "xb", "c")
SIZES = (4, 2, 2, 2, 2, 2, 2, 2)
GROUP = ("zb", "yb")
OTHERS = ("zh", "yu")
F32 = jnp.float32
BF16 = jnp.bfloat16
VMEM_LIMIT = 16 * 1024 * 1024


def params():
    return pltpu.CompilerParams(vmem_limit_bytes=VMEM_LIMIT)


def home_pairs(turn):
    pairs = []
    for d in range(32):
        for t in range(16):
            half = (d % 2) ^ turn
            pairs.append((d * 16 + t, (2 * t + half) * 16 + d // 2))
    return pairs


def swap(value, offset):
    return lax.ppermute(value, GROUP, [(i, i ^ offset) for i in range(4)])


def swap_core(value):
    return lax.ppermute(value, "c", [(0, 1), (1, 0)])


def block_of(part, core):
    return 4 * (core ^ (part // 4)) + part % 4


def cut_kernel(where_ref, states_ref, own_ref, one_ref, two_ref, three_ref, sems):
    core, place = where_ref[0], where_ref[1]
    copies = []
    for number, out in enumerate((own_ref, one_ref, two_ref, three_ref)):
        other = place ^ number
        for part in range(8 if number == 0 else 4):
            block = block_of(part, core)
            start = (block // 2) * 2048 + (block % 2) * 512 + (other // 2) * 1024 + (other % 2) * 256
            copies.append(
                pltpu.make_async_copy(
                    states_ref.at[:, pl.ds(pl.multiple_of(start, 256), 256)],
                    out.at[:, pl.ds(256 * part, 256)],
                    sems.at[len(copies)],
                )
            )
    for copy in copies:
        copy.start()
    for copy in copies:
        copy.wait()


def cut(where, states):
    part = jax.ShapeDtypeStruct((TOK, 1024), BF16)
    return pl.pallas_call(
        cut_kernel,
        out_shape=(jax.ShapeDtypeStruct((TOK, 2048), BF16), part, part, part),
        in_specs=[pl.BlockSpec(memory_space=pltpu.SMEM), pl.BlockSpec(memory_space=pl.ANY)],
        out_specs=(pl.BlockSpec(memory_space=pltpu.VMEM),) * 4,
        scratch_shapes=[pltpu.SemaphoreType.DMA((20,))],
        compiler_params=params(),
        name="cut_states",
    )(where, states)


def pack_kernel(where_ref, query, key_t, value_t, after, first, second):
    odd = where_ref[1] % 2
    for turn, out in enumerate((first, second)):
        half = odd ^ turn
        out[:256, :] = query[pl.ds(pl.multiple_of(256 * half, 256), 256), :]
        for chunk in range(2):
            lanes = pl.ds(pl.multiple_of(256 * half + 128 * chunk, 128), 128)
            base = 256 + 32 * chunk
            out[base : base + 16, :] = key_t[:, lanes]
            out[base + 16 : base + 32, :] = value_t[:, lanes]


def pack(where, query, key_t, value_t, after):
    part = jax.ShapeDtypeStruct((320, 128), BF16)
    vmem = pl.BlockSpec(memory_space=pltpu.VMEM)
    return pl.pallas_call(
        pack_kernel,
        out_shape=(part, part),
        in_specs=[
            pl.BlockSpec(memory_space=pltpu.SMEM),
            *[vmem] * 3,
            pl.BlockSpec(memory_space=pl.ANY),
        ],
        compiler_params=params(),
        name="pack_weights",
    )(where, query, key_t, value_t, after)


def copies_kernel(where_ref, first, second, n1, n2, n3, out):
    odd = where_ref[1] % 2
    for device in range(8):
        out[device, odd] = first[...]
        out[device, 1 - odd] = second[...]


def copies(where, first, second, near):
    vmem = pl.BlockSpec(memory_space=pltpu.VMEM)
    return pl.pallas_call(
        copies_kernel,
        out_shape=jax.ShapeDtypeStruct((8, 2, 320, 128), BF16),
        in_specs=[
            pl.BlockSpec(memory_space=pltpu.SMEM),
            *[vmem] * 2,
            *[pl.BlockSpec(memory_space=pl.ANY)] * 3,
        ],
        compiler_params=params(),
        name="weight_copies",
    )(where, first, second, *near)


def project_kernel(
    where_ref, own, n1, n2, n3, f1, f2, f3, weights, out, w_q, w_kv
):
    core = where_ref[0]
    for part in range(8):
        block = block_of(part, core)
        for head in range(2):
            rows, cols = pl.ds(256 * part, 256), pl.ds(HEAD * head, HEAD)
            w_q[rows, cols] = weights[block, head, :256, :]
            for chunk in range(2):
                lanes = pl.ds(256 * part + 128 * chunk, 128)
                base = 256 + 32 * chunk
                w_kv[16 * head : 16 * head + 16, lanes] = weights[block, head, base : base + 16, :]
                w_kv[32 + 16 * head : 48 + 16 * head, lanes] = weights[
                    block, head, base + 16 : base + 32, :
                ]

    def product(x, rows):
        q = jnp.dot(x, w_q[rows, :], preferred_element_type=F32)
        kv = lax.dot_general(
            x, w_kv[:, rows], (((1,), (1,)), ((), ())), preferred_element_type=F32
        )
        return q, kv

    low, high = pl.ds(0, 1024), pl.ds(1024, 1024)
    pieces = (
        (own[:, low], own[:, high]),
        (n1[...], f1[...]),
        (n2[...], f2[...]),
        (n3[...], f3[...]),
    )
    for number, (near, far) in enumerate(pieces):
        other = where_ref[1] ^ number
        q_near, kv_near = product(near, low)
        q_far, kv_far = product(far, high)
        out[other, :256, :] = (q_near + q_far).astype(BF16)
        out[other, 256:, :] = (kv_near + kv_far).T.astype(BF16)


def project(where, own, near, far, weights):
    return pl.pallas_call(
        project_kernel,
        out_shape=jax.ShapeDtypeStruct((4, 320, 256), BF16),
        in_specs=[pl.BlockSpec(memory_space=pltpu.SMEM)]
        + [pl.BlockSpec(memory_space=pltpu.VMEM)] * 8,
        scratch_shapes=[pltpu.VMEM((2048, 256), BF16), pltpu.VMEM((64, 2048), BF16)],
        compiler_params=params(),
        name="project",
    )(where, own, *near, *far, weights)


def attend_kernel(
    parts, kv, visible, weighted, cos_q, sin_q, cos_k, sin_k, attn_out, dq_out
):
    scaling = 1.0 / math.sqrt(HEAD)
    k_lin = jnp.concatenate([kv[s, :32, :] for s in range(4)], axis=0)
    values = jnp.concatenate([kv[s, 32:, :] for s in range(4)], axis=0).astype(BF16)
    k1, k2 = k_lin[:64], k_lin[64:]
    ck, sk = cos_k[...], sin_k[...]
    keys = jnp.concatenate([k1 * ck - k2 * sk, k2 * ck + k1 * sk], axis=0).astype(BF16)
    seen = visible[...] > 0
    cq, sq = cos_q[...], sin_q[...]
    for head in range(2):
        cols = pl.ds(head * HEAD, HEAD)
        q_lin = parts[0, :256, cols].astype(F32)
        for part in range(1, 4):
            q_lin = q_lin + parts[part, :256, cols].astype(F32)
        queries = ((q_lin * cq + pltpu.roll(q_lin, 64, 1) * sq) * scaling).astype(BF16)
        scores = jnp.dot(queries, keys, preferred_element_type=F32)
        raised = jnp.where(seen, jnp.exp(scores), 0.0)
        attend = raised / jnp.sum(raised, axis=1, keepdims=True)
        mixed = lax.dot_general(
            attend.astype(BF16), values, (((1,), (1,)), ((), ())), preferred_element_type=F32
        )
        attn_out[:, cols] = mixed.astype(BF16)
        pressure = jnp.dot(weighted[:, cols], values, preferred_element_type=F32)
        centre = jnp.sum(attend * pressure, axis=1, keepdims=True)
        slope = (attend * (pressure - centre)).astype(BF16)
        dq_rot = (
            lax.dot_general(slope, keys, (((1,), (1,)), ((), ())), preferred_element_type=F32)
            * scaling
        )
        dq = dq_rot * cq - pltpu.roll(dq_rot, 64, 1) * sq
        dq_t = dq.T.astype(BF16)
        for part in range(4):
            dq_out[part, cols, :] = dq_t


def attend(parts, kv, visible, weighted, tables):
    return pl.pallas_call(
        attend_kernel,
        out_shape=(
            jax.ShapeDtypeStruct((TOK, 256), BF16),
            jax.ShapeDtypeStruct((4, 256, TOK), BF16),
        ),
        compiler_params=params(),
        name="attend",
    )(parts, kv, visible, weighted, *tables)


def gradient_kernel(where_ref, own, n1, n2, n3, f1, f2, f3, slopes, out):
    core = where_ref[0]
    for part in range(8):
        near = part < 4
        cols = pl.ds(256 * (part % 4), 256)
        tokens = (own[:, pl.ds(256 * part, 256)],) + tuple(
            x[:, cols] for x in ((n1, n2, n3) if near else (f1, f2, f3))
        )
        total = None
        for number, x in enumerate(tokens):
            term = jnp.dot(slopes[where_ref[1] ^ number], x, preferred_element_type=F32)
            total = term if total is None else total + term
        out[block_of(part, core)] = total.astype(BF16)


def gradient(where, own, near, far, slopes):
    return pl.pallas_call(
        gradient_kernel,
        out_shape=jax.ShapeDtypeStruct((8, 256, 256), BF16),
        in_specs=[pl.BlockSpec(memory_space=pltpu.SMEM)]
        + [pl.BlockSpec(memory_space=pltpu.VMEM)] * 8,
        compiler_params=params(),
        name="gradient",
    )(where, own, *near, *far, slopes)


def total_kernel(terms, out):
    total = terms[0].astype(F32)
    for block in range(1, 8):
        total = total + terms[block].astype(F32)
    out[...] = total.T


def add_up(terms):
    return pl.pallas_call(
        total_kernel,
        out_shape=jax.ShapeDtypeStruct((256, 256), F32),
        compiler_params=params(),
        name="add_up",
    )(terms)


def shards(states, query_weight, key_matrix, value_matrix, block_mask, risk_weight, upstream):
    core = lax.axis_index("c")
    place = 2 * lax.axis_index("zb") + lax.axis_index("yb")
    where = jnp.stack([core, place]).astype(jnp.int32)

    own, *outgoing = cut(where, states)
    near = [swap(outgoing[j - 1], j) for j in (1, 2, 3)]
    far = [swap_core(x) for x in near]

    first, second = pack(where, query_weight, key_matrix.T, value_matrix.T, outgoing[0])
    first = lax.ppermute(first, AXES, home_pairs(0))
    second = lax.ppermute(second, AXES, home_pairs(1))
    weights = lax.all_to_all(
        copies(where, first, second, near), OTHERS, split_axis=0, concat_axis=0
    )

    parts = project(where, own, near, far, weights)
    parts = lax.all_to_all(parts, GROUP, split_axis=0, concat_axis=0)
    kv = jnp.sum(parts[:, 256:].astype(F32), axis=0)
    kv = lax.all_gather(kv, ("xb", "c"), axis=0, tiled=False)

    depths = jnp.sum(block_mask, axis=1) - 1
    places = (depths[:, None] * BS + jnp.arange(BS, dtype=jnp.int32)[None, :]).reshape(TOK)
    frequency = jnp.exp(
        -math.log(1000000.0) * jnp.arange(HEAD // 2, dtype=F32) * 2.0 / HEAD
    )
    angles = places.astype(F32)[:, None] * frequency[None, :]
    cosine, sine = jnp.cos(angles), jnp.sin(angles)
    tables = (
        jnp.concatenate([cosine, cosine], axis=1),
        jnp.concatenate([-sine, sine], axis=1),
        cosine.T,
        sine.T,
    )
    position = jnp.arange(TOK, dtype=jnp.int32)
    blocks = position // BS
    wide_mask = jnp.repeat(jnp.repeat(block_mask, BS, axis=0), BS, axis=1) > 0
    visible = wide_mask & (
        (blocks[:, None] != blocks[None, :]) | (position[:, None] >= position[None, :])
    )
    visible = visible.astype(F32)
    weighted = (upstream.astype(F32) * jnp.repeat(risk_weight, BS)[:, None]).astype(BF16)

    attn_out, dq = attend(parts, kv, visible, weighted, tables)
    slopes = lax.all_to_all(dq, GROUP, split_axis=0, concat_axis=0)
    terms = gradient(where, own, near, far, slopes)
    terms = lax.all_to_all(terms, OTHERS, split_axis=0, concat_axis=0)
    return attn_out, add_up(terms)


def solution(mesh):
    fine = Mesh(mesh.devices.reshape(SIZES), AXES)
    dp, tensor = AXES[:4], AXES[4:]
    in_specs = (
        P(dp, None),
        P(tensor, dp),
        P(tensor, dp),
        P(tensor, dp),
        P(dp, None),
        P(dp),
        P(dp, tensor),
    )
    out_specs = (P(dp, tensor), P(dp, tensor))
    return jax.shard_map(shards, mesh=fine, in_specs=in_specs, out_specs=out_specs, check_vma=False)
```

```python
import math

import jax
import jax.numpy as jnp
from jax import lax
from jax.experimental import pallas as pl
from jax.experimental.pallas import tpu as pltpu
from jax.sharding import Mesh
from jax.sharding import PartitionSpec as P

HEAD = 128
BS = 64
TOK = 256
AXES = ("zh", "zb", "yu", "yb", "yh", "xh", "xb", "c")
SIZES = (4, 2, 2, 2, 2, 2, 2, 2)
GROUP = ("zb", "yb")
OTHERS = ("zh", "yu")
F32 = jnp.float32
BF16 = jnp.bfloat16
VMEM_LIMIT = 16 * 1024 * 1024


def params():
    return pltpu.CompilerParams(vmem_limit_bytes=VMEM_LIMIT)


def home_pairs(turn, far):
    pairs = []
    for d in range(32):
        for t in range(16):
            half = (d % 2) ^ turn
            block = (2 * t + half) ^ (2 * far)
            pairs.append((d * 16 + t, block * 16 + d // 2))
    return pairs


def along_z(value, step):
    return lax.ppermute(value, "zh", [(i, (i + step) % 4) for i in range(4)])


def swap(value, offset):
    return lax.ppermute(value, GROUP, [(i, i ^ offset) for i in range(4)])


def swap_core(value):
    return lax.ppermute(value, "c", [(0, 1), (1, 0)])


def block_of(part, core):
    return 4 * (core ^ (part // 4)) + part % 4


def column_of(block, place):
    return pl.multiple_of(
        (block // 2) * 2048 + (block % 2) * 512 + (place // 2) * 1024 + (place % 2) * 256, 256
    )


def in_smem():
    return pl.BlockSpec(memory_space=pltpu.SMEM)


def in_vmem(count):
    return [pl.BlockSpec(memory_space=pltpu.VMEM)] * count


def in_hbm():
    return pl.BlockSpec(memory_space=pltpu.HBM)


def anywhere():
    return pl.BlockSpec(memory_space=pl.ANY)


def pack_kernel(where_ref, query, key_t, value_t, first, second):
    odd = where_ref[1] % 2
    for turn, out in enumerate((first, second)):
        half = odd ^ turn
        out[:256, :] = query[pl.ds(pl.multiple_of(256 * half, 256), 256), :]
        for chunk in range(2):
            lanes = pl.ds(pl.multiple_of(256 * half + 128 * chunk, 128), 128)
            base = 256 + 32 * chunk
            out[base : base + 16, :] = key_t[:, lanes]
            out[base + 16 : base + 32, :] = value_t[:, lanes]


def pack(where, query, key_t, value_t):
    part = jax.ShapeDtypeStruct((320, 128), BF16)
    return pl.pallas_call(
        pack_kernel,
        out_shape=(part, part),
        in_specs=[in_smem(), *in_vmem(3)],
        compiler_params=params(),
        name="pack_weights",
    )(where, query, key_t, value_t)


def cut_kernel(where_ref, states_ref, after, one_ref, two_ref, three_ref, sems):
    core, place = where_ref[0], where_ref[1]
    copies = []
    for number, out in enumerate((one_ref, two_ref, three_ref)):
        for part in range(4):
            start = column_of(block_of(part, core), place ^ (number + 1))
            copies.append(
                pltpu.make_async_copy(
                    states_ref.at[:, pl.ds(start, 256)],
                    out.at[:, pl.ds(256 * part, 256)],
                    sems.at[len(copies)],
                )
            )
    for copy in copies:
        copy.start()
    for copy in copies:
        copy.wait()


def cut(where, states, after):
    part = jax.ShapeDtypeStruct((TOK, 1024), BF16)
    return pl.pallas_call(
        cut_kernel,
        out_shape=(part, part, part),
        in_specs=[in_smem(), in_hbm(), anywhere()],
        out_specs=tuple(in_vmem(3)),
        scratch_shapes=[pltpu.SemaphoreType.DMA((12,))],
        compiler_params=params(),
        name="cut_states",
    )(where, states, after)


def own_columns(where_ref, states_ref, own, sems):
    copies = []
    for part in range(8):
        start = column_of(block_of(part, where_ref[0]), where_ref[1])
        copies.append(
            pltpu.make_async_copy(
                states_ref.at[:, pl.ds(start, 256)],
                own.at[:, pl.ds(256 * part, 256)],
                sems.at[part],
            )
        )
    return copies


def collect_kernel(where_ref, near_one, near_two, far_one, far_two, out):
    odd, upper = where_ref[1] % 2, where_ref[3]
    out[upper, odd] = near_one[...]
    out[upper, 1 - odd] = near_two[...]
    out[1 - upper, odd] = far_one[...]
    out[1 - upper, 1 - odd] = far_two[...]


def collect(where, pieces):
    return pl.pallas_call(
        collect_kernel,
        out_shape=jax.ShapeDtypeStruct((2, 2, 320, 128), BF16),
        in_specs=[in_smem(), *in_vmem(4)],
        compiler_params=params(),
        name="collect_weights",
    )(where, *pieces)


def project_kernel(
    where_ref, states_ref, n1, n2, n3, f1, f2, f3, w0, w1, w2_low, w2_high, w3, out, own, w_q, w_kv, sems
):
    core = where_ref[0]
    copies = own_columns(where_ref, states_ref, own, sems)
    for copy in copies:
        copy.start()
    for step in range(4):
        for upper in range(2):
            block = 2 * ((where_ref[2] + step) % 4) + upper
            start = pl.multiple_of(256 * block_of(block, core), 256)
            rows = pl.ds(start, 256)
            for head in range(2):
                if step == 2:
                    piece = (w2_low, w2_high)[upper].at[head]
                else:
                    piece = {0: w0, 1: w1, 3: w3}[step].at[upper, head]
                w_q[rows, pl.ds(HEAD * head, HEAD)] = piece[:256, :]
                for chunk in range(2):
                    lanes = pl.ds(start + 128 * chunk, 128)
                    base = 256 + 32 * chunk
                    w_kv[16 * head : 16 * head + 16, lanes] = piece[base : base + 16, :]
                    w_kv[32 + 16 * head : 48 + 16 * head, lanes] = piece[base + 16 : base + 32, :]

    def product(x, rows):
        q = jnp.dot(x, w_q[rows, :], preferred_element_type=F32)
        kv = lax.dot_general(
            x, w_kv[:, rows], (((1,), (1,)), ((), ())), preferred_element_type=F32
        )
        return q, kv

    low, high = pl.ds(0, 1024), pl.ds(1024, 1024)
    pieces = (
        (n1.at[:, :], f1.at[:, :]),
        (n2.at[:, :], f2.at[:, :]),
        (n3.at[:, :], f3.at[:, :]),
        (own.at[:, low], own.at[:, high]),
    )
    for number, (near_ref, far_ref) in enumerate(pieces):
        if number == 3:
            for copy in copies:
                copy.wait()
        near, far = near_ref[...], far_ref[...]
        other = where_ref[1] ^ ((number + 1) % 4)
        q_near, kv_near = product(near, low)
        q_far, kv_far = product(far, high)
        out[other, :256, :] = (q_near + q_far).astype(BF16)
        out[other, 256:, :] = (kv_near + kv_far).T.astype(BF16)


def project(where, states, near, far, weights):
    return pl.pallas_call(
        project_kernel,
        out_shape=jax.ShapeDtypeStruct((4, 320, 256), BF16),
        in_specs=[in_smem(), in_hbm(), *in_vmem(11)],
        scratch_shapes=[
            pltpu.VMEM((TOK, 2048), BF16),
            pltpu.VMEM((2048, 256), BF16),
            pltpu.VMEM((64, 2048), BF16),
            pltpu.SemaphoreType.DMA((8,)),
        ],
        compiler_params=params(),
        name="project",
    )(where, states, *near, *far, *weights)


def attend_kernel(
    mask_ref, risk_ref, parts, kv, upstream_ref, tables_ref, attn_out, dq_out, upstream, tables, sems
):
    copies = [
        pltpu.make_async_copy(tables_ref, tables, sems.at[0]),
        pltpu.make_async_copy(upstream_ref, upstream, sems.at[1]),
    ]
    for copy in copies:
        copy.start()
    scaling = 1.0 / math.sqrt(HEAD)
    k_lin = jnp.concatenate([kv[s, :32, :] for s in range(4)], axis=0)
    values = jnp.concatenate([kv[s, 32:, :] for s in range(4)], axis=0).astype(BF16)

    row = lax.broadcasted_iota(jnp.int32, (BS, TOK), 0)
    column = lax.broadcasted_iota(jnp.int32, (BS, TOK), 1)
    seen, risk = [], []
    for b in range(4):
        on_path = jnp.zeros((BS, TOK), jnp.int32)
        for c in range(4):
            on_path = jnp.where(column // BS == c, mask_ref[b, c], on_path)
        seen.append((on_path > 0) & ((column // BS != b) | (column - BS * b <= row)))
        risk.append(jnp.full((BS, 1), risk_ref[b], F32))
    seen = jnp.concatenate(seen, axis=0)
    risk = jnp.concatenate(risk, axis=0)

    copies[0].wait()
    cq, sq = tables[:, :HEAD], tables[:, HEAD:]
    ck, sk = cq[:, :64].T, sq[:, 64:].T
    k1, k2 = k_lin[:64], k_lin[64:]
    keys = jnp.concatenate([k1 * ck - k2 * sk, k2 * ck + k1 * sk], axis=0).astype(BF16)
    copies[1].wait()
    weighted = (upstream[...].astype(F32) * risk).astype(BF16)
    for head in range(2):
        cols = pl.ds(head * HEAD, HEAD)
        q_lin = parts[0, :256, cols].astype(F32)
        for part in range(1, 4):
            q_lin = q_lin + parts[part, :256, cols].astype(F32)
        queries = ((q_lin * cq + pltpu.roll(q_lin, 64, 1) * sq) * scaling).astype(BF16)
        scores = jnp.dot(queries, keys, preferred_element_type=F32)
        raised = jnp.where(seen, jnp.exp(scores), 0.0)
        attend = raised / jnp.sum(raised, axis=1, keepdims=True)
        mixed = lax.dot_general(
            attend.astype(BF16), values, (((1,), (1,)), ((), ())), preferred_element_type=F32
        )
        attn_out[:, cols] = mixed.astype(BF16)
        pressure = jnp.dot(weighted[:, HEAD * head : HEAD * head + HEAD], values, preferred_element_type=F32)
        centre = jnp.sum(attend * pressure, axis=1, keepdims=True)
        slope = (attend * (pressure - centre)).astype(BF16)
        dq_rot = (
            lax.dot_general(slope, keys, (((1,), (1,)), ((), ())), preferred_element_type=F32)
            * scaling
        )
        dq = dq_rot * cq - pltpu.roll(dq_rot, 64, 1) * sq
        dq_t = dq.T.astype(BF16)
        for part in range(4):
            dq_out[part, cols, :] = dq_t


def attend(block_mask, risk_weight, parts, kv, upstream, tables):
    return pl.pallas_call(
        attend_kernel,
        out_shape=(
            jax.ShapeDtypeStruct((TOK, 256), BF16),
            jax.ShapeDtypeStruct((4, 256, TOK), BF16),
        ),
        in_specs=[in_smem(), in_smem(), *in_vmem(2), in_hbm(), in_hbm()],
        scratch_shapes=[
            pltpu.VMEM((TOK, 256), BF16),
            pltpu.VMEM((TOK, 2 * HEAD), F32),
            pltpu.SemaphoreType.DMA((2,)),
        ],
        compiler_params=params(),
        name="attend",
    )(block_mask, risk_weight, parts, kv, upstream, tables)


def gradient_kernel(where_ref, states_ref, n1, n2, n3, f1, f2, f3, slopes, out, own, sems):
    core = where_ref[0]
    copies = own_columns(where_ref, states_ref, own, sems)
    for copy in copies:
        copy.start()
    for part in range(8):
        cols = pl.ds(256 * (part % 4), 256)
        total = None
        for number in (1, 2, 3, 0):
            if number == 0:
                copies[part].wait()
                x = own[:, pl.ds(256 * part, 256)]
            else:
                x = ((n1, n2, n3) if part < 4 else (f1, f2, f3))[number - 1][:, cols]
            term = jnp.dot(slopes[where_ref[1] ^ number], x, preferred_element_type=F32)
            total = term if total is None else total + term
        out[block_of(part, core)] = total.astype(BF16)


def gradient(where, states, near, far, slopes):
    return pl.pallas_call(
        gradient_kernel,
        out_shape=jax.ShapeDtypeStruct((8, 256, 256), BF16),
        in_specs=[in_smem(), in_hbm(), *in_vmem(7)],
        scratch_shapes=[pltpu.VMEM((TOK, 2048), BF16), pltpu.SemaphoreType.DMA((8,))],
        compiler_params=params(),
        name="gradient",
    )(where, states, *near, *far, slopes)


def total_kernel(terms, out):
    total = terms[0].astype(F32)
    for block in range(1, 8):
        total = total + terms[block].astype(F32)
    out[...] = total.T


def add_up(terms):
    return pl.pallas_call(
        total_kernel,
        out_shape=jax.ShapeDtypeStruct((256, 256), F32),
        compiler_params=params(),
        name="add_up",
    )(terms)


def shards(states, query_weight, key_matrix, value_matrix, block_mask, risk_weight, upstream):
    place = 2 * lax.axis_index("zb") + lax.axis_index("yb")
    where = jnp.stack([lax.axis_index("c"), place, lax.axis_index("zh"), lax.axis_index("yu")])
    where = where.astype(jnp.int32)

    halves = pack(where, query_weight, key_matrix.T, value_matrix.T)
    pieces = [
        lax.ppermute(halves[turn], AXES, home_pairs(turn, far))
        for far in range(2)
        for turn in range(2)
    ]

    outgoing = cut(where, states, halves[0])
    near = [swap(outgoing[j - 1], j) for j in (1, 2, 3)]
    far = [swap_core(x) for x in near]

    w0 = collect(where, pieces)
    w3 = along_z(w0, 1)
    w1 = along_z(w0, -1)
    w2_low = along_z(w3[0], 1)
    w2_high = along_z(w1[1], -1)

    parts = project(where, states, near, far, (w0, w1, w2_low, w2_high, w3))
    parts = lax.all_to_all(parts, GROUP, split_axis=0, concat_axis=0)
    kv = jnp.sum(parts[:, 256:].astype(F32), axis=0)
    kv = lax.all_gather(kv, ("xb", "c"), axis=0, tiled=False)

    depths = jnp.sum(block_mask, axis=1) - 1
    places = (depths[:, None] * BS + jnp.arange(BS, dtype=jnp.int32)[None, :]).reshape(TOK)
    frequency = jnp.exp(
        -math.log(1000000.0) * jnp.arange(HEAD // 2, dtype=F32) * 2.0 / HEAD
    )
    angles = places.astype(F32)[:, None] * frequency[None, :]
    cosine, sine = jnp.cos(angles), jnp.sin(angles)
    tables = jnp.concatenate([cosine, cosine, -sine, sine], axis=1)

    attn_out, dq = attend(block_mask, risk_weight, parts, kv, upstream, tables)
    slopes = lax.all_to_all(dq, GROUP, split_axis=0, concat_axis=0)
    terms = gradient(where, states, near, far, slopes)
    terms = lax.all_to_all(terms, OTHERS, split_axis=0, concat_axis=0)
    return attn_out, add_up(terms)


def solution(mesh):
    fine = Mesh(mesh.devices.reshape(SIZES), AXES)
    dp, tensor = AXES[:4], AXES[4:]
    in_specs = (
        P(dp, None),
        P(tensor, dp),
        P(tensor, dp),
        P(tensor, dp),
        P(dp, None),
        P(dp),
        P(dp, tensor),
    )
    out_specs = (P(dp, tensor), P(dp, tensor))
    return jax.shard_map(shards, mesh=fine, in_specs=in_specs, out_specs=out_specs, check_vma=False)
```

```python
import math

import jax
import jax.numpy as jnp
from jax import lax
from jax.experimental import pallas as pl
from jax.experimental.pallas import tpu as pltpu
from jax.sharding import Mesh
from jax.sharding import PartitionSpec as P

HEAD = 128
BS = 64
TOK = 256
AXES = ("zh", "zb", "yu", "yb", "yh", "xh", "xb", "c")
SIZES = (4, 2, 2, 2, 2, 2, 2, 2)
GROUP = ("yu", "yb")
OTHERS = ("zh", "zb")
F32 = jnp.float32
BF16 = jnp.bfloat16
VMEM_LIMIT = 16 * 1024 * 1024
VMEM_MOST = 56 * 1024 * 1024


def params(limit=VMEM_LIMIT):
    return pltpu.CompilerParams(vmem_limit_bytes=limit)


def home_pairs(turn):
    pairs = []
    for d in range(32):
        for t in range(16):
            half = (d % 2) ^ turn
            pairs.append((d * 16 + t, (2 * t + half) * 16 + d // 2))
    return pairs


def swap(value, offset):
    return lax.ppermute(value, GROUP, [(i, i ^ offset) for i in range(4)])


def swap_core(value):
    return lax.ppermute(value, "c", [(0, 1), (1, 0)])


def block_of(part, core):
    return 4 * (core ^ (part // 4)) + part % 4


def column_of(block, place):
    return pl.multiple_of(1024 * block + 256 * place, 256)


def in_smem():
    return pl.BlockSpec(memory_space=pltpu.SMEM)


def in_vmem(count):
    return [pl.BlockSpec(memory_space=pltpu.VMEM)] * count


def in_hbm():
    return pl.BlockSpec(memory_space=pltpu.HBM)


def anywhere():
    return pl.BlockSpec(memory_space=pl.ANY)


def pack_kernel(where_ref, query, key_t, value_t, first, second):
    odd = where_ref[1] % 2
    for turn, out in enumerate((first, second)):
        half = odd ^ turn
        out[:256, :] = query[pl.ds(pl.multiple_of(256 * half, 256), 256), :]
        for chunk in range(2):
            lanes = pl.ds(pl.multiple_of(256 * half + 128 * chunk, 128), 128)
            base = 256 + 32 * chunk
            out[base : base + 16, :] = key_t[:, lanes]
            out[base + 16 : base + 32, :] = value_t[:, lanes]


def pack(where, query, key_t, value_t):
    part = jax.ShapeDtypeStruct((320, 128), BF16)
    return pl.pallas_call(
        pack_kernel,
        out_shape=(part, part),
        in_specs=[in_smem(), *in_vmem(3)],
        compiler_params=params(),
        name="pack_weights",
    )(where, query, key_t, value_t)


def cut_kernel(where_ref, states_ref, after, one_ref, two_ref, three_ref, sems):
    core, place = where_ref[0], where_ref[1]
    copies = []
    for number, out in enumerate((one_ref, two_ref, three_ref)):
        for part in range(4):
            start = column_of(block_of(part, core), place ^ (number + 1))
            copies.append(
                pltpu.make_async_copy(
                    states_ref.at[:, pl.ds(start, 256)],
                    out.at[:, pl.ds(256 * part, 256)],
                    sems.at[len(copies)],
                )
            )
    for copy in copies:
        copy.start()
    for copy in copies:
        copy.wait()


def cut(where, states, after):
    part = jax.ShapeDtypeStruct((TOK, 1024), BF16)
    return pl.pallas_call(
        cut_kernel,
        out_shape=(part, part, part),
        in_specs=[in_smem(), in_hbm(), anywhere()],
        out_specs=tuple(in_vmem(3)),
        scratch_shapes=[pltpu.SemaphoreType.DMA((12,))],
        compiler_params=params(VMEM_MOST),
        name="cut_states",
    )(where, states, after)


def own_columns(where_ref, states_ref, own, sems):
    copies = []
    for part in range(8):
        start = column_of(block_of(part, where_ref[0]), where_ref[1])
        copies.append(
            pltpu.make_async_copy(
                states_ref.at[:, pl.ds(start, 256)],
                own.at[:, pl.ds(256 * part, 256)],
                sems.at[part],
            )
        )
    return copies


def collect_kernel(where_ref, first, second, out):
    odd = where_ref[1] % 2
    out[odd] = first[...]
    out[1 - odd] = second[...]


def collect(where, first, second):
    return pl.pallas_call(
        collect_kernel,
        out_shape=jax.ShapeDtypeStruct((2, 320, 128), BF16),
        in_specs=[in_smem(), *in_vmem(2)],
        compiler_params=params(),
        name="collect_weights",
    )(where, first, second)


def project_kernel(
    where_ref, states_ref, n1, n2, n3, f1, f2, f3, weights, out, own, w_q, w_kv, sems
):
    core = where_ref[0]
    copies = own_columns(where_ref, states_ref, own, sems)
    for copy in copies:
        copy.start()
    for part in range(8):
        block = block_of(part, core)
        for head in range(2):
            rows, cols = pl.ds(256 * part, 256), pl.ds(HEAD * head, HEAD)
            w_q[rows, cols] = weights[block, head, :256, :]
            for chunk in range(2):
                lanes = pl.ds(256 * part + 128 * chunk, 128)
                base = 256 + 32 * chunk
                w_kv[16 * head : 16 * head + 16, lanes] = weights[block, head, base : base + 16, :]
                w_kv[32 + 16 * head : 48 + 16 * head, lanes] = weights[
                    block, head, base + 16 : base + 32, :
                ]

    def product(x, rows):
        q = jnp.dot(x, w_q[rows, :], preferred_element_type=F32)
        kv = lax.dot_general(
            x, w_kv[:, rows], (((1,), (1,)), ((), ())), preferred_element_type=F32
        )
        return q, kv

    low, high = pl.ds(0, 1024), pl.ds(1024, 1024)
    pieces = (
        (n1.at[:, :], f1.at[:, :]),
        (n2.at[:, :], f2.at[:, :]),
        (n3.at[:, :], f3.at[:, :]),
        (own.at[:, low], own.at[:, high]),
    )
    for number, (near_ref, far_ref) in enumerate(pieces):
        if number == 3:
            for copy in copies:
                copy.wait()
        near, far = near_ref[...], far_ref[...]
        other = where_ref[1] ^ ((number + 1) % 4)
        q_near, kv_near = product(near, low)
        q_far, kv_far = product(far, high)
        out[other, :256, :] = (q_near + q_far).astype(BF16)
        out[other, 256:, :] = (kv_near + kv_far).T.astype(BF16)


def project(where, states, near, far, weights):
    return pl.pallas_call(
        project_kernel,
        out_shape=jax.ShapeDtypeStruct((4, 320, 256), BF16),
        in_specs=[in_smem(), in_hbm(), *in_vmem(7)],
        scratch_shapes=[
            pltpu.VMEM((TOK, 2048), BF16),
            pltpu.VMEM((2048, 256), BF16),
            pltpu.VMEM((64, 2048), BF16),
            pltpu.SemaphoreType.DMA((8,)),
        ],
        compiler_params=params(VMEM_MOST),
        name="project",
    )(where, states, *near, *far, weights)


def attend_kernel(
    mask_ref, risk_ref, parts, kv, upstream_ref, tables_ref, attn_out, dq_out, upstream, tables, sems
):
    copies = [
        pltpu.make_async_copy(tables_ref, tables, sems.at[0]),
        pltpu.make_async_copy(upstream_ref, upstream, sems.at[1]),
    ]
    for copy in copies:
        copy.start()
    scaling = 1.0 / math.sqrt(HEAD)
    k_lin = jnp.concatenate([kv[s, :32, :] for s in range(4)], axis=0)
    values = jnp.concatenate([kv[s, 32:, :] for s in range(4)], axis=0).astype(BF16)

    row = lax.broadcasted_iota(jnp.int32, (BS, TOK), 0)
    column = lax.broadcasted_iota(jnp.int32, (BS, TOK), 1)
    seen, risk = [], []
    for b in range(4):
        on_path = jnp.zeros((BS, TOK), jnp.int32)
        for c in range(4):
            on_path = jnp.where(column // BS == c, mask_ref[b, c], on_path)
        seen.append((on_path > 0) & ((column // BS != b) | (column - BS * b <= row)))
        risk.append(jnp.full((BS, 1), risk_ref[b], F32))
    seen = jnp.concatenate(seen, axis=0)
    risk = jnp.concatenate(risk, axis=0)

    copies[0].wait()
    cq, sq = tables[:, :HEAD], tables[:, HEAD:]
    ck, sk = cq[:, :64].T, sq[:, 64:].T
    k1, k2 = k_lin[:64], k_lin[64:]
    keys = jnp.concatenate([k1 * ck - k2 * sk, k2 * ck + k1 * sk], axis=0).astype(BF16)
    copies[1].wait()
    weighted = (upstream[...].astype(F32) * risk).astype(BF16)
    for head in range(2):
        cols = pl.ds(head * HEAD, HEAD)
        q_lin = parts[0, :256, cols].astype(F32)
        for part in range(1, 4):
            q_lin = q_lin + parts[part, :256, cols].astype(F32)
        queries = ((q_lin * cq + pltpu.roll(q_lin, 64, 1) * sq) * scaling).astype(BF16)
        scores = jnp.dot(queries, keys, preferred_element_type=F32)
        raised = jnp.where(seen, jnp.exp(scores), 0.0)
        attend = raised / jnp.sum(raised, axis=1, keepdims=True)
        mixed = lax.dot_general(
            attend.astype(BF16), values, (((1,), (1,)), ((), ())), preferred_element_type=F32
        )
        attn_out[:, cols] = mixed.astype(BF16)
        pressure = jnp.dot(weighted[:, HEAD * head : HEAD * head + HEAD], values, preferred_element_type=F32)
        centre = jnp.sum(attend * pressure, axis=1, keepdims=True)
        slope = (attend * (pressure - centre)).astype(BF16)
        dq_rot = (
            lax.dot_general(slope, keys, (((1,), (1,)), ((), ())), preferred_element_type=F32)
            * scaling
        )
        dq = dq_rot * cq - pltpu.roll(dq_rot, 64, 1) * sq
        dq_t = dq.T.astype(BF16)
        for part in range(4):
            dq_out[part, cols, :] = dq_t


def attend(block_mask, risk_weight, parts, kv, upstream, tables):
    return pl.pallas_call(
        attend_kernel,
        out_shape=(
            jax.ShapeDtypeStruct((TOK, 256), BF16),
            jax.ShapeDtypeStruct((4, 256, TOK), BF16),
        ),
        in_specs=[in_smem(), in_smem(), *in_vmem(2), in_hbm(), in_hbm()],
        scratch_shapes=[
            pltpu.VMEM((TOK, 256), BF16),
            pltpu.VMEM((TOK, 2 * HEAD), F32),
            pltpu.SemaphoreType.DMA((2,)),
        ],
        compiler_params=params(),
        name="attend",
    )(block_mask, risk_weight, parts, kv, upstream, tables)


def gradient_kernel(where_ref, states_ref, n1, n2, n3, f1, f2, f3, slopes, out, own, sems):
    core = where_ref[0]
    copies = own_columns(where_ref, states_ref, own, sems)
    for copy in copies:
        copy.start()
    for part in range(8):
        cols = pl.ds(256 * (part % 4), 256)
        total = None
        for number in (1, 2, 3, 0):
            if number == 0:
                copies[part].wait()
                x = own[:, pl.ds(256 * part, 256)]
            else:
                x = ((n1, n2, n3) if part < 4 else (f1, f2, f3))[number - 1][:, cols]
            term = jnp.dot(slopes[where_ref[1] ^ number], x, preferred_element_type=F32)
            total = term if total is None else total + term
        out[block_of(part, core)] = total.astype(BF16)


def gradient(where, states, near, far, slopes):
    return pl.pallas_call(
        gradient_kernel,
        out_shape=jax.ShapeDtypeStruct((8, 256, 256), BF16),
        in_specs=[in_smem(), in_hbm(), *in_vmem(7)],
        scratch_shapes=[pltpu.VMEM((TOK, 2048), BF16), pltpu.SemaphoreType.DMA((8,))],
        compiler_params=params(VMEM_MOST),
        name="gradient",
    )(where, states, *near, *far, slopes)


def total_kernel(terms, out):
    total = terms[0].astype(F32)
    for block in range(1, 8):
        total = total + terms[block].astype(F32)
    out[...] = total.T


def add_up(terms):
    return pl.pallas_call(
        total_kernel,
        out_shape=jax.ShapeDtypeStruct((256, 256), F32),
        compiler_params=params(),
        name="add_up",
    )(terms)


def shards(states, query_weight, key_matrix, value_matrix, block_mask, risk_weight, upstream):
    place = lax.axis_index(GROUP)
    where = jnp.stack([lax.axis_index("c"), place]).astype(jnp.int32)

    first, second = pack(where, query_weight, key_matrix.T, value_matrix.T)
    first = lax.ppermute(first, AXES, home_pairs(0))
    second = lax.ppermute(second, AXES, home_pairs(1))
    piece = collect(where, first, second)
    weights = lax.all_gather(piece, OTHERS, axis=0, tiled=False)

    outgoing = cut(where, states, piece)
    near = [swap(outgoing[j - 1], j) for j in (1, 2, 3)]
    far = [swap_core(x) for x in near]

    parts = project(where, states, near, far, weights)
    parts = lax.all_to_all(parts, GROUP, split_axis=0, concat_axis=0)
    kv = jnp.sum(parts[:, 256:].astype(F32), axis=0)
    kv = lax.all_gather(kv, ("xb", "c"), axis=0, tiled=False)

    depths = jnp.sum(block_mask, axis=1) - 1
    places = (depths[:, None] * BS + jnp.arange(BS, dtype=jnp.int32)[None, :]).reshape(TOK)
    frequency = jnp.exp(
        -math.log(1000000.0) * jnp.arange(HEAD // 2, dtype=F32) * 2.0 / HEAD
    )
    angles = places.astype(F32)[:, None] * frequency[None, :]
    cosine, sine = jnp.cos(angles), jnp.sin(angles)
    tables = jnp.concatenate([cosine, cosine, -sine, sine], axis=1)

    attn_out, dq = attend(block_mask, risk_weight, parts, kv, upstream, tables)
    slopes = lax.all_to_all(dq, GROUP, split_axis=0, concat_axis=0)
    terms = gradient(where, states, near, far, slopes)
    terms = lax.all_to_all(terms, OTHERS, split_axis=0, concat_axis=0)
    return attn_out, add_up(terms)


def solution(mesh):
    fine = Mesh(mesh.devices.reshape(SIZES), AXES)
    dp, tensor = AXES[:4], AXES[4:]
    in_specs = (
        P(dp, None),
        P(tensor, dp),
        P(tensor, dp),
        P(tensor, dp),
        P(dp, None),
        P(dp),
        P(dp, tensor),
    )
    out_specs = (P(dp, tensor), P(dp, tensor))
    return jax.shard_map(shards, mesh=fine, in_specs=in_specs, out_specs=out_specs, check_vma=False)
```

```python
import math

import jax
import jax.numpy as jnp
from jax import lax
from jax.experimental import pallas as pl
from jax.experimental.pallas import tpu as pltpu
from jax.sharding import Mesh
from jax.sharding import PartitionSpec as P

HEAD = 128
BS = 64
TOK = 256
AXES = ("zh", "zb", "yu", "yb", "yh", "xh", "xb", "c")
SIZES = (4, 2, 2, 2, 2, 2, 2, 2)
GROUP = ("yu", "yb")
OTHERS = ("zh", "zb")
F32 = jnp.float32
BF16 = jnp.bfloat16
VMEM_LIMIT = 16 * 1024 * 1024


def params():
    return pltpu.CompilerParams(vmem_limit_bytes=VMEM_LIMIT)


def home_pairs(turn):
    pairs = []
    for d in range(32):
        for t in range(16):
            half = (d % 2) ^ turn
            pairs.append((d * 16 + t, (2 * t + half) * 16 + d // 2))
    return pairs


def ring_pairs(first, second):
    pairs = []
    for z in range(8):
        for y in range(8):
            for x in range(4):
                for c in range(2):
                    to = (y + (second if c else first)) % 8

                    def index(y):
                        return (4 * z + y % 4) * 16 + (y // 4) * 8 + 2 * x + c

                    pairs.append((index(y), index(to)))
    return pairs


def swap_core(value):
    return lax.ppermute(value, "c", [(0, 1), (1, 0)])


def block_of(part, core):
    return 4 * (core ^ (part // 4)) + part % 4


def column_of(block, place):
    return pl.multiple_of(1024 * block + 256 * place, 256)


def in_smem():
    return pl.BlockSpec(memory_space=pltpu.SMEM)


def in_vmem(count):
    return [pl.BlockSpec(memory_space=pltpu.VMEM)] * count


def in_hbm():
    return pl.BlockSpec(memory_space=pltpu.HBM)


def anywhere():
    return pl.BlockSpec(memory_space=pl.ANY)


def pack_kernel(where_ref, query, key_t, value_t, first, second):
    odd = where_ref[1] % 2
    for turn, out in enumerate((first, second)):
        half = odd ^ turn
        out[:256, :] = query[pl.ds(pl.multiple_of(256 * half, 256), 256), :]
        for chunk in range(2):
            lanes = pl.ds(pl.multiple_of(256 * half + 128 * chunk, 128), 128)
            base = 256 + 32 * chunk
            out[base : base + 16, :] = key_t[:, lanes]
            out[base + 16 : base + 32, :] = value_t[:, lanes]


def pack(where, query, key_t, value_t):
    part = jax.ShapeDtypeStruct((320, 128), BF16)
    return pl.pallas_call(
        pack_kernel,
        out_shape=(part, part),
        in_specs=[in_smem(), *in_vmem(3)],
        compiler_params=params(),
        name="pack_weights",
    )(where, query, key_t, value_t)


def cut_kernel(where_ref, states_ref, after, up_ref, two_ref, down_ref, sems):
    core, place = where_ref[0], where_ref[1]
    copies = []
    for number, out in enumerate((up_ref, two_ref, down_ref)):
        for part in range(4):
            start = column_of(block_of(part, core), (place + number + 1) % 4)
            copies.append(
                pltpu.make_async_copy(
                    states_ref.at[:, pl.ds(start, 256)],
                    out.at[:, pl.ds(256 * part, 256)],
                    sems.at[len(copies)],
                )
            )
    for copy in copies:
        copy.start()
    for copy in copies:
        copy.wait()


def cut(where, states, after):
    part = jax.ShapeDtypeStruct((TOK, 1024), BF16)
    return pl.pallas_call(
        cut_kernel,
        out_shape=(part, part, part),
        in_specs=[in_smem(), in_hbm(), anywhere()],
        out_specs=tuple(in_vmem(3)),
        scratch_shapes=[pltpu.SemaphoreType.DMA((12,))],
        compiler_params=params(),
        name="cut_states",
    )(where, states, after)


def own_columns(where_ref, states_ref, own, sems):
    copies = []
    for part in range(8):
        start = column_of(block_of(part, where_ref[0]), where_ref[1])
        copies.append(
            pltpu.make_async_copy(
                states_ref.at[:, pl.ds(start, 256)],
                own.at[:, pl.ds(256 * part, 256)],
                sems.at[part],
            )
        )
    return copies


def copies_kernel(where_ref, first, second, out):
    odd = where_ref[1] % 2
    for device in range(8):
        out[device, odd] = first[...]
        out[device, 1 - odd] = second[...]


def copies(where, first, second):
    return pl.pallas_call(
        copies_kernel,
        out_shape=jax.ShapeDtypeStruct((8, 2, 320, 128), BF16),
        in_specs=[in_smem(), *in_vmem(2)],
        compiler_params=params(),
        name="weight_copies",
    )(where, first, second)


def project_kernel(
    where_ref, states_ref, n1, n2, n3, f1, f2, f3, weights, out, own, w_q, w_kv, sems
):
    core = where_ref[0]
    copies = own_columns(where_ref, states_ref, own, sems)
    for copy in copies:
        copy.start()
    for part in range(8):
        block = block_of(part, core)
        for head in range(2):
            rows, cols = pl.ds(256 * part, 256), pl.ds(HEAD * head, HEAD)
            w_q[rows, cols] = weights[block, head, :256, :]
            for chunk in range(2):
                lanes = pl.ds(256 * part + 128 * chunk, 128)
                base = 256 + 32 * chunk
                w_kv[16 * head : 16 * head + 16, lanes] = weights[block, head, base : base + 16, :]
                w_kv[32 + 16 * head : 48 + 16 * head, lanes] = weights[
                    block, head, base + 16 : base + 32, :
                ]

    def product(x, rows):
        q = jnp.dot(x, w_q[rows, :], preferred_element_type=F32)
        kv = lax.dot_general(
            x, w_kv[:, rows], (((1,), (1,)), ((), ())), preferred_element_type=F32
        )
        return q, kv

    low, high = pl.ds(0, 1024), pl.ds(1024, 1024)
    pieces = (
        (n1.at[:, :], f1.at[:, :]),
        (n2.at[:, :], f2.at[:, :]),
        (n3.at[:, :], f3.at[:, :]),
        (own.at[:, low], own.at[:, high]),
    )
    for number, (near_ref, far_ref) in enumerate(pieces):
        if number == 3:
            for copy in copies:
                copy.wait()
        near, far = near_ref[...], far_ref[...]
        other = (where_ref[1] + number + 1) % 4
        q_near, kv_near = product(near, low)
        q_far, kv_far = product(far, high)
        out[other, :256, :] = (q_near + q_far).astype(BF16)
        out[other, 256:, :] = (kv_near + kv_far).T.astype(BF16)


def project(where, states, near, far, weights):
    return pl.pallas_call(
        project_kernel,
        out_shape=(
            jax.ShapeDtypeStruct((4, 320, 256), BF16),
            jax.ShapeDtypeStruct((TOK, 2048), BF16),
        ),
        in_specs=[in_smem(), in_hbm(), *in_vmem(7)],
        scratch_shapes=[
            pltpu.VMEM((2048, 256), BF16),
            pltpu.VMEM((64, 2048), BF16),
            pltpu.SemaphoreType.DMA((8,)),
        ],
        compiler_params=params(),
        name="project",
    )(where, states, *near, *far, weights)


def attend_kernel(
    mask_ref, risk_ref, parts, kv, upstream_ref, tables_ref, attn_out, dq_out, upstream, tables, sems
):
    copies = [
        pltpu.make_async_copy(tables_ref, tables, sems.at[0]),
        pltpu.make_async_copy(upstream_ref, upstream, sems.at[1]),
    ]
    for copy in copies:
        copy.start()
    scaling = 1.0 / math.sqrt(HEAD)
    k_lin = jnp.concatenate([kv[s, :32, :] for s in range(4)], axis=0)
    values = jnp.concatenate([kv[s, 32:, :] for s in range(4)], axis=0).astype(BF16)

    row = lax.broadcasted_iota(jnp.int32, (BS, TOK), 0)
    column = lax.broadcasted_iota(jnp.int32, (BS, TOK), 1)
    seen, risk = [], []
    for b in range(4):
        on_path = jnp.zeros((BS, TOK), jnp.int32)
        for c in range(4):
            on_path = jnp.where(column // BS == c, mask_ref[b, c], on_path)
        seen.append((on_path > 0) & ((column // BS != b) | (column - BS * b <= row)))
        risk.append(jnp.full((BS, 1), risk_ref[b], F32))
    seen = jnp.concatenate(seen, axis=0)
    risk = jnp.concatenate(risk, axis=0)

    copies[0].wait()
    cq, sq = tables[:, :HEAD], tables[:, HEAD:]
    ck, sk = cq[:, :64].T, sq[:, 64:].T
    k1, k2 = k_lin[:64], k_lin[64:]
    keys = jnp.concatenate([k1 * ck - k2 * sk, k2 * ck + k1 * sk], axis=0).astype(BF16)
    copies[1].wait()
    weighted = (upstream[...].astype(F32) * risk).astype(BF16)
    for head in range(2):
        cols = pl.ds(head * HEAD, HEAD)
        q_lin = parts[0, :256, cols].astype(F32)
        for part in range(1, 4):
            q_lin = q_lin + parts[part, :256, cols].astype(F32)
        queries = ((q_lin * cq + pltpu.roll(q_lin, 64, 1) * sq) * scaling).astype(BF16)
        scores = jnp.dot(queries, keys, preferred_element_type=F32)
        raised = jnp.where(seen, jnp.exp(scores), 0.0)
        attend = raised / jnp.sum(raised, axis=1, keepdims=True)
        mixed = lax.dot_general(
            attend.astype(BF16), values, (((1,), (1,)), ((), ())), preferred_element_type=F32
        )
        attn_out[:, cols] = mixed.astype(BF16)
        pressure = jnp.dot(weighted[:, HEAD * head : HEAD * head + HEAD], values, preferred_element_type=F32)
        centre = jnp.sum(attend * pressure, axis=1, keepdims=True)
        slope = (attend * (pressure - centre)).astype(BF16)
        dq_rot = (
            lax.dot_general(slope, keys, (((1,), (1,)), ((), ())), preferred_element_type=F32)
            * scaling
        )
        dq = dq_rot * cq - pltpu.roll(dq_rot, 64, 1) * sq
        dq_t = dq.T.astype(BF16)
        for part in range(4):
            dq_out[part, cols, :] = dq_t


def attend(block_mask, risk_weight, parts, kv, upstream, tables):
    return pl.pallas_call(
        attend_kernel,
        out_shape=(
            jax.ShapeDtypeStruct((TOK, 256), BF16),
            jax.ShapeDtypeStruct((4, 256, TOK), BF16),
        ),
        in_specs=[in_smem(), in_smem(), *in_vmem(2), in_hbm(), in_hbm()],
        scratch_shapes=[
            pltpu.VMEM((TOK, 256), BF16),
            pltpu.VMEM((TOK, 2 * HEAD), F32),
            pltpu.SemaphoreType.DMA((2,)),
        ],
        compiler_params=params(),
        name="attend",
    )(block_mask, risk_weight, parts, kv, upstream, tables)


def gradient_kernel(where_ref, own, n1, n2, n3, f1, f2, f3, slopes, out):
    core = where_ref[0]
    for part in range(8):
        cols = pl.ds(256 * (part % 4), 256)
        total = None
        for number in range(4):
            if number == 0:
                x = own[:, pl.ds(256 * part, 256)]
            else:
                x = ((n1, n2, n3) if part < 4 else (f1, f2, f3))[number - 1][:, cols]
            term = jnp.dot(slopes[(where_ref[1] + number) % 4], x, preferred_element_type=F32)
            total = term if total is None else total + term
        out[block_of(part, core)] = total.astype(BF16)


def gradient(where, own, near, far, slopes):
    return pl.pallas_call(
        gradient_kernel,
        out_shape=jax.ShapeDtypeStruct((8, 256, 256), BF16),
        in_specs=[in_smem(), *in_vmem(8)],
        compiler_params=params(),
        name="gradient",
    )(where, own, *near, *far, slopes)


def total_kernel(terms, out):
    total = terms[0].astype(F32)
    for block in range(1, 8):
        total = total + terms[block].astype(F32)
    out[...] = total.T


def add_up(terms):
    return pl.pallas_call(
        total_kernel,
        out_shape=jax.ShapeDtypeStruct((256, 256), F32),
        compiler_params=params(),
        name="add_up",
    )(terms)


def shards(states, query_weight, key_matrix, value_matrix, block_mask, risk_weight, upstream):
    place = lax.axis_index(GROUP)
    where = jnp.stack([lax.axis_index("c"), place]).astype(jnp.int32)

    first, second = pack(where, query_weight, key_matrix.T, value_matrix.T)
    first = lax.ppermute(first, AXES, home_pairs(0))
    second = lax.ppermute(second, AXES, home_pairs(1))
    weights = copies(where, first, second)

    up, two, down = cut(where, states, weights)
    near = (
        lax.ppermute(down, AXES, ring_pairs(-1, -1)),
        lax.ppermute(two, AXES, ring_pairs(2, -2)),
        lax.ppermute(up, AXES, ring_pairs(1, 1)),
    )
    far = [swap_core(x) for x in near]
    weights = lax.all_to_all(weights, OTHERS, split_axis=0, concat_axis=0)

    parts, own = project(where, states, near, far, weights)
    parts = lax.all_to_all(parts, GROUP, split_axis=0, concat_axis=0)
    kv = jnp.sum(parts[:, 256:].astype(F32), axis=0)
    kv = lax.all_gather(kv, ("xb", "c"), axis=0, tiled=False)

    depths = jnp.sum(block_mask, axis=1) - 1
    places = (depths[:, None] * BS + jnp.arange(BS, dtype=jnp.int32)[None, :]).reshape(TOK)
    frequency = jnp.exp(
        -math.log(1000000.0) * jnp.arange(HEAD // 2, dtype=F32) * 2.0 / HEAD
    )
    angles = places.astype(F32)[:, None] * frequency[None, :]
    cosine, sine = jnp.cos(angles), jnp.sin(angles)
    tables = jnp.concatenate([cosine, cosine, -sine, sine], axis=1)

    attn_out, dq = attend(block_mask, risk_weight, parts, kv, upstream, tables)
    slopes = lax.all_to_all(dq, GROUP, split_axis=0, concat_axis=0)
    terms = gradient(where, own, near, far, slopes)
    terms = lax.all_to_all(terms, OTHERS, split_axis=0, concat_axis=0)
    return attn_out, add_up(terms)


def solution(mesh):
    fine = Mesh(mesh.devices.reshape(SIZES), AXES)
    dp, tensor = AXES[:4], AXES[4:]
    in_specs = (
        P(dp, None),
        P(tensor, dp),
        P(tensor, dp),
        P(tensor, dp),
        P(dp, None),
        P(dp),
        P(dp, tensor),
    )
    out_specs = (P(dp, tensor), P(dp, tensor))
    return jax.shard_map(shards, mesh=fine, in_specs=in_specs, out_specs=out_specs, check_vma=False)
```

```python
import math

import jax
import jax.numpy as jnp
from jax import lax
from jax.experimental import pallas as pl
from jax.experimental.pallas import tpu as pltpu
from jax.sharding import Mesh
from jax.sharding import PartitionSpec as P

HEAD = 128
BS = 64
TOK = 256
AXES = ("zh", "zb", "yu", "yb", "yh", "xh", "xb", "c")
SIZES = (4, 2, 2, 2, 2, 2, 2, 2)
GROUP = ("yu", "yb")
OTHERS = ("zh", "zb")
F32 = jnp.float32
BF16 = jnp.bfloat16
VMEM_LIMIT = 16 * 1024 * 1024


def params():
    return pltpu.CompilerParams(vmem_limit_bytes=VMEM_LIMIT)


def home_pairs(turn):
    pairs = []
    for d in range(32):
        for t in range(16):
            half = (d % 2) ^ turn
            block = 4 * ((t // 2) ^ (d // 4)) + 2 * (t % 2) + half
            pairs.append((d * 16 + t, block * 16 + d // 2))
    return pairs


def ring_pairs(first, second):
    pairs = []
    for z in range(8):
        for y in range(8):
            for x in range(4):
                for c in range(2):
                    to = (y + (second if c else first)) % 8

                    def index(y):
                        return (4 * z + y % 4) * 16 + (y // 4) * 8 + 2 * x + c

                    pairs.append((index(y), index(to)))
    return pairs


def swap_core(value):
    return lax.ppermute(value, "c", [(0, 1), (1, 0)])


def block_of(part, core):
    return 4 * (core ^ (part // 4)) + part % 4


def column_of(block, place):
    return pl.multiple_of(1024 * block + 256 * place, 256)


def in_smem():
    return pl.BlockSpec(memory_space=pltpu.SMEM)


def in_vmem(count):
    return [pl.BlockSpec(memory_space=pltpu.VMEM)] * count


def in_hbm():
    return pl.BlockSpec(memory_space=pltpu.HBM)


def held(value):
    return pltpu.with_memory_space_constraint(value, pltpu.HBM)


def anywhere():
    return pl.BlockSpec(memory_space=pl.ANY)


def pack_kernel(where_ref, query, key_t, value_t, first, second, sems):
    odd = where_ref[1] % 2
    copies = []

    def copy(source, target):
        copies.append(pltpu.make_async_copy(source, target, sems.at[len(copies)]))
        copies[-1].start()

    for turn, out in enumerate((first, second)):
        half = odd ^ turn
        rows = pl.ds(pl.multiple_of(256 * half, 256), 256)
        copy(query.at[rows, :], out.at[pl.ds(0, 256), :])
        for chunk in range(2):
            lanes = pl.ds(pl.multiple_of(256 * half + 128 * chunk, 128), 128)
            base = 256 + 32 * chunk
            copy(key_t.at[:, lanes], out.at[pl.ds(base, 16), :])
            copy(value_t.at[:, lanes], out.at[pl.ds(base + 16, 16), :])
    for each in copies:
        each.wait()


def pack(where, query, key_t, value_t):
    part = jax.ShapeDtypeStruct((320, 128), BF16)
    return pl.pallas_call(
        pack_kernel,
        out_shape=(part, part),
        in_specs=[in_smem(), in_hbm(), in_hbm(), in_hbm()],
        out_specs=tuple(in_vmem(2)),
        scratch_shapes=[pltpu.SemaphoreType.DMA((10,))],
        compiler_params=params(),
        name="pack_weights",
    )(where, held(query), held(key_t), held(value_t))


def cut_kernel(where_ref, states_ref, up_ref, two_ref, down_ref, sems):
    core, place = where_ref[0], where_ref[1]
    copies = []
    for number, out in enumerate((up_ref, two_ref, down_ref)):
        for part in range(4):
            start = column_of(block_of(part, core), (place + number + 1) % 4)
            copies.append(
                pltpu.make_async_copy(
                    states_ref.at[:, pl.ds(start, 256)],
                    out.at[:, pl.ds(256 * part, 256)],
                    sems.at[len(copies)],
                )
            )
    for copy in copies:
        copy.start()
    for copy in copies:
        copy.wait()


def cut(where, states):
    part = jax.ShapeDtypeStruct((TOK, 1024), BF16)
    return pl.pallas_call(
        cut_kernel,
        out_shape=(part, part, part),
        in_specs=[in_smem(), in_hbm()],
        out_specs=tuple(in_vmem(3)),
        scratch_shapes=[pltpu.SemaphoreType.DMA((12,))],
        compiler_params=params(),
        name="cut_states",
    )(where, held(states))


def gate_kernel(*refs):
    del refs


def gate(parts, after):
    count = len(parts)
    return pl.pallas_call(
        gate_kernel,
        out_shape=tuple(jax.ShapeDtypeStruct(x.shape, x.dtype) for x in parts),
        in_specs=[anywhere()] * (count + 1),
        out_specs=tuple([anywhere()] * count),
        input_output_aliases={i: i for i in range(count)},
        compiler_params=params(),
        name="gate",
    )(*parts, after)


def own_columns(where_ref, states_ref, own, sems):
    copies = []
    for part in range(8):
        start = column_of(block_of(part, where_ref[0]), where_ref[1])
        copies.append(
            pltpu.make_async_copy(
                states_ref.at[:, pl.ds(start, 256)],
                own.at[:, pl.ds(256 * part, 256)],
                sems.at[part],
            )
        )
    return copies


def copies_kernel(where_ref, first, second, out):
    odd = where_ref[1] % 2
    for device in range(8):
        out[device, odd] = first[...]
        out[device, 1 - odd] = second[...]


def copies(where, first, second):
    return pl.pallas_call(
        copies_kernel,
        out_shape=jax.ShapeDtypeStruct((8, 2, 320, 128), BF16),
        in_specs=[in_smem(), *in_vmem(2)],
        compiler_params=params(),
        name="weight_copies",
    )(where, first, second)


def project_kernel(
    where_ref, states_ref, n1, n2, n3, f1, f2, f3, weights, out, tokens, w_q, w_kv, result, sems, out_sems
):
    core = where_ref[0]
    arrivals = []
    for number, (near, far) in enumerate(((n1, f1), (n2, f2), (n3, f3))):
        place = tokens.at[number]
        arrivals.append(
            [
                pltpu.make_async_copy(near, place.at[:, pl.ds(0, 1024)], sems.at[8 + 2 * number]),
                pltpu.make_async_copy(far, place.at[:, pl.ds(1024, 1024)], sems.at[9 + 2 * number]),
            ]
        )
    arrivals.append(own_columns(where_ref, states_ref, tokens.at[3], sems))
    for copies in arrivals:
        for copy in copies:
            copy.start()
    for part in range(8):
        block = block_of(part, core) ^ where_ref[2]
        for head in range(2):
            rows, cols = pl.ds(256 * part, 256), pl.ds(HEAD * head, HEAD)
            w_q[rows, cols] = weights[block, head, :256, :]
            for chunk in range(2):
                lanes = pl.ds(256 * part + 128 * chunk, 128)
                base = 256 + 32 * chunk
                w_kv[16 * head : 16 * head + 16, lanes] = weights[block, head, base : base + 16, :]
                w_kv[32 + 16 * head : 48 + 16 * head, lanes] = weights[
                    block, head, base + 16 : base + 32, :
                ]
    departures = []
    for number in range(4):
        for copy in arrivals[number]:
            copy.wait()
        x = tokens[number]
        q = jnp.dot(x, w_q[...], preferred_element_type=F32)
        kv = lax.dot_general(x, w_kv[...], (((1,), (1,)), ((), ())), preferred_element_type=F32)
        result[number, :256, :] = q.astype(BF16)
        result[number, 256:, :] = kv.T.astype(BF16)
        other = (where_ref[1] + number + 1) % 4
        departures.append(
            pltpu.make_async_copy(result.at[number], out.at[other], out_sems.at[number])
        )
        departures[-1].start()
    for copy in departures:
        copy.wait()


def project(where, states, near, far, weights):
    return pl.pallas_call(
        project_kernel,
        out_shape=pltpu.HBM((4, 320, 256), BF16),
        in_specs=[in_smem(), in_hbm(), *[anywhere()] * 6, *in_vmem(1)],
        out_specs=in_hbm(),
        scratch_shapes=[
            pltpu.VMEM((4, TOK, 2048), BF16),
            pltpu.VMEM((2048, 256), BF16),
            pltpu.VMEM((64, 2048), BF16),
            pltpu.VMEM((4, 320, 256), BF16),
            pltpu.SemaphoreType.DMA((14,)),
            pltpu.SemaphoreType.DMA((4,)),
        ],
        compiler_params=params(),
        name="project",
    )(where, held(states), *near, *far, weights)


def attend_kernel(
    mask_ref, risk_ref, parts, kv, upstream_ref, tables_ref, attn_out, dq_out, upstream, tables, sems
):
    copies = [
        pltpu.make_async_copy(tables_ref, tables, sems.at[0]),
        pltpu.make_async_copy(upstream_ref, upstream, sems.at[1]),
    ]
    for copy in copies:
        copy.start()
    scaling = 1.0 / math.sqrt(HEAD)
    k_lin = jnp.concatenate([kv[s, :32, :] for s in range(4)], axis=0)
    values = jnp.concatenate([kv[s, 32:, :] for s in range(4)], axis=0).astype(BF16)

    row = lax.broadcasted_iota(jnp.int32, (BS, TOK), 0)
    column = lax.broadcasted_iota(jnp.int32, (BS, TOK), 1)
    seen, risk = [], []
    for b in range(4):
        on_path = jnp.zeros((BS, TOK), jnp.int32)
        for c in range(4):
            on_path = jnp.where(column // BS == c, mask_ref[b, c], on_path)
        seen.append((on_path > 0) & ((column // BS != b) | (column - BS * b <= row)))
        risk.append(jnp.full((BS, 1), risk_ref[b], F32))
    seen = jnp.concatenate(seen, axis=0)
    risk = jnp.concatenate(risk, axis=0)

    copies[0].wait()
    cq, sq = tables[:, :HEAD], tables[:, HEAD:]
    ck, sk = cq[:, :64].T, sq[:, 64:].T
    k1, k2 = k_lin[:64], k_lin[64:]
    keys = jnp.concatenate([k1 * ck - k2 * sk, k2 * ck + k1 * sk], axis=0).astype(BF16)
    copies[1].wait()
    weighted = (upstream[...].astype(F32) * risk).astype(BF16)
    for head in range(2):
        cols = pl.ds(head * HEAD, HEAD)
        q_lin = parts[0, :256, cols].astype(F32)
        for part in range(1, 4):
            q_lin = q_lin + parts[part, :256, cols].astype(F32)
        queries = ((q_lin * cq + pltpu.roll(q_lin, 64, 1) * sq) * scaling).astype(BF16)
        scores = jnp.dot(queries, keys, preferred_element_type=F32)
        raised = jnp.where(seen, jnp.exp(scores), 0.0)
        attend = raised / jnp.sum(raised, axis=1, keepdims=True)
        mixed = lax.dot_general(
            attend.astype(BF16), values, (((1,), (1,)), ((), ())), preferred_element_type=F32
        )
        attn_out[:, cols] = mixed.astype(BF16)
        pressure = jnp.dot(weighted[:, HEAD * head : HEAD * head + HEAD], values, preferred_element_type=F32)
        centre = jnp.sum(attend * pressure, axis=1, keepdims=True)
        slope = (attend * (pressure - centre)).astype(BF16)
        dq_rot = (
            lax.dot_general(slope, keys, (((1,), (1,)), ((), ())), preferred_element_type=F32)
            * scaling
        )
        dq = dq_rot * cq - pltpu.roll(dq_rot, 64, 1) * sq
        dq_out[cols, :] = dq.T.astype(BF16)


def attend(block_mask, risk_weight, parts, kv, upstream, tables):
    return pl.pallas_call(
        attend_kernel,
        out_shape=(
            jax.ShapeDtypeStruct((TOK, 256), BF16),
            jax.ShapeDtypeStruct((256, TOK), BF16),
        ),
        in_specs=[in_smem(), in_smem(), *in_vmem(2), in_hbm(), in_hbm()],
        scratch_shapes=[
            pltpu.VMEM((TOK, 256), BF16),
            pltpu.VMEM((TOK, 2 * HEAD), F32),
            pltpu.SemaphoreType.DMA((2,)),
        ],
        compiler_params=params(),
        name="attend",
    )(block_mask, risk_weight, parts, kv, held(upstream), held(tables))


def gradient_kernel(where_ref, states_ref, n1, n2, n3, f1, f2, f3, slopes, out, own, sems):
    core = where_ref[0]
    copies = own_columns(where_ref, states_ref, own, sems)
    for copy in copies:
        copy.start()
    for part in range(8):
        cols = pl.ds(256 * (part % 4), 256)
        total = None
        for number in (1, 2, 3, 0):
            if number == 0:
                copies[part].wait()
                x = own[:, pl.ds(256 * part, 256)]
            else:
                x = ((n1, n2, n3) if part < 4 else (f1, f2, f3))[number - 1][:, cols]
            term = jnp.dot(slopes[(where_ref[1] + number) % 4], x, preferred_element_type=F32)
            total = term if total is None else total + term
        out[block_of(part, core)] = total.astype(BF16)


def gradient(where, states, near, far, slopes):
    return pl.pallas_call(
        gradient_kernel,
        out_shape=jax.ShapeDtypeStruct((8, 256, 256), BF16),
        in_specs=[in_smem(), in_hbm(), *in_vmem(7)],
        scratch_shapes=[pltpu.VMEM((TOK, 2048), BF16), pltpu.SemaphoreType.DMA((8,))],
        compiler_params=params(),
        name="gradient",
    )(where, held(states), *near, *far, slopes)


def total_kernel(terms, out):
    total = terms[0].astype(F32)
    for block in range(1, 8):
        total = total + terms[block].astype(F32)
    out[...] = total.T


def add_up(terms):
    return pl.pallas_call(
        total_kernel,
        out_shape=jax.ShapeDtypeStruct((256, 256), F32),
        compiler_params=params(),
        name="add_up",
    )(terms)


def shards(states, query_weight, key_matrix, value_matrix, block_mask, risk_weight, upstream):
    place = lax.axis_index(GROUP)
    plane = lax.axis_index(("yh", "xh", "xb"))
    where = jnp.stack([lax.axis_index("c"), place, plane]).astype(jnp.int32)

    first, second = pack(where, query_weight, key_matrix.T, value_matrix.T)
    first = lax.ppermute(first, AXES, home_pairs(0))
    second = lax.ppermute(second, AXES, home_pairs(1))
    weights = copies(where, first, second)

    up, two, down = gate(cut(where, states), weights)
    near = (
        lax.ppermute(down, AXES, ring_pairs(-1, -1)),
        lax.ppermute(two, AXES, ring_pairs(2, -2)),
        lax.ppermute(up, AXES, ring_pairs(1, 1)),
    )
    far = [swap_core(x) for x in near]
    weights = lax.all_to_all(weights, OTHERS, split_axis=0, concat_axis=0)

    parts = project(where, states, near, far, weights)
    parts = lax.all_to_all(parts, GROUP, split_axis=0, concat_axis=0)
    kv = jnp.sum(parts[:, 256:].astype(F32), axis=0)
    kv = lax.all_gather(kv, ("xb", "c"), axis=0, tiled=False)

    depths = jnp.sum(block_mask, axis=1) - 1
    places = (depths[:, None] * BS + jnp.arange(BS, dtype=jnp.int32)[None, :]).reshape(TOK)
    frequency = jnp.exp(
        -math.log(1000000.0) * jnp.arange(HEAD // 2, dtype=F32) * 2.0 / HEAD
    )
    angles = places.astype(F32)[:, None] * frequency[None, :]
    cosine, sine = jnp.cos(angles), jnp.sin(angles)
    tables = jnp.concatenate([cosine, cosine, -sine, sine], axis=1)

    attn_out, dq = attend(block_mask, risk_weight, parts, kv, upstream, tables)
    slopes = lax.all_gather(dq, GROUP, axis=0, tiled=False)
    terms = gradient(where, states, near, far, slopes)
    terms = lax.all_to_all(terms, OTHERS, split_axis=0, concat_axis=0)
    return attn_out, add_up(terms)


def solution(mesh):
    fine = Mesh(mesh.devices.reshape(SIZES), AXES)
    dp, tensor = AXES[:4], AXES[4:]
    in_specs = (
        P(dp, None),
        P(tensor, dp),
        P(tensor, dp),
        P(tensor, dp),
        P(dp, None),
        P(dp),
        P(dp, tensor),
    )
    out_specs = (P(dp, tensor), P(dp, tensor))
    return jax.shard_map(shards, mesh=fine, in_specs=in_specs, out_specs=out_specs, check_vma=False)
```

```python
import math

import jax
import jax.numpy as jnp
from jax import lax
from jax.experimental import pallas as pl
from jax.experimental.pallas import tpu as pltpu
from jax.sharding import Mesh
from jax.sharding import PartitionSpec as P

HEAD = 128
BS = 64
TOK = 256
AXES = ("zh", "zb", "yu", "yb", "yh", "xh", "xb", "c")
SIZES = (4, 2, 2, 2, 2, 2, 2, 2)
GROUP = ("yu", "yb")
OTHERS = ("zh", "zb")
F32 = jnp.float32
BF16 = jnp.bfloat16
VMEM_LIMIT = 16 * 1024 * 1024


def params():
    return pltpu.CompilerParams(vmem_limit_bytes=VMEM_LIMIT)


def home_pairs(turn):
    pairs = []
    for d in range(32):
        for t in range(16):
            half = (d % 2) ^ turn
            block = 4 * ((t // 2) ^ (d // 4)) + 2 * (t % 2) + half
            pairs.append((d * 16 + t, block * 16 + d // 2))
    return pairs


def ring_pairs(first, second):
    pairs = []
    for z in range(8):
        for y in range(8):
            for x in range(4):
                for c in range(2):
                    to = (y + (second if c else first)) % 8

                    def index(y):
                        return (4 * z + y % 4) * 16 + (y // 4) * 8 + 2 * x + c

                    pairs.append((index(y), index(to)))
    return pairs


def swap_core(value):
    return lax.ppermute(value, "c", [(0, 1), (1, 0)])


def block_of(part, core):
    return 4 * (core ^ (part // 4)) + part % 4


def column_of(block, place):
    return pl.multiple_of(1024 * block + 256 * place, 256)


def in_smem():
    return pl.BlockSpec(memory_space=pltpu.SMEM)


def in_vmem(count):
    return [pl.BlockSpec(memory_space=pltpu.VMEM)] * count


def in_hbm():
    return pl.BlockSpec(memory_space=pltpu.HBM)


def held(value):
    return pltpu.with_memory_space_constraint(value, pltpu.HBM)


def anywhere():
    return pl.BlockSpec(memory_space=pl.ANY)


def pack_kernel(where_ref, query, key_t, value_t, first, second, sems):
    odd = where_ref[1] % 2
    copies = []

    def copy(source, target):
        copies.append(pltpu.make_async_copy(source, target, sems.at[len(copies)]))
        copies[-1].start()

    for turn, out in enumerate((first, second)):
        half = odd ^ turn
        rows = pl.ds(pl.multiple_of(256 * half, 256), 256)
        copy(query.at[rows, :], out.at[pl.ds(0, 256), :])
        for chunk in range(2):
            lanes = pl.ds(pl.multiple_of(256 * half + 128 * chunk, 128), 128)
            base = 256 + 32 * chunk
            copy(key_t.at[:, lanes], out.at[pl.ds(base, 16), :])
            copy(value_t.at[:, lanes], out.at[pl.ds(base + 16, 16), :])
    for each in copies:
        each.wait()


def pack(where, query, key_t, value_t):
    part = jax.ShapeDtypeStruct((320, 128), BF16)
    return pl.pallas_call(
        pack_kernel,
        out_shape=(part, part),
        in_specs=[in_smem(), in_hbm(), in_hbm(), in_hbm()],
        out_specs=tuple(in_vmem(2)),
        scratch_shapes=[pltpu.SemaphoreType.DMA((10,))],
        compiler_params=params(),
        name="pack_weights",
    )(where, held(query), held(key_t), held(value_t))


def cut_kernel(where_ref, states_ref, up_ref, two_ref, down_ref, sems):
    core, place = where_ref[0], where_ref[1]
    copies = []
    for number, out in enumerate((up_ref, two_ref, down_ref)):
        for part in range(4):
            start = column_of(block_of(part, core), (place + number + 1) % 4)
            copies.append(
                pltpu.make_async_copy(
                    states_ref.at[:, pl.ds(start, 256)],
                    out.at[:, pl.ds(256 * part, 256)],
                    sems.at[len(copies)],
                )
            )
    for copy in copies:
        copy.start()
    for copy in copies:
        copy.wait()


def cut(where, states):
    part = jax.ShapeDtypeStruct((TOK, 1024), BF16)
    return pl.pallas_call(
        cut_kernel,
        out_shape=(part, part, part),
        in_specs=[in_smem(), in_hbm()],
        out_specs=tuple(in_vmem(3)),
        scratch_shapes=[pltpu.SemaphoreType.DMA((12,))],
        compiler_params=params(),
        name="cut_states",
    )(where, held(states))


def gate_kernel(*refs):
    del refs


def gate(parts, after):
    count = len(parts)
    return pl.pallas_call(
        gate_kernel,
        out_shape=tuple(jax.ShapeDtypeStruct(x.shape, x.dtype) for x in parts),
        in_specs=[anywhere()] * (count + 1),
        out_specs=tuple([anywhere()] * count),
        input_output_aliases={i: i for i in range(count)},
        compiler_params=params(),
        name="gate",
    )(*parts, after)


def own_columns(where_ref, states_ref, own, sems):
    copies = []
    for part in range(8):
        start = column_of(block_of(part, where_ref[0]), where_ref[1])
        copies.append(
            pltpu.make_async_copy(
                states_ref.at[:, pl.ds(start, 256)],
                own.at[:, pl.ds(256 * part, 256)],
                sems.at[part],
            )
        )
    return copies


def copies_kernel(where_ref, first, second, after, out):
    del after
    odd = where_ref[1] % 2
    for device in range(8):
        out[device, odd] = first[...]
        out[device, 1 - odd] = second[...]


def copies(where, first, second, after):
    return pl.pallas_call(
        copies_kernel,
        out_shape=jax.ShapeDtypeStruct((8, 2, 320, 128), BF16),
        in_specs=[in_smem(), *in_vmem(2), anywhere()],
        compiler_params=params(),
        name="weight_copies",
    )(where, first, second, after)


def project_kernel(
    where_ref, states_ref, n1, n2, n3, f1, f2, f3, weights, out, tokens, w_q, w_kv, result, sems, out_sems
):
    core = where_ref[0]
    arrivals = []
    for number, far in enumerate((f1, f2, f3)):
        place = tokens.at[number, :, pl.ds(0, 1024)]
        arrivals.append([pltpu.make_async_copy(far, place, sems.at[8 + number])])
    arrivals.append(own_columns(where_ref, states_ref, tokens.at[3], sems))
    for copies in arrivals:
        for copy in copies:
            copy.start()
    for part in range(8):
        block = block_of(part, core) ^ where_ref[2]
        for head in range(2):
            rows, cols = pl.ds(256 * part, 256), pl.ds(HEAD * head, HEAD)
            w_q[rows, cols] = weights[block, head, :256, :]
            for chunk in range(2):
                lanes = pl.ds(256 * part + 128 * chunk, 128)
                base = 256 + 32 * chunk
                w_kv[16 * head : 16 * head + 16, lanes] = weights[block, head, base : base + 16, :]
                w_kv[32 + 16 * head : 48 + 16 * head, lanes] = weights[
                    block, head, base + 16 : base + 32, :
                ]
    def product(x, rows):
        q = jnp.dot(x, w_q[rows, :], preferred_element_type=F32)
        kv = lax.dot_general(
            x, w_kv[:, rows], (((1,), (1,)), ((), ())), preferred_element_type=F32
        )
        return q, kv

    low, high = pl.ds(0, 1024), pl.ds(1024, 1024)
    departures = []
    for number, near in enumerate((n1, n2, n3, None)):
        if near is None:
            for copy in arrivals[number]:
                copy.wait()
            q, kv = product(tokens[number], pl.ds(0, 2048))
        else:
            q_near, kv_near = product(near[...], low)
            arrivals[number][0].wait()
            q_far, kv_far = product(tokens[number, :, :1024], high)
            q, kv = q_near + q_far, kv_near + kv_far
        result[number, :256, :] = q.astype(BF16)
        result[number, 256:, :] = kv.T.astype(BF16)
        other = (where_ref[1] + number + 1) % 4
        departures.append(
            pltpu.make_async_copy(result.at[number], out.at[other], out_sems.at[number])
        )
        departures[-1].start()
    for copy in departures:
        copy.wait()


def project(where, states, near, far, weights):
    return pl.pallas_call(
        project_kernel,
        out_shape=pltpu.HBM((4, 320, 256), BF16),
        in_specs=[in_smem(), in_hbm(), *in_vmem(3), *[in_hbm()] * 3, *in_vmem(1)],
        out_specs=in_hbm(),
        scratch_shapes=[
            pltpu.VMEM((4, TOK, 2048), BF16),
            pltpu.VMEM((2048, 256), BF16),
            pltpu.VMEM((64, 2048), BF16),
            pltpu.VMEM((4, 320, 256), BF16),
            pltpu.SemaphoreType.DMA((11,)),
            pltpu.SemaphoreType.DMA((4,)),
        ],
        compiler_params=params(),
        name="project",
    )(where, held(states), *near, *[held(x) for x in far], weights)


def attend_kernel(
    where_ref,
    mask_ref,
    risk_ref,
    parts,
    kv,
    upstream_ref,
    tables_ref,
    states_ref,
    f1_ref,
    f2_ref,
    f3_ref,
    attn_out,
    dq_out,
    own,
    f1,
    f2,
    f3,
    upstream,
    tables,
    sems,
):
    copies = [
        pltpu.make_async_copy(tables_ref, tables, sems.at[8]),
        pltpu.make_async_copy(upstream_ref, upstream, sems.at[9]),
        pltpu.make_async_copy(f1_ref, f1, sems.at[10]),
        pltpu.make_async_copy(f2_ref, f2, sems.at[11]),
        pltpu.make_async_copy(f3_ref, f3, sems.at[12]),
        *own_columns(where_ref, states_ref, own, sems),
    ]
    for copy in copies:
        copy.start()
    scaling = 1.0 / math.sqrt(HEAD)
    k_lin = jnp.concatenate([kv[s, :32, :] for s in range(4)], axis=0)
    values = jnp.concatenate([kv[s, 32:, :] for s in range(4)], axis=0).astype(BF16)

    row = lax.broadcasted_iota(jnp.int32, (BS, TOK), 0)
    column = lax.broadcasted_iota(jnp.int32, (BS, TOK), 1)
    seen, risk = [], []
    for b in range(4):
        on_path = jnp.zeros((BS, TOK), jnp.int32)
        for c in range(4):
            on_path = jnp.where(column // BS == c, mask_ref[b, c], on_path)
        seen.append(jnp.where((column // BS != b) | (column - BS * b <= row), on_path, 0))
        risk.append(jnp.full((BS, 1), risk_ref[b], F32))
    seen = jnp.concatenate(seen, axis=0) > 0
    risk = jnp.concatenate(risk, axis=0)

    copies[0].wait()
    cq, sq = tables[:, :HEAD], tables[:, HEAD:]
    ck, sk = cq[:, :64].T, sq[:, 64:].T
    k1, k2 = k_lin[:64], k_lin[64:]
    keys = jnp.concatenate([k1 * ck - k2 * sk, k2 * ck + k1 * sk], axis=0).astype(BF16)
    copies[1].wait()
    weighted = (upstream[...].astype(F32) * risk).astype(BF16)
    for head in range(2):
        cols = pl.ds(head * HEAD, HEAD)
        q_lin = parts[0, :256, cols].astype(F32)
        for part in range(1, 4):
            q_lin = q_lin + parts[part, :256, cols].astype(F32)
        queries = ((q_lin * cq + pltpu.roll(q_lin, 64, 1) * sq) * scaling).astype(BF16)
        scores = jnp.dot(queries, keys, preferred_element_type=F32)
        raised = jnp.where(seen, jnp.exp(scores), 0.0)
        attend = raised / jnp.sum(raised, axis=1, keepdims=True)
        mixed = lax.dot_general(
            attend.astype(BF16), values, (((1,), (1,)), ((), ())), preferred_element_type=F32
        )
        attn_out[:, cols] = mixed.astype(BF16)
        pressure = jnp.dot(weighted[:, HEAD * head : HEAD * head + HEAD], values, preferred_element_type=F32)
        centre = jnp.sum(attend * pressure, axis=1, keepdims=True)
        slope = (attend * (pressure - centre)).astype(BF16)
        dq_rot = (
            lax.dot_general(slope, keys, (((1,), (1,)), ((), ())), preferred_element_type=F32)
            * scaling
        )
        dq = dq_rot * cq - pltpu.roll(dq_rot, 64, 1) * sq
        dq_out[cols, :] = dq.astype(BF16).T
    for copy in copies[2:]:
        copy.wait()


def attend(where, block_mask, risk_weight, parts, kv, upstream, tables, states, far):
    own = jax.ShapeDtypeStruct((TOK, 2048), BF16)
    part = jax.ShapeDtypeStruct((TOK, 1024), BF16)
    square = jax.ShapeDtypeStruct((TOK, 256), BF16)
    return pl.pallas_call(
        attend_kernel,
        out_shape=(square, square, own, part, part, part),
        in_specs=[*[in_smem()] * 3, *in_vmem(2), *[in_hbm()] * 6],
        out_specs=tuple(in_vmem(6)),
        scratch_shapes=[
            pltpu.VMEM((TOK, 256), BF16),
            pltpu.VMEM((TOK, 2 * HEAD), F32),
            pltpu.SemaphoreType.DMA((13,)),
        ],
        compiler_params=params(),
        name="attend",
    )(
        where,
        block_mask,
        risk_weight,
        parts,
        kv,
        held(upstream),
        held(tables),
        held(states),
        *[held(x) for x in far],
    )


def gradient_kernel(where_ref, own, n1, n2, n3, f1, f2, f3, slopes, out):
    core = where_ref[0]
    for part in range(8):
        cols = pl.ds(256 * (part % 4), 256)
        total = None
        for number in range(4):
            if number == 0:
                x = own[:, pl.ds(256 * part, 256)]
            else:
                x = ((n1, n2, n3) if part < 4 else (f1, f2, f3))[number - 1][:, cols]
            term = jnp.dot(slopes[(where_ref[1] + number) % 4], x, preferred_element_type=F32)
            total = term if total is None else total + term
        out[block_of(part, core)] = total.astype(BF16)


def gradient(where, own, near, far, slopes):
    return pl.pallas_call(
        gradient_kernel,
        out_shape=jax.ShapeDtypeStruct((8, 256, 256), BF16),
        in_specs=[in_smem(), *in_vmem(8)],
        compiler_params=params(),
        name="gradient",
    )(where, own, *near, *far, slopes)


def total_kernel(terms, out):
    total = terms[0].astype(F32)
    for block in range(1, 8):
        total = total + terms[block].astype(F32)
    out[...] = total.T


def add_up(terms):
    return pl.pallas_call(
        total_kernel,
        out_shape=jax.ShapeDtypeStruct((256, 256), F32),
        compiler_params=params(),
        name="add_up",
    )(terms)


def shards(states, query_weight, key_matrix, value_matrix, block_mask, risk_weight, upstream):
    place = lax.axis_index(GROUP)
    plane = lax.axis_index(("yh", "xh", "xb"))
    where = jnp.stack([lax.axis_index("c"), place, plane]).astype(jnp.int32)

    first, second = pack(where, query_weight, key_matrix.T, value_matrix.T)
    first = lax.ppermute(first, AXES, home_pairs(0))
    second = lax.ppermute(second, AXES, home_pairs(1))
    outgoing = cut(where, states)
    weights = copies(where, first, second, outgoing[0])

    up, two, down = gate(outgoing, weights)
    near = (
        lax.ppermute(down, AXES, ring_pairs(-1, -1)),
        lax.ppermute(two, AXES, ring_pairs(2, -2)),
        lax.ppermute(up, AXES, ring_pairs(1, 1)),
    )
    far = [swap_core(x) for x in near]
    weights = lax.all_to_all(weights, OTHERS, split_axis=0, concat_axis=0)

    parts = project(where, states, near, far, weights)
    parts = lax.all_to_all(parts, GROUP, split_axis=0, concat_axis=0)
    kv = jnp.sum(parts[:, 256:].astype(F32), axis=0)
    kv = lax.all_gather(kv, ("xb", "c"), axis=0, tiled=False)

    depths = jnp.sum(block_mask, axis=1) - 1
    places = (depths[:, None] * BS + jnp.arange(BS, dtype=jnp.int32)[None, :]).reshape(TOK)
    frequency = jnp.exp(
        -math.log(1000000.0) * jnp.arange(HEAD // 2, dtype=F32) * 2.0 / HEAD
    )
    angles = places.astype(F32)[:, None] * frequency[None, :]
    cosine, sine = jnp.cos(angles), jnp.sin(angles)
    tables = jnp.concatenate([cosine, cosine, -sine, sine], axis=1)

    attn_out, dq, own, *far = attend(
        where, block_mask, risk_weight, parts, kv, upstream, tables, states, far
    )
    slopes = lax.all_gather(dq, GROUP, axis=0, tiled=False)
    terms = gradient(where, own, near, far, slopes)
    terms = lax.all_to_all(terms, OTHERS, split_axis=0, concat_axis=0)
    return attn_out, add_up(terms)


def solution(mesh):
    fine = Mesh(mesh.devices.reshape(SIZES), AXES)
    dp, tensor = AXES[:4], AXES[4:]
    in_specs = (
        P(dp, None),
        P(tensor, dp),
        P(tensor, dp),
        P(tensor, dp),
        P(dp, None),
        P(dp),
        P(dp, tensor),
    )
    out_specs = (P(dp, tensor), P(dp, tensor))
    return jax.shard_map(shards, mesh=fine, in_specs=in_specs, out_specs=out_specs, check_vma=False)
```

```python
import math

import jax
import jax.numpy as jnp
from jax import lax
from jax.experimental import pallas as pl
from jax.experimental.pallas import tpu as pltpu
from jax.sharding import Mesh
from jax.sharding import PartitionSpec as P

HEAD = 128
BS = 64
TOK = 256
AXES = ("zh", "zb", "yu", "yb", "yh", "xh", "xb", "c")
SIZES = (4, 2, 2, 2, 2, 2, 2, 2)
GROUP = ("yu", "yb")
OTHERS = ("zh", "zb")
SENDERS = ("zh", "zb", "yb")
F32 = jnp.float32
BF16 = jnp.bfloat16
VMEM_LIMIT = 16 * 1024 * 1024


def params():
    return pltpu.CompilerParams(vmem_limit_bytes=VMEM_LIMIT)


def home_pairs():
    pairs = []
    for d in range(32):
        for t in range(16):
            block = 4 * ((t // 2) ^ (d // 4)) + 2 * (t % 2) + d % 2
            pairs.append((d * 16 + t, block * 16 + d // 2))
    return pairs


def ring_pairs(first, second):
    pairs = []
    for z in range(8):
        for y in range(8):
            for x in range(4):
                for c in range(2):
                    to = (y + (second if c else first)) % 8

                    def index(y):
                        return (4 * z + y % 4) * 16 + (y // 4) * 8 + 2 * x + c

                    pairs.append((index(y), index(to)))
    return pairs


def swap_core(value):
    return lax.ppermute(value, "c", [(0, 1), (1, 0)])


def block_of(part, core):
    return 4 * (core ^ (part // 4)) + part % 4


def column_of(block, place):
    return pl.multiple_of(1024 * block + 256 * place, 256)


def in_smem():
    return pl.BlockSpec(memory_space=pltpu.SMEM)


def in_vmem(count):
    return [pl.BlockSpec(memory_space=pltpu.VMEM)] * count


def in_hbm():
    return pl.BlockSpec(memory_space=pltpu.HBM)


def held(value):
    return pltpu.with_memory_space_constraint(value, pltpu.HBM)


def anywhere():
    return pl.BlockSpec(memory_space=pl.ANY)


def pack_kernel(query, key_t, value_t, out, sems):
    copies = []

    def copy(source, target):
        copies.append(pltpu.make_async_copy(source, target, sems.at[len(copies)]))
        copies[-1].start()

    for half in range(2):
        copy(query.at[pl.ds(256 * half, 256), :], out.at[half, pl.ds(0, 256), :])
        for chunk in range(2):
            lanes = pl.ds(256 * half + 128 * chunk, 128)
            base = 256 + 32 * chunk
            copy(key_t.at[:, lanes], out.at[half, pl.ds(base, 16), :])
            copy(value_t.at[:, lanes], out.at[half, pl.ds(base + 16, 16), :])
    for each in copies:
        each.wait()


def pack(query, key_t, value_t):
    return pl.pallas_call(
        pack_kernel,
        out_shape=jax.ShapeDtypeStruct((2, 320, 128), BF16),
        in_specs=[in_hbm(), in_hbm(), in_hbm()],
        out_specs=in_vmem(1)[0],
        scratch_shapes=[pltpu.SemaphoreType.DMA((10,))],
        compiler_params=params(),
        name="pack_weights",
    )(held(query), held(key_t), held(value_t))


def cut_kernel(where_ref, states_ref, up_ref, two_ref, down_ref, columns, sems, out_sems):
    core, place = where_ref[0], where_ref[1]
    copies = []
    for number in range(3):
        for part in range(4):
            start = column_of(block_of(part, core), (place + number + 1) % 4)
            copies.append(
                pltpu.make_async_copy(
                    states_ref.at[:, pl.ds(start, 256)],
                    columns.at[number, :, pl.ds(256 * part, 256)],
                    sems.at[len(copies)],
                )
            )
            copies[-1].start()
    departures = []
    for number, out in enumerate((up_ref, two_ref, down_ref)):
        for copy in copies[4 * number : 4 * number + 4]:
            copy.wait()
        departures.append(pltpu.make_async_copy(columns.at[number], out, out_sems.at[number]))
        departures[-1].start()
    for copy in departures:
        copy.wait()


def cut(where, states):
    return pl.pallas_call(
        cut_kernel,
        out_shape=(pltpu.HBM((TOK, 1024), BF16),) * 3,
        in_specs=[in_smem(), in_hbm()],
        out_specs=(in_hbm(),) * 3,
        scratch_shapes=[
            pltpu.VMEM((3, TOK, 1024), BF16),
            pltpu.SemaphoreType.DMA((12,)),
            pltpu.SemaphoreType.DMA((3,)),
        ],
        compiler_params=params(),
        name="cut_states",
    )(where, held(states))


def gate_kernel(*refs):
    del refs


def gate(parts, after):
    count = len(parts)
    return pl.pallas_call(
        gate_kernel,
        out_shape=tuple(pltpu.HBM(x.shape, x.dtype) for x in parts),
        in_specs=[*[in_hbm()] * count, anywhere()],
        out_specs=tuple([in_hbm()] * count),
        input_output_aliases={i: i for i in range(count)},
        compiler_params=params(),
        name="gate",
    )(*[held(x) for x in parts], after)


def own_columns(where_ref, states_ref, own, sems):
    copies = []
    for part in range(8):
        start = column_of(block_of(part, where_ref[0]), where_ref[1])
        copies.append(
            pltpu.make_async_copy(
                states_ref.at[:, pl.ds(start, 256)],
                own.at[:, pl.ds(256 * part, 256)],
                sems.at[part],
            )
        )
    return copies


def copies_kernel(piece, after, out):
    del after
    for device in range(8):
        out[device] = piece[...]


def copies(piece, after):
    return pl.pallas_call(
        copies_kernel,
        out_shape=jax.ShapeDtypeStruct((8, 2, 320, 128), BF16),
        in_specs=[*in_vmem(1), anywhere()],
        compiler_params=params(),
        name="weight_copies",
    )(piece, after)


def project_kernel(
    where_ref, states_ref, n1, n2, n3, f1, f2, f3, weights, out, own, w_q, w_kv, result, sems, out_sems
):
    core = where_ref[0]
    copies = own_columns(where_ref, states_ref, own, sems)
    for copy in copies:
        copy.start()
    for part in range(8):
        block = block_of(part, core) ^ where_ref[2]
        for head in range(2):
            rows, cols = pl.ds(256 * part, 256), pl.ds(HEAD * head, HEAD)
            w_q[rows, cols] = weights[block, head, :256, :]
            for chunk in range(2):
                lanes = pl.ds(256 * part + 128 * chunk, 128)
                base = 256 + 32 * chunk
                w_kv[16 * head : 16 * head + 16, lanes] = weights[block, head, base : base + 16, :]
                w_kv[32 + 16 * head : 48 + 16 * head, lanes] = weights[
                    block, head, base + 16 : base + 32, :
                ]
    def product(x, rows):
        q = jnp.dot(x, w_q[rows, :], preferred_element_type=F32)
        kv = lax.dot_general(
            x, w_kv[:, rows], (((1,), (1,)), ((), ())), preferred_element_type=F32
        )
        return q, kv

    low, high = pl.ds(0, 1024), pl.ds(1024, 1024)
    departures = []
    for number, (near, far) in enumerate(((n1, f1), (n2, f2), (n3, f3), (None, None))):
        if near is None:
            for copy in copies:
                copy.wait()
            q, kv = product(own[...], pl.ds(0, 2048))
        else:
            q_near, kv_near = product(near[...], low)
            q_far, kv_far = product(far[...], high)
            q, kv = q_near + q_far, kv_near + kv_far
        result[number, :256, :] = q.astype(BF16)
        result[number, 256:, :] = kv.T.astype(BF16)
        other = (where_ref[1] + number + 1) % 4
        departures.append(
            pltpu.make_async_copy(result.at[number], out.at[other], out_sems.at[number])
        )
        departures[-1].start()
    for copy in departures:
        copy.wait()


def project(where, states, near, far, weights):
    return pl.pallas_call(
        project_kernel,
        out_shape=pltpu.HBM((4, 320, 256), BF16),
        in_specs=[in_smem(), in_hbm(), *in_vmem(7)],
        out_specs=in_hbm(),
        scratch_shapes=[
            pltpu.VMEM((TOK, 2048), BF16),
            pltpu.VMEM((2048, 256), BF16),
            pltpu.VMEM((64, 2048), BF16),
            pltpu.VMEM((4, 320, 256), BF16),
            pltpu.SemaphoreType.DMA((8,)),
            pltpu.SemaphoreType.DMA((4,)),
        ],
        compiler_params=params(),
        name="project",
    )(where, held(states), *near, *far, weights)


def attend_kernel(
    where_ref,
    mask_ref,
    risk_ref,
    parts,
    kv,
    upstream_ref,
    tables_ref,
    states_ref,
    attn_out,
    dq_out,
    own,
    upstream,
    tables,
    sems,
):
    copies = [
        pltpu.make_async_copy(tables_ref, tables, sems.at[8]),
        pltpu.make_async_copy(upstream_ref, upstream, sems.at[9]),
        *own_columns(where_ref, states_ref, own, sems),
    ]
    for copy in copies:
        copy.start()
    scaling = 1.0 / math.sqrt(HEAD)
    k_lin = jnp.concatenate([kv[s, :32, :] for s in range(4)], axis=0)
    values = jnp.concatenate([kv[s, 32:, :] for s in range(4)], axis=0).astype(BF16)

    row = lax.broadcasted_iota(jnp.int32, (BS, TOK), 0)
    column = lax.broadcasted_iota(jnp.int32, (BS, TOK), 1)
    seen, risk = [], []
    for b in range(4):
        on_path = jnp.zeros((BS, TOK), jnp.int32)
        for c in range(4):
            on_path = jnp.where(column // BS == c, mask_ref[b, c], on_path)
        seen.append(jnp.where((column // BS != b) | (column - BS * b <= row), on_path, 0))
        risk.append(jnp.full((BS, 1), risk_ref[b], F32))
    seen = jnp.concatenate(seen, axis=0) > 0
    risk = jnp.concatenate(risk, axis=0)

    copies[0].wait()
    cq, sq = tables[:, :HEAD], tables[:, HEAD:]
    ck, sk = cq[:, :64].T, sq[:, 64:].T
    k1, k2 = k_lin[:64], k_lin[64:]
    keys = jnp.concatenate([k1 * ck - k2 * sk, k2 * ck + k1 * sk], axis=0).astype(BF16)
    copies[1].wait()
    weighted = (upstream[...].astype(F32) * risk).astype(BF16)
    for head in range(2):
        cols = pl.ds(head * HEAD, HEAD)
        q_lin = parts[0, :256, cols].astype(F32)
        for part in range(1, 4):
            q_lin = q_lin + parts[part, :256, cols].astype(F32)
        queries = ((q_lin * cq + pltpu.roll(q_lin, 64, 1) * sq) * scaling).astype(BF16)
        scores = jnp.dot(queries, keys, preferred_element_type=F32)
        raised = jnp.where(seen, jnp.exp(scores), 0.0)
        attend = raised / jnp.sum(raised, axis=1, keepdims=True)
        mixed = lax.dot_general(
            attend.astype(BF16), values, (((1,), (1,)), ((), ())), preferred_element_type=F32
        )
        attn_out[:, cols] = mixed.astype(BF16)
        pressure = jnp.dot(weighted[:, HEAD * head : HEAD * head + HEAD], values, preferred_element_type=F32)
        centre = jnp.sum(attend * pressure, axis=1, keepdims=True)
        slope = (attend * (pressure - centre)).astype(BF16)
        dq_rot = (
            lax.dot_general(slope, keys, (((1,), (1,)), ((), ())), preferred_element_type=F32)
            * scaling
        )
        dq = dq_rot * cq - pltpu.roll(dq_rot, 64, 1) * sq
        dq_out[cols, :] = dq.astype(BF16).T
    for copy in copies[2:]:
        copy.wait()


def attend(where, block_mask, risk_weight, parts, kv, upstream, tables, states):
    own = jax.ShapeDtypeStruct((TOK, 2048), BF16)
    square = jax.ShapeDtypeStruct((TOK, 256), BF16)
    return pl.pallas_call(
        attend_kernel,
        out_shape=(square, square, own),
        in_specs=[*[in_smem()] * 3, *in_vmem(2), *[in_hbm()] * 3],
        out_specs=tuple(in_vmem(3)),
        scratch_shapes=[
            pltpu.VMEM((TOK, 256), BF16),
            pltpu.VMEM((TOK, 2 * HEAD), F32),
            pltpu.SemaphoreType.DMA((10,)),
        ],
        compiler_params=params(),
        name="attend",
    )(
        where,
        block_mask,
        risk_weight,
        parts,
        kv,
        held(upstream),
        held(tables),
        held(states),
    )


def gradient_kernel(where_ref, own, n1, n2, n3, f1, f2, f3, slopes, out):
    core = where_ref[0]
    for part in range(8):
        cols = pl.ds(256 * (part % 4), 256)
        total = None
        for number in range(4):
            if number == 0:
                x = own[:, pl.ds(256 * part, 256)]
            else:
                x = ((n1, n2, n3) if part < 4 else (f1, f2, f3))[number - 1][:, cols]
            term = jnp.dot(slopes[(where_ref[1] + number) % 4], x, preferred_element_type=F32)
            total = term if total is None else total + term
        out[block_of(part, core)] = total.astype(BF16)


def gradient(where, own, near, far, slopes):
    return pl.pallas_call(
        gradient_kernel,
        out_shape=jax.ShapeDtypeStruct((8, 256, 256), BF16),
        in_specs=[in_smem(), *in_vmem(8)],
        compiler_params=params(),
        name="gradient",
    )(where, own, *near, *far, slopes)


def total_kernel(terms, out):
    total = terms[0].astype(F32)
    for block in range(1, 8):
        total = total + terms[block].astype(F32)
    out[...] = total.T


def add_up(terms):
    return pl.pallas_call(
        total_kernel,
        out_shape=jax.ShapeDtypeStruct((256, 256), F32),
        compiler_params=params(),
        name="add_up",
    )(terms)


def shards(states, query_weight, key_matrix, value_matrix, block_mask, risk_weight, upstream):
    place = lax.axis_index(GROUP)
    plane = lax.axis_index(("yh", "xh", "xb"))
    where = jnp.stack([lax.axis_index("c"), place, plane]).astype(jnp.int32)

    piece = pack(query_weight, key_matrix.T, value_matrix.T)
    piece = lax.ppermute(piece, AXES, home_pairs())
    outgoing = cut(where, states)
    weights = copies(piece, outgoing[0])

    up, two, down = gate(outgoing, weights)
    near = (
        lax.ppermute(down, AXES, ring_pairs(-1, -1)),
        lax.ppermute(two, AXES, ring_pairs(2, -2)),
        lax.ppermute(up, AXES, ring_pairs(1, 1)),
    )
    far = [swap_core(x) for x in near]
    weights = lax.all_to_all(
        weights.reshape(16, 320, 128), SENDERS, split_axis=0, concat_axis=0
    ).reshape(8, 2, 320, 128)

    parts = project(where, states, near, far, weights)
    parts = lax.all_to_all(parts, GROUP, split_axis=0, concat_axis=0)
    kv = jnp.sum(parts[:, 256:].astype(F32), axis=0)
    kv = lax.all_gather(kv, ("xb", "c"), axis=0, tiled=False)

    depths = jnp.sum(block_mask, axis=1) - 1
    places = (depths[:, None] * BS + jnp.arange(BS, dtype=jnp.int32)[None, :]).reshape(TOK)
    frequency = jnp.exp(
        -math.log(1000000.0) * jnp.arange(HEAD // 2, dtype=F32) * 2.0 / HEAD
    )
    angles = places.astype(F32)[:, None] * frequency[None, :]
    cosine, sine = jnp.cos(angles), jnp.sin(angles)
    tables = jnp.concatenate([cosine, cosine, -sine, sine], axis=1)

    attn_out, dq, own = attend(
        where, block_mask, risk_weight, parts, kv, upstream, tables, states
    )
    slopes = lax.all_gather(dq, GROUP, axis=0, tiled=False)
    terms = gradient(where, own, near, far, slopes)
    terms = lax.all_to_all(terms, OTHERS, split_axis=0, concat_axis=0)
    return attn_out, add_up(terms)


def solution(mesh):
    fine = Mesh(mesh.devices.reshape(SIZES), AXES)
    dp, tensor = AXES[:4], AXES[4:]
    in_specs = (
        P(dp, None),
        P(tensor, dp),
        P(tensor, dp),
        P(tensor, dp),
        P(dp, None),
        P(dp),
        P(dp, tensor),
    )
    out_specs = (P(dp, tensor), P(dp, tensor))
    return jax.shard_map(shards, mesh=fine, in_specs=in_specs, out_specs=out_specs, check_vma=False)
```

```python
import math

import jax
import jax.numpy as jnp
import numpy as np
from jax import lax
from jax.experimental import pallas as pl
from jax.experimental.pallas import tpu as pltpu
from jax.sharding import Mesh
from jax.sharding import PartitionSpec as P

HEAD = 128
BS = 64
TOK = 256
AXES = ("zh", "zb", "yu", "yb", "yh", "xh", "xb", "c")
SIZES = (4, 2, 2, 2, 2, 2, 2, 2)
GROUP = ("yu", "yb")
OTHERS = ("zh", "zb")
F32 = jnp.float32
BF16 = jnp.bfloat16
VMEM_LIMIT = 16 * 1024 * 1024


def params():
    return pltpu.CompilerParams(vmem_limit_bytes=VMEM_LIMIT)


STEPS = ((4, 3, 6, 5), (2, 1, 0, 7))


def resting_z(z, block):
    return (z + STEPS[(z // 4) ^ (block // 4)][(z - block) % 4]) % 8


def home_pairs(turn):
    pairs = []
    for d in range(32):
        for t in range(16):
            half = (d % 2) ^ turn
            block = 4 * resting_z(d // 4, t // 2) + 2 * (t % 2) + half
            pairs.append((d * 16 + t, block * 16 + d // 2))
    return pairs


def ring_pairs(first, second):
    pairs = []
    for z in range(8):
        for y in range(8):
            for x in range(4):
                for c in range(2):
                    to = (y + (second if c else first)) % 8

                    def index(y):
                        return (4 * z + y % 4) * 16 + (y // 4) * 8 + 2 * x + c

                    pairs.append((index(y), index(to)))
    return pairs


def swap_core(value):
    return lax.ppermute(value, "c", [(0, 1), (1, 0)])


def block_of(part, core):
    return 4 * (core ^ (part // 4)) + part % 4


def column_of(block, place):
    return pl.multiple_of(1024 * block + 256 * place, 256)


def in_smem():
    return pl.BlockSpec(memory_space=pltpu.SMEM)


def in_vmem(count):
    return [pl.BlockSpec(memory_space=pltpu.VMEM)] * count


def in_hbm():
    return pl.BlockSpec(memory_space=pltpu.HBM)


def held(value):
    return pltpu.with_memory_space_constraint(value, pltpu.HBM)


def anywhere():
    return pl.BlockSpec(memory_space=pl.ANY)


def pack_kernel(where_ref, query, key_t, value_t, first, second, sems):
    odd = where_ref[1] % 2
    copies = []

    def copy(source, target):
        copies.append(pltpu.make_async_copy(source, target, sems.at[len(copies)]))
        copies[-1].start()

    for turn, out in enumerate((first, second)):
        half = odd ^ turn
        rows = pl.ds(pl.multiple_of(256 * half, 256), 256)
        copy(query.at[rows, :], out.at[pl.ds(0, 256), :])
        for chunk in range(2):
            lanes = pl.ds(pl.multiple_of(256 * half + 128 * chunk, 128), 128)
            base = 256 + 32 * chunk
            copy(key_t.at[:, lanes], out.at[pl.ds(base, 16), :])
            copy(value_t.at[:, lanes], out.at[pl.ds(base + 16, 16), :])
    for each in copies:
        each.wait()


def pack(where, query, key_t, value_t):
    part = jax.ShapeDtypeStruct((320, 128), BF16)
    return pl.pallas_call(
        pack_kernel,
        out_shape=(part, part),
        in_specs=[in_smem(), in_hbm(), in_hbm(), in_hbm()],
        out_specs=tuple(in_vmem(2)),
        scratch_shapes=[pltpu.SemaphoreType.DMA((10,))],
        compiler_params=params(),
        name="pack_weights",
    )(where, held(query), held(key_t), held(value_t))


def cut_kernel(where_ref, states_ref, up_ref, two_ref, down_ref, sems):
    core, place = where_ref[0], where_ref[1]
    copies = []
    for number, out in enumerate((up_ref, two_ref, down_ref)):
        for part in range(4):
            start = column_of(block_of(part, core), (place + number + 1) % 4)
            copies.append(
                pltpu.make_async_copy(
                    states_ref.at[:, pl.ds(start, 256)],
                    out.at[:, pl.ds(256 * part, 256)],
                    sems.at[len(copies)],
                )
            )
    for copy in copies:
        copy.start()
    for copy in copies:
        copy.wait()


def cut(where, states):
    part = jax.ShapeDtypeStruct((TOK, 1024), BF16)
    return pl.pallas_call(
        cut_kernel,
        out_shape=(part, part, part),
        in_specs=[in_smem(), in_hbm()],
        out_specs=tuple(in_vmem(3)),
        scratch_shapes=[pltpu.SemaphoreType.DMA((12,))],
        compiler_params=params(),
        name="cut_states",
    )(where, held(states))


def gate_kernel(*refs):
    del refs


def gate(parts, after):
    count = len(parts)
    return pl.pallas_call(
        gate_kernel,
        out_shape=tuple(jax.ShapeDtypeStruct(x.shape, x.dtype) for x in parts),
        in_specs=[anywhere()] * (count + 1),
        out_specs=tuple([anywhere()] * count),
        input_output_aliases={i: i for i in range(count)},
        compiler_params=params(),
        name="gate",
    )(*parts, after)


def own_columns(where_ref, states_ref, own, sems):
    copies = []
    for part in range(8):
        start = column_of(block_of(part, where_ref[0]), where_ref[1])
        copies.append(
            pltpu.make_async_copy(
                states_ref.at[:, pl.ds(start, 256)],
                own.at[:, pl.ds(256 * part, 256)],
                sems.at[part],
            )
        )
    return copies


def copies_kernel(where_ref, first, second, after, out):
    del after
    odd = where_ref[1] % 2
    for device in range(8):
        out[device, odd] = first[...]
        out[device, 1 - odd] = second[...]


def copies(where, first, second, after):
    return pl.pallas_call(
        copies_kernel,
        out_shape=jax.ShapeDtypeStruct((8, 2, 320, 128), BF16),
        in_specs=[in_smem(), *in_vmem(2), anywhere()],
        compiler_params=params(),
        name="weight_copies",
    )(where, first, second, after)


def project_kernel(
    where_ref,
    states_ref,
    n1,
    n2,
    n3,
    f1,
    f2,
    f3,
    weights_ref,
    out,
    own,
    weights,
    w_q,
    w_kv,
    result,
    sems,
    out_sems,
):
    core = where_ref[0]
    arrivals = []
    for part in range(8):
        block = where_ref[2 + block_of(part, core)]
        arrivals.append(
            pltpu.make_async_copy(weights_ref.at[block], weights.at[part], sems.at[8 + part])
        )
    copies = own_columns(where_ref, states_ref, own, sems)
    for copy in arrivals + copies:
        copy.start()
    for part in range(8):
        arrivals[part].wait()
        for head in range(2):
            rows, cols = pl.ds(256 * part, 256), pl.ds(HEAD * head, HEAD)
            w_q[rows, cols] = weights[part, head, :256, :]
            for chunk in range(2):
                lanes = pl.ds(256 * part + 128 * chunk, 128)
                base = 256 + 32 * chunk
                w_kv[16 * head : 16 * head + 16, lanes] = weights[part, head, base : base + 16, :]
                w_kv[32 + 16 * head : 48 + 16 * head, lanes] = weights[
                    part, head, base + 16 : base + 32, :
                ]
    def product(x, rows):
        q = jnp.dot(x, w_q[rows, :], preferred_element_type=F32)
        kv = lax.dot_general(
            x, w_kv[:, rows], (((1,), (1,)), ((), ())), preferred_element_type=F32
        )
        return q, kv

    low, high = pl.ds(0, 1024), pl.ds(1024, 1024)
    departures = []
    for number, (near, far) in enumerate(((n1, f1), (n2, f2), (n3, f3), (None, None))):
        if near is None:
            for copy in copies:
                copy.wait()
            q, kv = product(own[...], pl.ds(0, 2048))
        else:
            q_near, kv_near = product(near[...], low)
            q_far, kv_far = product(far[...], high)
            q, kv = q_near + q_far, kv_near + kv_far
        result[number, :256, :] = q.astype(BF16)
        result[number, 256:, :] = kv.T.astype(BF16)
        other = (where_ref[1] + number + 1) % 4
        departures.append(
            pltpu.make_async_copy(result.at[number], out.at[other], out_sems.at[number])
        )
        departures[-1].start()
    for copy in departures:
        copy.wait()


def project(where, states, near, far, weights):
    return pl.pallas_call(
        project_kernel,
        out_shape=pltpu.HBM((4, 320, 256), BF16),
        in_specs=[in_smem(), in_hbm(), *in_vmem(6), in_hbm()],
        out_specs=in_hbm(),
        scratch_shapes=[
            pltpu.VMEM((TOK, 2048), BF16),
            pltpu.VMEM((8, 2, 320, 128), BF16),
            pltpu.VMEM((2048, 256), BF16),
            pltpu.VMEM((64, 2048), BF16),
            pltpu.VMEM((4, 320, 256), BF16),
            pltpu.SemaphoreType.DMA((16,)),
            pltpu.SemaphoreType.DMA((4,)),
        ],
        compiler_params=params(),
        name="project",
    )(where, held(states), *near, *far, held(weights))


def attend_kernel(
    where_ref,
    mask_ref,
    risk_ref,
    parts,
    kv,
    upstream_ref,
    tables_ref,
    states_ref,
    attn_out,
    dq_out,
    own,
    upstream,
    tables,
    sems,
):
    copies = [
        pltpu.make_async_copy(tables_ref, tables, sems.at[8]),
        pltpu.make_async_copy(upstream_ref, upstream, sems.at[9]),
        *own_columns(where_ref, states_ref, own, sems),
    ]
    for copy in copies:
        copy.start()
    scaling = 1.0 / math.sqrt(HEAD)
    k_lin = jnp.concatenate([kv[s, :32, :] for s in range(4)], axis=0)
    values = jnp.concatenate([kv[s, 32:, :] for s in range(4)], axis=0).astype(BF16)

    row = lax.broadcasted_iota(jnp.int32, (BS, TOK), 0)
    column = lax.broadcasted_iota(jnp.int32, (BS, TOK), 1)
    seen, risk = [], []
    for b in range(4):
        on_path = jnp.zeros((BS, TOK), jnp.int32)
        for c in range(4):
            on_path = jnp.where(column // BS == c, mask_ref[b, c], on_path)
        seen.append(jnp.where((column // BS != b) | (column - BS * b <= row), on_path, 0))
        risk.append(jnp.full((BS, 1), risk_ref[b], F32))
    seen = jnp.concatenate(seen, axis=0) > 0
    risk = jnp.concatenate(risk, axis=0)

    copies[0].wait()
    cq, sq = tables[:, :HEAD], tables[:, HEAD:]
    ck, sk = cq[:, :64].T, sq[:, 64:].T
    k1, k2 = k_lin[:64], k_lin[64:]
    keys = jnp.concatenate([k1 * ck - k2 * sk, k2 * ck + k1 * sk], axis=0).astype(BF16)
    copies[1].wait()
    weighted = (upstream[...].astype(F32) * risk).astype(BF16)
    for head in range(2):
        cols = pl.ds(head * HEAD, HEAD)
        q_lin = parts[0, :256, cols].astype(F32)
        for part in range(1, 4):
            q_lin = q_lin + parts[part, :256, cols].astype(F32)
        queries = ((q_lin * cq + pltpu.roll(q_lin, 64, 1) * sq) * scaling).astype(BF16)
        scores = jnp.dot(queries, keys, preferred_element_type=F32)
        raised = jnp.where(seen, jnp.exp(scores), 0.0)
        attend = raised / jnp.sum(raised, axis=1, keepdims=True)
        mixed = lax.dot_general(
            attend.astype(BF16), values, (((1,), (1,)), ((), ())), preferred_element_type=F32
        )
        attn_out[:, cols] = mixed.astype(BF16)
        pressure = jnp.dot(weighted[:, HEAD * head : HEAD * head + HEAD], values, preferred_element_type=F32)
        centre = jnp.sum(attend * pressure, axis=1, keepdims=True)
        slope = (attend * (pressure - centre)).astype(BF16)
        dq_rot = (
            lax.dot_general(slope, keys, (((1,), (1,)), ((), ())), preferred_element_type=F32)
            * scaling
        )
        dq = dq_rot * cq - pltpu.roll(dq_rot, 64, 1) * sq
        dq_out[cols, :] = dq.astype(BF16).T
    for copy in copies[2:]:
        copy.wait()


def attend(where, block_mask, risk_weight, parts, kv, upstream, tables, states):
    own = jax.ShapeDtypeStruct((TOK, 2048), BF16)
    square = jax.ShapeDtypeStruct((TOK, 256), BF16)
    return pl.pallas_call(
        attend_kernel,
        out_shape=(square, square, own),
        in_specs=[*[in_smem()] * 3, *in_vmem(2), *[in_hbm()] * 3],
        out_specs=tuple(in_vmem(3)),
        scratch_shapes=[
            pltpu.VMEM((TOK, 256), BF16),
            pltpu.VMEM((TOK, 2 * HEAD), F32),
            pltpu.SemaphoreType.DMA((10,)),
        ],
        compiler_params=params(),
        name="attend",
    )(
        where,
        block_mask,
        risk_weight,
        parts,
        kv,
        held(upstream),
        held(tables),
        held(states),
    )


def gradient_kernel(where_ref, own, n1, n2, n3, f1, f2, f3, slopes, out):
    core = where_ref[0]
    for part in range(8):
        cols = pl.ds(256 * (part % 4), 256)
        total = None
        for number in range(4):
            if number == 0:
                x = own[:, pl.ds(256 * part, 256)]
            else:
                x = ((n1, n2, n3) if part < 4 else (f1, f2, f3))[number - 1][:, cols]
            term = jnp.dot(slopes[(where_ref[1] + number) % 4], x, preferred_element_type=F32)
            total = term if total is None else total + term
        out[block_of(part, core)] = total.astype(BF16)


def gradient(where, own, near, far, slopes):
    return pl.pallas_call(
        gradient_kernel,
        out_shape=jax.ShapeDtypeStruct((8, 256, 256), BF16),
        in_specs=[in_smem(), *in_vmem(8)],
        compiler_params=params(),
        name="gradient",
    )(where, own, *near, *far, slopes)


def total_kernel(terms, out):
    total = terms[0].astype(F32)
    for block in range(1, 8):
        total = total + terms[block].astype(F32)
    out[...] = total.T


def add_up(terms):
    return pl.pallas_call(
        total_kernel,
        out_shape=jax.ShapeDtypeStruct((256, 256), F32),
        compiler_params=params(),
        name="add_up",
    )(terms)


def shards(states, query_weight, key_matrix, value_matrix, block_mask, risk_weight, upstream):
    place = lax.axis_index(GROUP)
    resting = np.array([[resting_z(z, block) for block in range(8)] for z in range(8)], np.int32)
    resting = jnp.asarray(resting)[lax.axis_index(("yh", "xh", "xb"))]
    where = jnp.stack([lax.axis_index("c"), place]).astype(jnp.int32)

    first, second = pack(where, query_weight, key_matrix.T, value_matrix.T)
    first = lax.ppermute(first, AXES, home_pairs(0))
    second = lax.ppermute(second, AXES, home_pairs(1))
    outgoing = cut(where, states)
    weights = copies(where, first, second, outgoing[0])

    up, two, down = gate(outgoing, weights)
    near = (
        lax.ppermute(down, AXES, ring_pairs(-1, -1)),
        lax.ppermute(two, AXES, ring_pairs(2, -2)),
        lax.ppermute(up, AXES, ring_pairs(1, 1)),
    )
    far = [swap_core(x) for x in near]
    weights = lax.all_to_all(weights, OTHERS, split_axis=0, concat_axis=0)

    parts = project(jnp.concatenate([where, resting]), states, near, far, weights)
    parts = lax.all_to_all(parts, GROUP, split_axis=0, concat_axis=0)
    kv = jnp.sum(parts[:, 256:].astype(F32), axis=0)
    kv = lax.all_gather(kv, ("xb", "c"), axis=0, tiled=False)

    depths = jnp.sum(block_mask, axis=1) - 1
    places = (depths[:, None] * BS + jnp.arange(BS, dtype=jnp.int32)[None, :]).reshape(TOK)
    frequency = jnp.exp(
        -math.log(1000000.0) * jnp.arange(HEAD // 2, dtype=F32) * 2.0 / HEAD
    )
    angles = places.astype(F32)[:, None] * frequency[None, :]
    cosine, sine = jnp.cos(angles), jnp.sin(angles)
    tables = jnp.concatenate([cosine, cosine, -sine, sine], axis=1)

    attn_out, dq, own = attend(
        where, block_mask, risk_weight, parts, kv, upstream, tables, states
    )
    slopes = lax.all_gather(dq, GROUP, axis=0, tiled=False)
    terms = gradient(where, own, near, far, slopes)
    terms = lax.all_to_all(terms, OTHERS, split_axis=0, concat_axis=0)
    return attn_out, add_up(terms)


def solution(mesh):
    fine = Mesh(mesh.devices.reshape(SIZES), AXES)
    dp, tensor = AXES[:4], AXES[4:]
    in_specs = (
        P(dp, None),
        P(tensor, dp),
        P(tensor, dp),
        P(tensor, dp),
        P(dp, None),
        P(dp),
        P(dp, tensor),
    )
    out_specs = (P(dp, tensor), P(dp, tensor))
    return jax.shard_map(shards, mesh=fine, in_specs=in_specs, out_specs=out_specs, check_vma=False)
```

```python
import math

import jax
import jax.numpy as jnp
from jax import lax
from jax.experimental import pallas as pl
from jax.experimental.pallas import tpu as pltpu
from jax.sharding import Mesh
from jax.sharding import PartitionSpec as P

HEAD = 128
BS = 64
TOK = 256
AXES = ("zh", "zb", "yu", "yb", "yh", "xh", "xb", "c")
SIZES = (4, 2, 2, 2, 2, 2, 2, 2)
GROUP = ("yu", "yb")
OTHERS = ("zh", "zb")
F32 = jnp.float32
BF16 = jnp.bfloat16
VMEM_LIMIT = 16 * 1024 * 1024


def params():
    return pltpu.CompilerParams(vmem_limit_bytes=VMEM_LIMIT)


def resting_z(z, block):
    way = (z + 4 - block % 4) % 4
    same = 1 - ((z // 4) ^ (block // 4))
    return (z + 10 - way + same * (2 + 4 * (way // 2))) % 8


def home_pairs(turn):
    pairs = []
    for d in range(32):
        for t in range(16):
            half = (d % 2) ^ turn
            block = 4 * resting_z(d // 4, t // 2) + 2 * (t % 2) + half
            pairs.append((d * 16 + t, block * 16 + d // 2))
    return pairs


def ring_pairs(first, second):
    pairs = []
    for z in range(8):
        for y in range(8):
            for x in range(4):
                for c in range(2):
                    to = (y + (second if c else first)) % 8

                    def index(y):
                        return (4 * z + y % 4) * 16 + (y // 4) * 8 + 2 * x + c

                    pairs.append((index(y), index(to)))
    return pairs


def swap_core(value):
    return lax.ppermute(value, "c", [(0, 1), (1, 0)])


def block_of(part, core):
    return 4 * (core ^ (part // 4)) + part % 4


def column_of(block, place):
    return pl.multiple_of(1024 * block + 256 * place, 256)


def in_smem():
    return pl.BlockSpec(memory_space=pltpu.SMEM)


def in_vmem(count):
    return [pl.BlockSpec(memory_space=pltpu.VMEM)] * count


def in_hbm():
    return pl.BlockSpec(memory_space=pltpu.HBM)


def held(value):
    return pltpu.with_memory_space_constraint(value, pltpu.HBM)


def anywhere():
    return pl.BlockSpec(memory_space=pl.ANY)


def pack_kernel(where_ref, query, key_t, value_t, first, second, sems):
    odd = where_ref[1] % 2
    copies = []

    def copy(source, target):
        copies.append(pltpu.make_async_copy(source, target, sems.at[len(copies)]))
        copies[-1].start()

    for turn, out in enumerate((first, second)):
        half = odd ^ turn
        rows = pl.ds(pl.multiple_of(256 * half, 256), 256)
        copy(query.at[rows, :], out.at[pl.ds(0, 256), :])
        for chunk in range(2):
            lanes = pl.ds(pl.multiple_of(256 * half + 128 * chunk, 128), 128)
            base = 256 + 32 * chunk
            copy(key_t.at[:, lanes], out.at[pl.ds(base, 16), :])
            copy(value_t.at[:, lanes], out.at[pl.ds(base + 16, 16), :])
    for each in copies:
        each.wait()


def pack(where, query, key_t, value_t):
    part = jax.ShapeDtypeStruct((320, 128), BF16)
    return pl.pallas_call(
        pack_kernel,
        out_shape=(part, part),
        in_specs=[in_smem(), in_hbm(), in_hbm(), in_hbm()],
        out_specs=tuple(in_vmem(2)),
        scratch_shapes=[pltpu.SemaphoreType.DMA((10,))],
        compiler_params=params(),
        name="pack_weights",
    )(where, held(query), held(key_t), held(value_t))


def cut_kernel(where_ref, states_ref, up_ref, two_ref, down_ref, sems):
    core, place = where_ref[0], where_ref[1]
    copies = []
    for number, out in enumerate((up_ref, two_ref, down_ref)):
        for part in range(4):
            start = column_of(block_of(part, core), (place + number + 1) % 4)
            copies.append(
                pltpu.make_async_copy(
                    states_ref.at[:, pl.ds(start, 256)],
                    out.at[:, pl.ds(256 * part, 256)],
                    sems.at[len(copies)],
                )
            )
    for copy in copies:
        copy.start()
    for copy in copies:
        copy.wait()


def cut(where, states):
    part = jax.ShapeDtypeStruct((TOK, 1024), BF16)
    return pl.pallas_call(
        cut_kernel,
        out_shape=(part, part, part),
        in_specs=[in_smem(), in_hbm()],
        out_specs=tuple(in_vmem(3)),
        scratch_shapes=[pltpu.SemaphoreType.DMA((12,))],
        compiler_params=params(),
        name="cut_states",
    )(where, held(states))


def gate_kernel(*refs):
    del refs


def gate(parts, after):
    count = len(parts)
    return pl.pallas_call(
        gate_kernel,
        out_shape=tuple(jax.ShapeDtypeStruct(x.shape, x.dtype) for x in parts),
        in_specs=[anywhere()] * (count + 1),
        out_specs=tuple([anywhere()] * count),
        input_output_aliases={i: i for i in range(count)},
        compiler_params=params(),
        name="gate",
    )(*parts, after)


def own_columns(where_ref, states_ref, own, sems):
    copies = []
    for part in range(8):
        start = column_of(block_of(part, where_ref[0]), where_ref[1])
        copies.append(
            pltpu.make_async_copy(
                states_ref.at[:, pl.ds(start, 256)],
                own.at[:, pl.ds(256 * part, 256)],
                sems.at[part],
            )
        )
    return copies


def copies_kernel(where_ref, first, second, after, out, sems):
    del after
    odd = where_ref[1] % 2
    sent = []
    for device in range(8):
        for turn, piece in enumerate((first, second)):
            copy = pltpu.make_async_copy(piece, out.at[device, odd ^ turn], sems.at[len(sent)])
            copy.start()
            sent.append(copy)
    for copy in sent:
        copy.wait()


def copies(where, first, second, after):
    return pl.pallas_call(
        copies_kernel,
        out_shape=pltpu.HBM((8, 2, 320, 128), BF16),
        in_specs=[in_smem(), *in_vmem(2), anywhere()],
        out_specs=in_hbm(),
        scratch_shapes=[pltpu.SemaphoreType.DMA((16,))],
        compiler_params=params(),
        name="weight_copies",
    )(where, first, second, after)


def project_kernel(
    where_ref,
    states_ref,
    n1,
    n2,
    n3,
    f1,
    f2,
    f3,
    weights_ref,
    out,
    own,
    weights,
    w_all,
    result,
    sems,
    out_sems,
):
    core = where_ref[0]
    arrivals = []
    for part in range(8):
        block = resting_z(where_ref[2], block_of(part, core))
        arrivals.append(
            pltpu.make_async_copy(weights_ref.at[block], weights.at[part], sems.at[8 + part])
        )
    copies = own_columns(where_ref, states_ref, own, sems)
    for copy in arrivals + copies:
        copy.start()
    for part in range(8):
        arrivals[part].wait()
        start = 256 * part
        for head in range(2):
            w_all[start : start + 256, HEAD * head : HEAD * head + HEAD] = weights[
                part, head, :256, :
            ]
        for chunk in range(2):
            base = 256 + 32 * chunk
            pair = [weights[part, head, base : base + 32, :] for head in range(2)]
            columns = [pair[0][:16], pair[1][:16], pair[0][16:], pair[1][16:]]
            rows = pl.ds(start + 128 * chunk, 128)
            w_all[rows, 256:] = jnp.concatenate(columns, axis=0).T

    def product(x, rows):
        return jnp.dot(x, w_all[rows, :], preferred_element_type=F32)

    low, high = pl.ds(0, 1024), pl.ds(1024, 1024)
    departures = []
    for number, (near, far) in enumerate(((n1, f1), (n2, f2), (n3, f3), (None, None))):
        if near is None:
            for copy in copies:
                copy.wait()
            linear = product(own[...], pl.ds(0, 2048))
        else:
            linear = product(near[...], low) + product(far[...], high)
        result[number, :256, :] = linear[:, :256].astype(BF16)
        result[number, 256:, :] = linear[:, 256:].T.astype(BF16)
        other = (where_ref[1] + number + 1) % 4
        departures.append(
            pltpu.make_async_copy(result.at[number], out.at[other], out_sems.at[number])
        )
        departures[-1].start()
    for copy in departures:
        copy.wait()


def project(where, states, near, far, weights):
    return pl.pallas_call(
        project_kernel,
        out_shape=pltpu.HBM((4, 320, 256), BF16),
        in_specs=[in_smem(), in_hbm(), *in_vmem(6), in_hbm()],
        out_specs=in_hbm(),
        scratch_shapes=[
            pltpu.VMEM((TOK, 2048), BF16),
            pltpu.VMEM((8, 2, 320, 128), BF16),
            pltpu.VMEM((2048, 320), BF16),
            pltpu.VMEM((4, 320, 256), BF16),
            pltpu.SemaphoreType.DMA((16,)),
            pltpu.SemaphoreType.DMA((4,)),
        ],
        compiler_params=params(),
        name="project",
    )(where, held(states), *near, *far, held(weights))


def attend_kernel(
    where_ref,
    mask_ref,
    risk_ref,
    parts,
    kv,
    upstream_ref,
    tables_ref,
    turned_ref,
    states_ref,
    attn_out,
    dq_out,
    own,
    upstream,
    tables,
    turned,
    sems,
):
    copies = [
        pltpu.make_async_copy(tables_ref, tables, sems.at[8]),
        pltpu.make_async_copy(turned_ref, turned, sems.at[9]),
        pltpu.make_async_copy(upstream_ref, upstream, sems.at[10]),
        *own_columns(where_ref, states_ref, own, sems),
    ]
    for copy in copies:
        copy.start()
    scaling = 1.0 / math.sqrt(HEAD)
    k_lin = jnp.concatenate([kv[s, :32, :] for s in range(4)], axis=0)
    values = jnp.concatenate([kv[s, 32:, :] for s in range(4)], axis=0).astype(BF16)

    row = lax.broadcasted_iota(jnp.int32, (BS, TOK), 0)
    column = lax.broadcasted_iota(jnp.int32, (BS, TOK), 1)
    seen, risk = [], []
    for b in range(4):
        on_path = jnp.zeros((BS, TOK), jnp.int32)
        for c in range(4):
            on_path = jnp.where(column // BS == c, mask_ref[b, c], on_path)
        seen.append(jnp.where((column // BS != b) | (column - BS * b <= row), on_path, 0))
        risk.append(jnp.full((BS, 1), risk_ref[b], F32))
    seen = jnp.concatenate(seen, axis=0) > 0
    risk = jnp.concatenate(risk, axis=0)

    copies[0].wait()
    copies[1].wait()
    cq, sq = tables[:, :HEAD], tables[:, HEAD:]
    ck, sk = turned[:64], turned[64:]
    k1, k2 = k_lin[:64], k_lin[64:]
    keys = jnp.concatenate([k1 * ck - k2 * sk, k2 * ck + k1 * sk], axis=0).astype(BF16)
    copies[2].wait()
    weighted = (upstream[...].astype(F32) * risk).astype(BF16)
    for head in range(2):
        cols = pl.ds(head * HEAD, HEAD)
        q_lin = parts[0, :256, cols].astype(F32)
        for part in range(1, 4):
            q_lin = q_lin + parts[part, :256, cols].astype(F32)
        queries = ((q_lin * cq + pltpu.roll(q_lin, 64, 1) * sq) * scaling).astype(BF16)
        scores = jnp.dot(queries, keys, preferred_element_type=F32)
        raised = jnp.where(seen, jnp.exp(scores), 0.0)
        attend = raised / jnp.sum(raised, axis=1, keepdims=True)
        mixed = lax.dot_general(
            attend.astype(BF16), values, (((1,), (1,)), ((), ())), preferred_element_type=F32
        )
        attn_out[:, cols] = mixed.astype(BF16)
        pressure = jnp.dot(weighted[:, HEAD * head : HEAD * head + HEAD], values, preferred_element_type=F32)
        centre = jnp.sum(attend * pressure, axis=1, keepdims=True)
        slope = (attend * (pressure - centre)).astype(BF16)
        turned_dq = (
            lax.dot_general(keys, slope, (((1,), (1,)), ((), ())), preferred_element_type=F32)
            * scaling
        )
        d1, d2 = turned_dq[:64], turned_dq[64:]
        dq_out[HEAD * head : HEAD * head + 64, :] = (d1 * ck + d2 * sk).astype(BF16)
        dq_out[HEAD * head + 64 : HEAD * head + HEAD, :] = (d2 * ck - d1 * sk).astype(BF16)
    for copy in copies[3:]:
        copy.wait()


def attend(where, block_mask, risk_weight, parts, kv, upstream, tables, turned, states):
    own = jax.ShapeDtypeStruct((TOK, 2048), BF16)
    square = jax.ShapeDtypeStruct((TOK, 256), BF16)
    return pl.pallas_call(
        attend_kernel,
        out_shape=(square, square, own),
        in_specs=[*[in_smem()] * 3, *in_vmem(2), *[in_hbm()] * 4],
        out_specs=tuple(in_vmem(3)),
        scratch_shapes=[
            pltpu.VMEM((TOK, 256), BF16),
            pltpu.VMEM((TOK, 2 * HEAD), F32),
            pltpu.VMEM((HEAD, TOK), F32),
            pltpu.SemaphoreType.DMA((11,)),
        ],
        compiler_params=params(),
        name="attend",
    )(
        where,
        block_mask,
        risk_weight,
        parts,
        kv,
        held(upstream),
        held(tables),
        held(turned),
        held(states),
    )


def gradient_kernel(where_ref, own, n1, n2, n3, f1, f2, f3, slopes, out):
    core = where_ref[0]
    for part in range(8):
        cols = pl.ds(256 * (part % 4), 256)
        total = None
        for number in range(4):
            if number == 0:
                x = own[:, pl.ds(256 * part, 256)]
            else:
                x = ((n1, n2, n3) if part < 4 else (f1, f2, f3))[number - 1][:, cols]
            term = jnp.dot(slopes[(where_ref[1] + number) % 4], x, preferred_element_type=F32)
            total = term if total is None else total + term
        out[block_of(part, core)] = total.astype(BF16)


def gradient(where, own, near, far, slopes):
    return pl.pallas_call(
        gradient_kernel,
        out_shape=jax.ShapeDtypeStruct((8, 256, 256), BF16),
        in_specs=[in_smem(), *in_vmem(8)],
        compiler_params=params(),
        name="gradient",
    )(where, own, *near, *far, slopes)


def total_kernel(terms, out):
    total = terms[0].astype(F32)
    for block in range(1, 8):
        total = total + terms[block].astype(F32)
    out[...] = total.T


def add_up(terms):
    return pl.pallas_call(
        total_kernel,
        out_shape=jax.ShapeDtypeStruct((256, 256), F32),
        compiler_params=params(),
        name="add_up",
    )(terms)


def shards(states, query_weight, key_matrix, value_matrix, block_mask, risk_weight, upstream):
    place = lax.axis_index(GROUP)
    plane = lax.axis_index(("yh", "xh", "xb"))
    where = jnp.stack([lax.axis_index("c"), place, plane]).astype(jnp.int32)

    first, second = pack(where, query_weight, key_matrix.T, value_matrix.T)
    first = lax.ppermute(first, AXES, home_pairs(0))
    second = lax.ppermute(second, AXES, home_pairs(1))
    outgoing = cut(where, states)
    weights = copies(where, first, second, outgoing[0])

    (two,) = gate(outgoing[1:2], second)
    up, down = gate((outgoing[0], outgoing[2]), held(weights))
    near = (
        lax.ppermute(down, AXES, ring_pairs(-1, -1)),
        lax.ppermute(two, AXES, ring_pairs(2, -2)),
        lax.ppermute(up, AXES, ring_pairs(1, 1)),
    )
    far = [swap_core(x) for x in near]
    weights = lax.all_to_all(weights, OTHERS, split_axis=0, concat_axis=0)

    parts = project(where, states, near, far, weights)
    parts = lax.all_to_all(parts, GROUP, split_axis=0, concat_axis=0)
    kv = jnp.sum(parts[:, 256:].astype(F32), axis=0)
    kv = lax.all_gather(kv, ("xb", "c"), axis=0, tiled=False)

    depths = jnp.sum(block_mask, axis=1) - 1
    places = (depths[:, None] * BS + jnp.arange(BS, dtype=jnp.int32)[None, :]).reshape(TOK)
    frequency = jnp.exp(
        -math.log(1000000.0) * jnp.arange(HEAD // 2, dtype=F32) * 2.0 / HEAD
    )
    angles = places.astype(F32)[:, None] * frequency[None, :]
    cosine, sine = jnp.cos(angles), jnp.sin(angles)
    tables = jnp.concatenate([cosine, cosine, -sine, sine], axis=1)
    turned = jnp.concatenate([cosine.T, sine.T], axis=0)

    attn_out, dq, own = attend(
        where, block_mask, risk_weight, parts, kv, upstream, tables, turned, states
    )
    slopes = lax.all_gather(dq, GROUP, axis=0, tiled=False)
    terms = gradient(where, own, near, far, slopes)
    terms = lax.all_to_all(terms, OTHERS, split_axis=0, concat_axis=0)
    return attn_out, add_up(terms)


def solution(mesh):
    fine = Mesh(mesh.devices.reshape(SIZES), AXES)
    dp, tensor = AXES[:4], AXES[4:]
    in_specs = (
        P(dp, None),
        P(tensor, dp),
        P(tensor, dp),
        P(tensor, dp),
        P(dp, None),
        P(dp),
        P(dp, tensor),
    )
    out_specs = (P(dp, tensor), P(dp, tensor))
    return jax.shard_map(shards, mesh=fine, in_specs=in_specs, out_specs=out_specs, check_vma=False)
```

```python
import math

import jax
import jax.numpy as jnp
from jax import lax
from jax.experimental import pallas as pl
from jax.experimental.pallas import tpu as pltpu
from jax.sharding import Mesh
from jax.sharding import PartitionSpec as P

HEAD = 128
BS = 64
TOK = 256
AXES = ("zh", "zb", "yu", "yb", "yh", "xh", "xb", "c")
SIZES = (4, 2, 2, 2, 2, 2, 2, 2)
GROUP = ("yu", "yb")
OTHERS = ("zh", "zb")
F32 = jnp.float32
BF16 = jnp.bfloat16
VMEM_LIMIT = 16 * 1024 * 1024


def params():
    return pltpu.CompilerParams(vmem_limit_bytes=VMEM_LIMIT)


def resting_z(z, block):
    way = (z + 4 - block % 4) % 4
    same = 1 - ((z // 4) ^ (block // 4))
    return (z + 10 - way + same * (2 + 4 * (way // 2))) % 8


def home_pairs(turn):
    pairs = []
    for d in range(32):
        for t in range(16):
            half = (d % 2) ^ turn
            block = 4 * resting_z(d // 4, t // 2) + 2 * (t % 2) + half
            pairs.append((d * 16 + t, block * 16 + d // 2))
    return pairs


def ring_pairs(first, second):
    pairs = []
    for z in range(8):
        for y in range(8):
            for x in range(4):
                for c in range(2):
                    to = (y + (second if c else first)) % 8

                    def index(y):
                        return (4 * z + y % 4) * 16 + (y // 4) * 8 + 2 * x + c

                    pairs.append((index(y), index(to)))
    return pairs


def swap_core(value):
    return lax.ppermute(value, "c", [(0, 1), (1, 0)])


def block_of(part, core):
    return 4 * (core ^ (part // 4)) + part % 4


def column_of(block, place):
    return pl.multiple_of(1024 * block + 256 * place, 256)


def in_smem():
    return pl.BlockSpec(memory_space=pltpu.SMEM)


def in_vmem(count):
    return [pl.BlockSpec(memory_space=pltpu.VMEM)] * count


def in_hbm():
    return pl.BlockSpec(memory_space=pltpu.HBM)


def held(value):
    return pltpu.with_memory_space_constraint(value, pltpu.HBM)


def anywhere():
    return pl.BlockSpec(memory_space=pl.ANY)


def pack_kernel(where_ref, query, key_t, value_t, first, second, sems):
    odd = where_ref[1] % 2
    copies = []

    def copy(source, target):
        copies.append(pltpu.make_async_copy(source, target, sems.at[len(copies)]))
        copies[-1].start()

    for turn, out in enumerate((first, second)):
        half = odd ^ turn
        rows = pl.ds(pl.multiple_of(256 * half, 256), 256)
        copy(query.at[rows, :], out.at[pl.ds(0, 256), :])
        for chunk in range(2):
            lanes = pl.ds(pl.multiple_of(256 * half + 128 * chunk, 128), 128)
            base = 256 + 32 * chunk
            copy(key_t.at[:, lanes], out.at[pl.ds(base, 16), :])
            copy(value_t.at[:, lanes], out.at[pl.ds(base + 16, 16), :])
    for each in copies:
        each.wait()


def pack(where, query, key_t, value_t):
    part = jax.ShapeDtypeStruct((320, 128), BF16)
    return pl.pallas_call(
        pack_kernel,
        out_shape=(part, part),
        in_specs=[in_smem(), in_hbm(), in_hbm(), in_hbm()],
        out_specs=tuple(in_vmem(2)),
        scratch_shapes=[pltpu.SemaphoreType.DMA((10,))],
        compiler_params=params(),
        name="pack_weights",
    )(where, held(query), held(key_t), held(value_t))


def cut_kernel(where_ref, states_ref, up_ref, two_ref, down_ref, sems):
    core, place = where_ref[0], where_ref[1]
    copies = []
    for number, out in enumerate((up_ref, two_ref, down_ref)):
        for part in range(4):
            start = column_of(block_of(part, core), (place + number + 1) % 4)
            copies.append(
                pltpu.make_async_copy(
                    states_ref.at[:, pl.ds(start, 256)],
                    out.at[:, pl.ds(256 * part, 256)],
                    sems.at[len(copies)],
                )
            )
    for copy in copies:
        copy.start()
    for copy in copies:
        copy.wait()


def cut(where, states):
    part = jax.ShapeDtypeStruct((TOK, 1024), BF16)
    return pl.pallas_call(
        cut_kernel,
        out_shape=(part, part, part),
        in_specs=[in_smem(), in_hbm()],
        out_specs=tuple(in_vmem(3)),
        scratch_shapes=[pltpu.SemaphoreType.DMA((12,))],
        compiler_params=params(),
        name="cut_states",
    )(where, held(states))


def gate_kernel(*refs):
    del refs


def gate(parts, after, cost=0):
    count = len(parts)
    return pl.pallas_call(
        gate_kernel,
        out_shape=tuple(jax.ShapeDtypeStruct(x.shape, x.dtype) for x in parts),
        in_specs=[anywhere()] * (count + 1),
        out_specs=tuple([anywhere()] * count),
        input_output_aliases={i: i for i in range(count)},
        cost_estimate=pl.CostEstimate(flops=cost, bytes_accessed=0, transcendentals=0),
        compiler_params=params(),
        name="gate",
    )(*parts, after)


def own_columns(where_ref, states_ref, own, sems):
    copies = []
    for part in range(8):
        start = column_of(block_of(part, where_ref[0]), where_ref[1])
        copies.append(
            pltpu.make_async_copy(
                states_ref.at[:, pl.ds(start, 256)],
                own.at[:, pl.ds(256 * part, 256)],
                sems.at[part],
            )
        )
    return copies


def copies_kernel(where_ref, first, second, after, out, sems):
    del after
    odd = where_ref[1] % 2
    sent = []
    for device in range(8):
        for turn, piece in enumerate((first, second)):
            copy = pltpu.make_async_copy(piece, out.at[device, odd ^ turn], sems.at[len(sent)])
            copy.start()
            sent.append(copy)
    for copy in sent:
        copy.wait()


def copies(where, first, second, after):
    return pl.pallas_call(
        copies_kernel,
        out_shape=pltpu.HBM((8, 2, 320, 128), BF16),
        in_specs=[in_smem(), *in_vmem(2), anywhere()],
        out_specs=in_hbm(),
        scratch_shapes=[pltpu.SemaphoreType.DMA((16,))],
        compiler_params=params(),
        name="weight_copies",
    )(where, first, second, after)


def project_kernel(
    where_ref,
    states_ref,
    n1,
    n2,
    n3,
    f1,
    f2,
    f3,
    weights_ref,
    out,
    own,
    weights,
    w_all,
    total,
    result,
    sems,
    out_sems,
):
    core = where_ref[0]
    arrivals = []
    for part in range(8):
        block = resting_z(where_ref[2], block_of(part, core))
        arrivals.append(
            pltpu.make_async_copy(weights_ref.at[block], weights.at[part], sems.at[8 + part])
        )
    copies = own_columns(where_ref, states_ref, own, sems)
    for copy in arrivals + copies:
        copy.start()
    def unpack(part):
        arrivals[part].wait()
        start = 256 * part
        for head in range(2):
            w_all[start : start + 256, HEAD * head : HEAD * head + HEAD] = weights[
                part, head, :256, :
            ]
        for chunk in range(2):
            base = 256 + 32 * chunk
            pair = [weights[part, head, base : base + 32, :] for head in range(2)]
            columns = [pair[0][:16], pair[1][:16], pair[0][16:], pair[1][16:]]
            rows = pl.ds(start + 128 * chunk, 128)
            w_all[rows, 256:] = jnp.concatenate(columns, axis=0).T

    def product(x, rows):
        return jnp.dot(x, w_all[rows, :], preferred_element_type=F32)

    low, high = pl.ds(0, 1024), pl.ds(1024, 1024)
    for part in range(4):
        unpack(part)
    for number, near in enumerate((n1, n2, n3)):
        total[number] = product(near[...], low)
    for part in range(4, 8):
        unpack(part)
    departures = []
    for number, far in enumerate((f1, f2, f3, None)):
        if far is None:
            for copy in copies:
                copy.wait()
            linear = product(own[...], pl.ds(0, 2048))
        else:
            linear = total[number] + product(far[...], high)
        result[number, :256, :] = linear[:, :256].astype(BF16)
        result[number, 256:, :] = linear[:, 256:].T.astype(BF16)
        other = (where_ref[1] + number + 1) % 4
        departures.append(
            pltpu.make_async_copy(result.at[number], out.at[other], out_sems.at[number])
        )
        departures[-1].start()
    for copy in departures:
        copy.wait()


def project(where, states, near, far, weights):
    return pl.pallas_call(
        project_kernel,
        out_shape=pltpu.HBM((4, 320, 256), BF16),
        in_specs=[in_smem(), in_hbm(), *in_vmem(6), in_hbm()],
        out_specs=in_hbm(),
        scratch_shapes=[
            pltpu.VMEM((TOK, 2048), BF16),
            pltpu.VMEM((8, 2, 320, 128), BF16),
            pltpu.VMEM((2048, 320), BF16),
            pltpu.VMEM((3, TOK, 320), F32),
            pltpu.VMEM((4, 320, 256), BF16),
            pltpu.SemaphoreType.DMA((16,)),
            pltpu.SemaphoreType.DMA((4,)),
        ],
        compiler_params=params(),
        name="project",
    )(where, held(states), *near, *far, held(weights))


def attend_kernel(
    where_ref,
    mask_ref,
    risk_ref,
    parts,
    kv,
    upstream_ref,
    tables_ref,
    turned_ref,
    states_ref,
    attn_out,
    dq_out,
    own,
    upstream,
    tables,
    turned,
    sems,
):
    copies = [
        pltpu.make_async_copy(tables_ref, tables, sems.at[8]),
        pltpu.make_async_copy(turned_ref, turned, sems.at[9]),
        pltpu.make_async_copy(upstream_ref, upstream, sems.at[10]),
    ]
    for copy in copies:
        copy.start()
    scaling = 1.0 / math.sqrt(HEAD)
    k_lin = jnp.concatenate([kv[s, :32, :] for s in range(4)], axis=0)
    values = jnp.concatenate([kv[s, 32:, :] for s in range(4)], axis=0).astype(BF16)

    row = lax.broadcasted_iota(jnp.int32, (BS, TOK), 0)
    column = lax.broadcasted_iota(jnp.int32, (BS, TOK), 1)
    seen, risk = [], []
    for b in range(4):
        on_path = jnp.zeros((BS, TOK), jnp.int32)
        for c in range(4):
            on_path = jnp.where(column // BS == c, mask_ref[b, c], on_path)
        seen.append(jnp.where((column // BS != b) | (column - BS * b <= row), on_path, 0))
        risk.append(jnp.full((BS, 1), risk_ref[b], F32))
    seen = jnp.concatenate(seen, axis=0) > 0
    risk = jnp.concatenate(risk, axis=0)

    copies[0].wait()
    copies[1].wait()
    copies[2].wait()
    columns = own_columns(where_ref, states_ref, own, sems)
    for copy in columns:
        copy.start()
    half = lax.broadcasted_iota(jnp.int32, (TOK, HEAD), 1) < HEAD // 2
    table = tables[...]
    turned_table = pltpu.roll(table, HEAD // 2, 1)
    cq = jnp.where(half, table, turned_table)
    sq = jnp.where(half, -turned_table, table)
    ck, sk = turned[:64], turned[64:]
    k1, k2 = k_lin[:64], k_lin[64:]
    keys = jnp.concatenate([k1 * ck - k2 * sk, k2 * ck + k1 * sk], axis=0).astype(BF16)
    weighted = (upstream[...].astype(F32) * risk).astype(BF16)
    for head in range(2):
        cols = pl.ds(head * HEAD, HEAD)
        q_lin = parts[0, :256, cols].astype(F32)
        for part in range(1, 4):
            q_lin = q_lin + parts[part, :256, cols].astype(F32)
        queries = ((q_lin * cq + pltpu.roll(q_lin, 64, 1) * sq) * scaling).astype(BF16)
        scores = jnp.dot(queries, keys, preferred_element_type=F32)
        raised = jnp.where(seen, jnp.exp(scores), 0.0)
        attend = raised / jnp.sum(raised, axis=1, keepdims=True)
        mixed = lax.dot_general(
            attend.astype(BF16), values, (((1,), (1,)), ((), ())), preferred_element_type=F32
        )
        attn_out[:, cols] = mixed.astype(BF16)
        pressure = jnp.dot(weighted[:, HEAD * head : HEAD * head + HEAD], values, preferred_element_type=F32)
        centre = jnp.sum(attend * pressure, axis=1, keepdims=True)
        slope = (attend * (pressure - centre)).astype(BF16)
        turned_dq = (
            lax.dot_general(keys, slope, (((1,), (1,)), ((), ())), preferred_element_type=F32)
            * scaling
        )
        d1, d2 = turned_dq[:64], turned_dq[64:]
        dq_out[HEAD * head : HEAD * head + 64, :] = (d1 * ck + d2 * sk).astype(BF16)
        dq_out[HEAD * head + 64 : HEAD * head + HEAD, :] = (d2 * ck - d1 * sk).astype(BF16)
    for copy in columns:
        copy.wait()


def attend(where, block_mask, risk_weight, parts, kv, upstream, tables, turned, states):
    own = jax.ShapeDtypeStruct((TOK, 2048), BF16)
    square = jax.ShapeDtypeStruct((TOK, 256), BF16)
    return pl.pallas_call(
        attend_kernel,
        out_shape=(square, square, own),
        in_specs=[*[in_smem()] * 3, *in_vmem(2), *[in_hbm()] * 4],
        out_specs=tuple(in_vmem(3)),
        scratch_shapes=[
            pltpu.VMEM((TOK, 256), BF16),
            pltpu.VMEM((TOK, HEAD), F32),
            pltpu.VMEM((HEAD, TOK), F32),
            pltpu.SemaphoreType.DMA((11,)),
        ],
        compiler_params=params(),
        name="attend",
    )(
        where,
        block_mask,
        risk_weight,
        parts,
        kv,
        held(upstream),
        held(tables),
        held(turned),
        held(states),
    )


def gradient_kernel(where_ref, own, n1, n2, n3, f1, f2, f3, slopes, out):
    core = where_ref[0]
    for part in range(8):
        cols = pl.ds(256 * (part % 4), 256)
        total = None
        for number in range(4):
            if number == 0:
                x = own[:, pl.ds(256 * part, 256)]
            else:
                x = ((n1, n2, n3) if part < 4 else (f1, f2, f3))[number - 1][:, cols]
            term = jnp.dot(slopes[(where_ref[1] + number) % 4], x, preferred_element_type=F32)
            total = term if total is None else total + term
        out[block_of(part, core)] = total.astype(BF16)


def gradient(where, own, near, far, slopes):
    return pl.pallas_call(
        gradient_kernel,
        out_shape=jax.ShapeDtypeStruct((8, 256, 256), BF16),
        in_specs=[in_smem(), *in_vmem(8)],
        compiler_params=params(),
        name="gradient",
    )(where, own, *near, *far, slopes)


def total_kernel(terms, out):
    total = terms[0].astype(F32)
    for block in range(1, 8):
        total = total + terms[block].astype(F32)
    out[...] = total.T


def add_up(terms):
    return pl.pallas_call(
        total_kernel,
        out_shape=jax.ShapeDtypeStruct((256, 256), F32),
        compiler_params=params(),
        name="add_up",
    )(terms)


def shards(states, query_weight, key_matrix, value_matrix, block_mask, risk_weight, upstream):
    place = lax.axis_index(GROUP)
    plane = lax.axis_index(("yh", "xh", "xb"))
    where = jnp.stack([lax.axis_index("c"), place, plane]).astype(jnp.int32)

    first, second = pack(where, query_weight, key_matrix.T, value_matrix.T)
    first = lax.ppermute(first, AXES, home_pairs(0))
    second = lax.ppermute(second, AXES, home_pairs(1))
    outgoing = cut(where, states)
    weights = copies(where, first, second, outgoing[0])

    up, two, down = gate(outgoing, second)
    near = (
        lax.ppermute(down, AXES, ring_pairs(-1, -1)),
        lax.ppermute(two, AXES, ring_pairs(2, -2)),
        lax.ppermute(up, AXES, ring_pairs(1, 1)),
    )
    far = [swap_core(x) for x in near]
    tokens = gate((*near, *far), where, cost=10**11)
    near, far = tokens[:3], tokens[3:]
    weights = lax.all_to_all(weights, OTHERS, split_axis=0, concat_axis=0)

    parts = project(where, states, near, far, weights)
    parts = lax.all_to_all(parts, GROUP, split_axis=0, concat_axis=0)
    kv = jnp.sum(parts[:, 256:].astype(F32), axis=0)
    kv = lax.all_gather(kv, ("xb", "c"), axis=0, tiled=False)

    depths = jnp.sum(block_mask, axis=1) - 1
    places = (depths[:, None] * BS + jnp.arange(BS, dtype=jnp.int32)[None, :]).reshape(TOK)
    frequency = jnp.exp(
        -math.log(1000000.0) * jnp.arange(HEAD // 2, dtype=F32) * 2.0 / HEAD
    )
    angles = places.astype(F32)[:, None] * frequency[None, :]
    cosine, sine = jnp.cos(angles), jnp.sin(angles)
    tables = jnp.concatenate([cosine, sine], axis=1)
    turned = jnp.concatenate([cosine.T, sine.T], axis=0)

    attn_out, dq, own = attend(
        where, block_mask, risk_weight, parts, kv, upstream, tables, turned, states
    )
    slopes = lax.all_gather(dq, GROUP, axis=0, tiled=False)
    terms = gradient(where, own, near, far, slopes)
    terms = lax.all_to_all(terms, OTHERS, split_axis=0, concat_axis=0)
    return attn_out, add_up(terms)


def solution(mesh):
    fine = Mesh(mesh.devices.reshape(SIZES), AXES)
    dp, tensor = AXES[:4], AXES[4:]
    in_specs = (
        P(dp, None),
        P(tensor, dp),
        P(tensor, dp),
        P(tensor, dp),
        P(dp, None),
        P(dp),
        P(dp, tensor),
    )
    out_specs = (P(dp, tensor), P(dp, tensor))
    return jax.shard_map(shards, mesh=fine, in_specs=in_specs, out_specs=out_specs, check_vma=False)
```

```python
import functools
import math

import jax
import jax.numpy as jnp
from jax import lax
from jax.experimental import pallas as pl
from jax.experimental.pallas import tpu as pltpu
from jax.sharding import Mesh
from jax.sharding import PartitionSpec as P

HEAD = 128
BS = 64
TOK = 256
AXES = ("zh", "zb", "yu", "yb", "yh", "xh", "xb", "c")
SIZES = (4, 2, 2, 2, 2, 2, 2, 2)
GROUP = ("yu", "yb")
OTHERS = ("zh", "zb")
F32 = jnp.float32
BF16 = jnp.bfloat16
VMEM_LIMIT = 16 * 1024 * 1024


def params():
    return pltpu.CompilerParams(vmem_limit_bytes=VMEM_LIMIT)


def resting_z(z, block):
    way = (z + 4 - block % 4) % 4
    same = 1 - ((z // 4) ^ (block // 4))
    return (z + 10 - way + same * (2 + 4 * (way // 2))) % 8


def home_pairs(turn):
    pairs = []
    for d in range(32):
        for t in range(16):
            half = (d % 2) ^ turn
            block = 4 * resting_z(d // 4, t // 2) + 2 * (t % 2) + half
            pairs.append((d * 16 + t, block * 16 + d // 2))
    return pairs


def ring_pairs(first, second):
    pairs = []
    for z in range(8):
        for y in range(8):
            for x in range(4):
                for c in range(2):
                    to = (y + (second if c else first)) % 8

                    def index(y):
                        return (4 * z + y % 4) * 16 + (y // 4) * 8 + 2 * x + c

                    pairs.append((index(y), index(to)))
    return pairs


def swap_core(value):
    return lax.ppermute(value, "c", [(0, 1), (1, 0)])


def block_of(part, core):
    return 4 * (core ^ (part // 4)) + part % 4


def column_of(block, place):
    return pl.multiple_of(1024 * block + 256 * place, 256)


def in_smem():
    return pl.BlockSpec(memory_space=pltpu.SMEM)


def in_vmem(count):
    return [pl.BlockSpec(memory_space=pltpu.VMEM)] * count


def in_hbm():
    return pl.BlockSpec(memory_space=pltpu.HBM)


def held(value):
    return pltpu.with_memory_space_constraint(value, pltpu.HBM)


def anywhere():
    return pl.BlockSpec(memory_space=pl.ANY)


def pack_kernel(where_ref, query, key_t, value_t, after, first, second, sems):
    del after
    odd = where_ref[1] % 2
    copies = []

    def copy(source, target):
        copies.append(pltpu.make_async_copy(source, target, sems.at[len(copies)]))
        copies[-1].start()

    for turn, out in enumerate((first, second)):
        half = odd ^ turn
        rows = pl.ds(pl.multiple_of(256 * half, 256), 256)
        copy(query.at[rows, :], out.at[pl.ds(0, 256), :])
        for chunk in range(2):
            lanes = pl.ds(pl.multiple_of(256 * half + 128 * chunk, 128), 128)
            base = 256 + 32 * chunk
            copy(key_t.at[:, lanes], out.at[pl.ds(base, 16), :])
            copy(value_t.at[:, lanes], out.at[pl.ds(base + 16, 16), :])
    for each in copies:
        each.wait()


def pack(where, query, key_t, value_t, after):
    part = jax.ShapeDtypeStruct((320, 128), BF16)
    return pl.pallas_call(
        pack_kernel,
        out_shape=(part, part),
        in_specs=[in_smem(), in_hbm(), in_hbm(), in_hbm(), anywhere()],
        out_specs=tuple(in_vmem(2)),
        scratch_shapes=[pltpu.SemaphoreType.DMA((10,))],
        compiler_params=params(),
        name="pack_weights",
    )(where, held(query), held(key_t), held(value_t), after)


def cut_kernel(ways, where_ref, states_ref, *refs):
    core, place = where_ref[0], where_ref[1]
    outs, sems = refs[:-1], refs[-1]
    copies = []
    for way, out in zip(ways, outs):
        for part in range(4):
            start = column_of(block_of(part, core), (place + way) % 4)
            copies.append(
                pltpu.make_async_copy(
                    states_ref.at[:, pl.ds(start, 256)],
                    out.at[:, pl.ds(256 * part, 256)],
                    sems.at[len(copies)],
                )
            )
    for copy in copies:
        copy.start()
    for copy in copies:
        copy.wait()


def cut(where, states, ways):
    part = jax.ShapeDtypeStruct((TOK, 1024), BF16)
    return pl.pallas_call(
        functools.partial(cut_kernel, ways),
        out_shape=(part,) * len(ways),
        in_specs=[in_smem(), in_hbm()],
        out_specs=tuple(in_vmem(len(ways))),
        scratch_shapes=[pltpu.SemaphoreType.DMA((4 * len(ways),))],
        compiler_params=params(),
        name="cut_states",
    )(where, held(states))


def gate_kernel(*refs):
    del refs


def gate(parts, after):
    count = len(parts)
    return pl.pallas_call(
        gate_kernel,
        out_shape=tuple(jax.ShapeDtypeStruct(x.shape, x.dtype) for x in parts),
        in_specs=[anywhere()] * (count + 1),
        out_specs=tuple([anywhere()] * count),
        input_output_aliases={i: i for i in range(count)},
        compiler_params=params(),
        name="gate",
    )(*parts, after)


def own_columns(where_ref, states_ref, own, sems):
    copies = []
    for part in range(8):
        start = column_of(block_of(part, where_ref[0]), where_ref[1])
        copies.append(
            pltpu.make_async_copy(
                states_ref.at[:, pl.ds(start, 256)],
                own.at[:, pl.ds(256 * part, 256)],
                sems.at[part],
            )
        )
    return copies


def copies_kernel(where_ref, first, second, after, out, sems):
    del after
    odd = where_ref[1] % 2
    sent = []
    for device in range(8):
        for turn, piece in enumerate((first, second)):
            copy = pltpu.make_async_copy(piece, out.at[device, odd ^ turn], sems.at[len(sent)])
            copy.start()
            sent.append(copy)
    for copy in sent:
        copy.wait()


def copies(where, first, second, after):
    return pl.pallas_call(
        copies_kernel,
        out_shape=pltpu.HBM((8, 2, 320, 128), BF16),
        in_specs=[in_smem(), *in_vmem(2), anywhere()],
        out_specs=in_hbm(),
        scratch_shapes=[pltpu.SemaphoreType.DMA((16,))],
        compiler_params=params(),
        name="weight_copies",
    )(where, first, second, after)


def project_kernel(
    where_ref,
    states_ref,
    n2,
    f2,
    n1,
    n3,
    f1,
    f3,
    weights,
    out,
    own,
    joined,
    w_all,
    result,
    sems,
    out_sems,
):
    core = where_ref[0]
    copies = own_columns(where_ref, states_ref, own, sems)
    first = [
        pltpu.make_async_copy(n2, joined.at[:, pl.ds(0, 1024)], sems.at[8]),
        pltpu.make_async_copy(f2, joined.at[:, pl.ds(1024, 1024)], sems.at[9]),
    ]
    for copy in first + copies:
        copy.start()
    for part in range(8):
        block = resting_z(where_ref[2], block_of(part, core))
        start = 256 * part
        for head in range(2):
            w_all[start : start + 256, HEAD * head : HEAD * head + HEAD] = weights[
                block, head, :256, :
            ]
        for chunk in range(2):
            base = 256 + 32 * chunk
            pair = [weights[block, head, base : base + 32, :] for head in range(2)]
            columns = [pair[0][:16], pair[1][:16], pair[0][16:], pair[1][16:]]
            rows = pl.ds(start + 128 * chunk, 128)
            w_all[rows, 256:] = jnp.concatenate(columns, axis=0).T

    def product(x, rows):
        return jnp.dot(x, w_all[rows, :], preferred_element_type=F32)

    low, high = pl.ds(0, 1024), pl.ds(1024, 1024)
    departures = []
    for number in (0, 2, 1, 3):
        if number % 2 == 0:
            near, far = ((n1, f1), (n3, f3))[number // 2]
            linear = product(near[...], low) + product(far[...], high)
        else:
            tokens, arrivals = ((joined, first), (own, copies))[number // 3]
            for copy in arrivals:
                copy.wait()
            linear = product(tokens[...], pl.ds(0, 2048))
        result[number, :256, :] = linear[:, :256].astype(BF16)
        result[number, 256:, :] = linear[:, 256:].T.astype(BF16)
        other = (where_ref[1] + number + 1) % 4
        departures.append(
            pltpu.make_async_copy(result.at[number], out.at[other], out_sems.at[number])
        )
        departures[-1].start()
    for copy in departures:
        copy.wait()


def project(where, states, near, far, weights):
    return pl.pallas_call(
        project_kernel,
        out_shape=pltpu.HBM((4, 320, 256), BF16),
        in_specs=[in_smem(), *[in_hbm()] * 3, *in_vmem(5)],
        out_specs=in_hbm(),
        scratch_shapes=[
            pltpu.VMEM((TOK, 2048), BF16),
            pltpu.VMEM((TOK, 2048), BF16),
            pltpu.VMEM((2048, 320), BF16),
            pltpu.VMEM((4, 320, 256), BF16),
            pltpu.SemaphoreType.DMA((10,)),
            pltpu.SemaphoreType.DMA((4,)),
        ],
        compiler_params=params(),
        name="project",
    )(where, held(states), held(near[1]), held(far[1]), *near[::2], *far[::2], weights)


def attend_kernel(
    where_ref,
    mask_ref,
    risk_ref,
    parts,
    kv,
    upstream_ref,
    tables_ref,
    turned_ref,
    states_ref,
    attn_out,
    dq_out,
    own,
    upstream,
    tables,
    turned,
    sems,
):
    copies = [
        pltpu.make_async_copy(tables_ref, tables, sems.at[8]),
        pltpu.make_async_copy(turned_ref, turned, sems.at[9]),
        pltpu.make_async_copy(upstream_ref, upstream, sems.at[10]),
        *own_columns(where_ref, states_ref, own, sems),
    ]
    for copy in copies:
        copy.start()
    scaling = 1.0 / math.sqrt(HEAD)
    k_lin = jnp.concatenate([kv[s, :32, :] for s in range(4)], axis=0)
    values = jnp.concatenate([kv[s, 32:, :] for s in range(4)], axis=0).astype(BF16)

    row = lax.broadcasted_iota(jnp.int32, (BS, TOK), 0)
    column = lax.broadcasted_iota(jnp.int32, (BS, TOK), 1)
    seen, risk = [], []
    for b in range(4):
        on_path = jnp.zeros((BS, TOK), jnp.int32)
        for c in range(4):
            on_path = jnp.where(column // BS == c, mask_ref[b, c], on_path)
        seen.append(jnp.where((column // BS != b) | (column - BS * b <= row), on_path, 0))
        risk.append(jnp.full((BS, 1), risk_ref[b], F32))
    seen = jnp.concatenate(seen, axis=0) > 0
    risk = jnp.concatenate(risk, axis=0)

    copies[0].wait()
    copies[1].wait()
    half = lax.broadcasted_iota(jnp.int32, (TOK, HEAD), 1) < HEAD // 2
    table = tables[...]
    turned_table = pltpu.roll(table, HEAD // 2, 1)
    cq = jnp.where(half, table, turned_table)
    sq = jnp.where(half, -turned_table, table)
    ck, sk = turned[:64], turned[64:]
    k1, k2 = k_lin[:64], k_lin[64:]
    keys = jnp.concatenate([k1 * ck - k2 * sk, k2 * ck + k1 * sk], axis=0).astype(BF16)
    copies[2].wait()
    weighted = (upstream[...].astype(F32) * risk).astype(BF16)
    for head in range(2):
        cols = pl.ds(head * HEAD, HEAD)
        q_lin = parts[0, :256, cols].astype(F32)
        for part in range(1, 4):
            q_lin = q_lin + parts[part, :256, cols].astype(F32)
        queries = ((q_lin * cq + pltpu.roll(q_lin, 64, 1) * sq) * scaling).astype(BF16)
        scores = jnp.dot(queries, keys, preferred_element_type=F32)
        raised = jnp.where(seen, jnp.exp(scores), 0.0)
        attend = raised * (1.0 / jnp.sum(raised, axis=1, keepdims=True))
        mixed = lax.dot_general(
            attend.astype(BF16), values, (((1,), (1,)), ((), ())), preferred_element_type=F32
        )
        attn_out[:, cols] = mixed.astype(BF16)
        pressure = jnp.dot(weighted[:, HEAD * head : HEAD * head + HEAD], values, preferred_element_type=F32)
        centre = jnp.sum(attend * pressure, axis=1, keepdims=True)
        slope = (attend * (pressure - centre)).astype(BF16)
        turned_dq = (
            lax.dot_general(keys, slope, (((1,), (1,)), ((), ())), preferred_element_type=F32)
            * scaling
        )
        d1, d2 = turned_dq[:64], turned_dq[64:]
        dq_out[HEAD * head : HEAD * head + 64, :] = (d1 * ck + d2 * sk).astype(BF16)
        dq_out[HEAD * head + 64 : HEAD * head + HEAD, :] = (d2 * ck - d1 * sk).astype(BF16)
    for copy in copies[3:]:
        copy.wait()


def attend(where, block_mask, risk_weight, parts, kv, upstream, tables, turned, states):
    own = jax.ShapeDtypeStruct((TOK, 2048), BF16)
    square = jax.ShapeDtypeStruct((TOK, 256), BF16)
    return pl.pallas_call(
        attend_kernel,
        out_shape=(square, square, own),
        in_specs=[*[in_smem()] * 3, *in_vmem(2), *[in_hbm()] * 4],
        out_specs=tuple(in_vmem(3)),
        scratch_shapes=[
            pltpu.VMEM((TOK, 256), BF16),
            pltpu.VMEM((TOK, HEAD), F32),
            pltpu.VMEM((HEAD, TOK), F32),
            pltpu.SemaphoreType.DMA((11,)),
        ],
        compiler_params=params(),
        name="attend",
    )(
        where,
        block_mask,
        risk_weight,
        parts,
        kv,
        held(upstream),
        held(tables),
        held(turned),
        held(states),
    )


def gradient_kernel(where_ref, own, n1, n2, n3, f1, f2, f3, slopes, out):
    core = where_ref[0]
    for part in range(8):
        cols = pl.ds(256 * (part % 4), 256)
        total = None
        for number in range(4):
            if number == 0:
                x = own[:, pl.ds(256 * part, 256)]
            else:
                x = ((n1, n2, n3) if part < 4 else (f1, f2, f3))[number - 1][:, cols]
            term = jnp.dot(slopes[(where_ref[1] + number) % 4], x, preferred_element_type=F32)
            total = term if total is None else total + term
        out[block_of(part, core)] = total.astype(BF16)


def gradient(where, own, near, far, slopes):
    return pl.pallas_call(
        gradient_kernel,
        out_shape=jax.ShapeDtypeStruct((8, 256, 256), BF16),
        in_specs=[in_smem(), *in_vmem(8)],
        compiler_params=params(),
        name="gradient",
    )(where, own, *near, *far, slopes)


def total_kernel(terms, out):
    total = terms[0].astype(F32)
    for block in range(1, 8):
        total = total + terms[block].astype(F32)
    out[...] = total.T


def add_up(terms):
    return pl.pallas_call(
        total_kernel,
        out_shape=jax.ShapeDtypeStruct((256, 256), F32),
        compiler_params=params(),
        name="add_up",
    )(terms)


def shards(states, query_weight, key_matrix, value_matrix, block_mask, risk_weight, upstream):
    place = lax.axis_index(GROUP)
    plane = lax.axis_index(("yh", "xh", "xb"))
    where = jnp.stack([lax.axis_index("c"), place, plane]).astype(jnp.int32)

    (two,) = cut(where, states, (2,))
    n2 = lax.ppermute(two, AXES, ring_pairs(2, -2))

    first, second = pack(where, query_weight, key_matrix.T, value_matrix.T, two)
    first = lax.ppermute(first, AXES, home_pairs(0))
    second = lax.ppermute(second, AXES, home_pairs(1))
    outgoing = cut(where, states, (1, 3))
    weights = copies(where, first, second, outgoing[0])

    up, down = gate(outgoing, held(weights))
    n1 = lax.ppermute(down, AXES, ring_pairs(-1, -1))
    n3 = lax.ppermute(up, AXES, ring_pairs(1, 1))
    near = (n1, n2, n3)
    far = [swap_core(x) for x in near]
    weights = lax.all_to_all(weights, OTHERS, split_axis=0, concat_axis=0)

    parts = project(where, states, near, far, weights)
    parts = lax.all_to_all(parts, GROUP, split_axis=0, concat_axis=0)
    kv = jnp.sum(parts[:, 256:].astype(F32), axis=0)
    kv = lax.all_gather(kv, ("xb", "c"), axis=0, tiled=False)

    depths = jnp.sum(block_mask, axis=1) - 1
    places = (depths[:, None] * BS + jnp.arange(BS, dtype=jnp.int32)[None, :]).reshape(TOK)
    frequency = jnp.exp(
        -math.log(1000000.0) * jnp.arange(HEAD // 2, dtype=F32) * 2.0 / HEAD
    )
    angles = places.astype(F32)[:, None] * frequency[None, :]
    cosine, sine = jnp.cos(angles), jnp.sin(angles)
    tables = jnp.concatenate([cosine, sine], axis=1)
    turned = jnp.concatenate([cosine.T, sine.T], axis=0)

    attn_out, dq, own = attend(
        where, block_mask, risk_weight, parts, kv, upstream, tables, turned, states
    )
    slopes = lax.all_gather(dq, GROUP, axis=0, tiled=False)
    terms = gradient(where, own, near, far, slopes)
    terms = lax.all_to_all(terms, OTHERS, split_axis=0, concat_axis=0)
    return attn_out, add_up(terms)


def solution(mesh):
    fine = Mesh(mesh.devices.reshape(SIZES), AXES)
    dp, tensor = AXES[:4], AXES[4:]
    in_specs = (
        P(dp, None),
        P(tensor, dp),
        P(tensor, dp),
        P(tensor, dp),
        P(dp, None),
        P(dp),
        P(dp, tensor),
    )
    out_specs = (P(dp, tensor), P(dp, tensor))
    return jax.shard_map(shards, mesh=fine, in_specs=in_specs, out_specs=out_specs, check_vma=False)
```

```python
import functools
import math

import jax
import jax.numpy as jnp
from jax import lax
from jax.experimental import pallas as pl
from jax.experimental.pallas import tpu as pltpu
from jax.sharding import Mesh
from jax.sharding import PartitionSpec as P

HEAD = 128
BS = 64
TOK = 256
AXES = ("zh", "zb", "yu", "yb", "yh", "xh", "xb", "c")
SIZES = (4, 2, 2, 2, 2, 2, 2, 2)
GROUP = ("yu", "yb")
OTHERS = ("zh", "zb")
F32 = jnp.float32
BF16 = jnp.bfloat16
VMEM_LIMIT = 16 * 1024 * 1024


def params():
    return pltpu.CompilerParams(vmem_limit_bytes=VMEM_LIMIT)


def resting_z(z, block):
    way = (z + 4 - block % 4) % 4
    same = 1 - ((z // 4) ^ (block // 4))
    return (z + 10 - way + same * (2 + 4 * (way // 2))) % 8


def home_pairs(turn):
    pairs = []
    for d in range(32):
        for t in range(16):
            half = (d % 2) ^ turn
            block = 4 * resting_z(d // 4, t // 2) + 2 * (t % 2) + half
            pairs.append((d * 16 + t, block * 16 + d // 2))
    return pairs


def ring_pairs(first, second):
    pairs = []
    for z in range(8):
        for y in range(8):
            for x in range(4):
                for c in range(2):
                    to = (y + (second if c else first)) % 8

                    def index(y):
                        return (4 * z + y % 4) * 16 + (y // 4) * 8 + 2 * x + c

                    pairs.append((index(y), index(to)))
    return pairs


def swap_core(value):
    return lax.ppermute(value, "c", [(0, 1), (1, 0)])


def block_of(part, core):
    return 4 * (core ^ (part // 4)) + part % 4


def column_of(block, place):
    return pl.multiple_of(1024 * block + 256 * place, 256)


def in_smem():
    return pl.BlockSpec(memory_space=pltpu.SMEM)


def in_vmem(count):
    return [pl.BlockSpec(memory_space=pltpu.VMEM)] * count


def in_hbm():
    return pl.BlockSpec(memory_space=pltpu.HBM)


def held(value):
    return pltpu.with_memory_space_constraint(value, pltpu.HBM)


def anywhere():
    return pl.BlockSpec(memory_space=pl.ANY)


def pack_kernel(where_ref, query, key_t, value_t, after, first, second, sems):
    del after
    odd = where_ref[1] % 2
    copies = []

    def copy(source, target):
        copies.append(pltpu.make_async_copy(source, target, sems.at[len(copies)]))
        copies[-1].start()

    for turn, out in enumerate((first, second)):
        half = odd ^ turn
        rows = pl.ds(pl.multiple_of(256 * half, 256), 256)
        copy(query.at[rows, :], out.at[pl.ds(0, 256), :])
        for chunk in range(2):
            lanes = pl.ds(pl.multiple_of(256 * half + 128 * chunk, 128), 128)
            base = 256 + 32 * chunk
            copy(key_t.at[:, lanes], out.at[pl.ds(base, 16), :])
            copy(value_t.at[:, lanes], out.at[pl.ds(base + 16, 16), :])
    for each in copies:
        each.wait()


def pack(where, query, key_t, value_t, after):
    part = jax.ShapeDtypeStruct((320, 128), BF16)
    return pl.pallas_call(
        pack_kernel,
        out_shape=(part, part),
        in_specs=[in_smem(), in_hbm(), in_hbm(), in_hbm(), anywhere()],
        out_specs=tuple(in_vmem(2)),
        scratch_shapes=[pltpu.SemaphoreType.DMA((10,))],
        compiler_params=params(),
        name="pack_weights",
    )(where, held(query), held(key_t), held(value_t), after)


def cut_kernel(ways, where_ref, states_ref, *refs):
    core, place = where_ref[0], where_ref[1]
    outs, sems = refs[:-1], refs[-1]
    copies = []
    for way, out in zip(ways, outs):
        for part in range(4):
            start = column_of(block_of(part, core), (place + way) % 4)
            copies.append(
                pltpu.make_async_copy(
                    states_ref.at[:, pl.ds(start, 256)],
                    out.at[:, pl.ds(256 * part, 256)],
                    sems.at[len(copies)],
                )
            )
    for copy in copies:
        copy.start()
    for copy in copies:
        copy.wait()


def cut(where, states, ways):
    part = jax.ShapeDtypeStruct((TOK, 1024), BF16)
    return pl.pallas_call(
        functools.partial(cut_kernel, ways),
        out_shape=(part,) * len(ways),
        in_specs=[in_smem(), in_hbm()],
        out_specs=tuple(in_vmem(len(ways))),
        scratch_shapes=[pltpu.SemaphoreType.DMA((4 * len(ways),))],
        compiler_params=params(),
        name="cut_states",
    )(where, held(states))


def gate_kernel(*refs):
    del refs


def gate(parts, after):
    count = len(parts)
    return pl.pallas_call(
        gate_kernel,
        out_shape=tuple(jax.ShapeDtypeStruct(x.shape, x.dtype) for x in parts),
        in_specs=[anywhere()] * (count + 1),
        out_specs=tuple([anywhere()] * count),
        input_output_aliases={i: i for i in range(count)},
        compiler_params=params(),
        name="gate",
    )(*parts, after)


def own_columns(where_ref, states_ref, own, sems):
    copies = []
    for part in range(8):
        start = column_of(block_of(part, where_ref[0]), where_ref[1])
        copies.append(
            pltpu.make_async_copy(
                states_ref.at[:, pl.ds(start, 256)],
                own.at[:, pl.ds(256 * part, 256)],
                sems.at[part],
            )
        )
    return copies


def copies_kernel(where_ref, first, second, after, later, out, sems):
    del after, later
    odd = where_ref[1] % 2
    sent = []
    for device in range(8):
        for turn, piece in enumerate((first, second)):
            copy = pltpu.make_async_copy(piece, out.at[device, odd ^ turn], sems.at[len(sent)])
            copy.start()
            sent.append(copy)
    for copy in sent:
        copy.wait()


def copies(where, first, second, after, later):
    return pl.pallas_call(
        copies_kernel,
        out_shape=pltpu.HBM((8, 2, 320, 128), BF16),
        in_specs=[in_smem(), *in_vmem(2), anywhere(), anywhere()],
        out_specs=in_hbm(),
        scratch_shapes=[pltpu.SemaphoreType.DMA((16,))],
        compiler_params=params(),
        name="weight_copies",
    )(where, first, second, after, later)


def project_kernel(
    where_ref,
    states_ref,
    n2,
    f2,
    n1,
    n3,
    f1,
    f3,
    weights,
    out,
    own,
    joined,
    w_q,
    w_kv,
    result,
    sems,
    out_sems,
):
    core = where_ref[0]
    copies = own_columns(where_ref, states_ref, own, sems)
    first = [
        pltpu.make_async_copy(n2, joined.at[:, pl.ds(0, 1024)], sems.at[8]),
        pltpu.make_async_copy(f2, joined.at[:, pl.ds(1024, 1024)], sems.at[9]),
    ]
    for copy in first + copies:
        copy.start()
    for part in range(8):
        block = resting_z(where_ref[2], block_of(part, core))
        start = 256 * part
        for head in range(2):
            rows, cols = pl.ds(start, 256), pl.ds(HEAD * head, HEAD)
            w_q[rows, cols] = weights[block, head, :256, :]
            for chunk in range(2):
                lanes = pl.ds(start + 128 * chunk, 128)
                base = 256 + 32 * chunk
                w_kv[16 * head : 16 * head + 16, lanes] = weights[block, head, base : base + 16, :]
                w_kv[32 + 16 * head : 48 + 16 * head, lanes] = weights[
                    block, head, base + 16 : base + 32, :
                ]

    def product(x, rows):
        q = jnp.dot(x, w_q[rows, :], preferred_element_type=F32)
        kv = lax.dot_general(
            x, w_kv[:, rows], (((1,), (1,)), ((), ())), preferred_element_type=F32
        )
        return q, kv

    low, high = pl.ds(0, 1024), pl.ds(1024, 1024)
    departures = []
    for number in (0, 2, 1, 3):
        if number % 2 == 0:
            near, far = ((n1, f1), (n3, f3))[number // 2]
            q_near, kv_near = product(near[...], low)
            q_far, kv_far = product(far[...], high)
            q, kv = q_near + q_far, kv_near + kv_far
        else:
            tokens, arrivals = ((joined, first), (own, copies))[number // 3]
            for copy in arrivals:
                copy.wait()
            q, kv = product(tokens[...], pl.ds(0, 2048))
        result[number, :256, :] = q.astype(BF16)
        result[number, 256:, :] = kv.T.astype(BF16)
        other = (where_ref[1] + number + 1) % 4
        departures.append(
            pltpu.make_async_copy(result.at[number], out.at[other], out_sems.at[number])
        )
        departures[-1].start()
    for copy in departures:
        copy.wait()


def project(where, states, near, far, weights):
    return pl.pallas_call(
        project_kernel,
        out_shape=pltpu.HBM((4, 320, 256), BF16),
        in_specs=[in_smem(), *[in_hbm()] * 3, *in_vmem(5)],
        out_specs=in_hbm(),
        scratch_shapes=[
            pltpu.VMEM((TOK, 2048), BF16),
            pltpu.VMEM((TOK, 2048), BF16),
            pltpu.VMEM((2048, 256), BF16),
            pltpu.VMEM((64, 2048), BF16),
            pltpu.VMEM((4, 320, 256), BF16),
            pltpu.SemaphoreType.DMA((10,)),
            pltpu.SemaphoreType.DMA((4,)),
        ],
        compiler_params=params(),
        name="project",
    )(where, held(states), held(near[1]), held(far[1]), *near[::2], *far[::2], weights)


def attend_kernel(
    where_ref,
    mask_ref,
    risk_ref,
    parts,
    kv,
    upstream_ref,
    tables_ref,
    turned_ref,
    states_ref,
    n2_ref,
    f2_ref,
    attn_out,
    dq_out,
    own,
    n2,
    f2,
    upstream,
    tables,
    turned,
    sems,
):
    copies = [
        pltpu.make_async_copy(tables_ref, tables, sems.at[8]),
        pltpu.make_async_copy(turned_ref, turned, sems.at[9]),
        pltpu.make_async_copy(upstream_ref, upstream, sems.at[10]),
        *own_columns(where_ref, states_ref, own, sems),
        pltpu.make_async_copy(n2_ref, n2, sems.at[11]),
        pltpu.make_async_copy(f2_ref, f2, sems.at[12]),
    ]
    for copy in copies:
        copy.start()
    scaling = 1.0 / math.sqrt(HEAD)
    k_lin = jnp.concatenate([kv[s, :32, :] for s in range(4)], axis=0)
    values = jnp.concatenate([kv[s, 32:, :] for s in range(4)], axis=0).astype(BF16)

    row = lax.broadcasted_iota(jnp.int32, (BS, TOK), 0)
    column = lax.broadcasted_iota(jnp.int32, (BS, TOK), 1)
    seen, risk = [], []
    for b in range(4):
        on_path = jnp.zeros((BS, TOK), jnp.int32)
        for c in range(4):
            on_path = jnp.where(column // BS == c, mask_ref[b, c], on_path)
        seen.append(jnp.where((column // BS != b) | (column - BS * b <= row), on_path, 0))
        risk.append(jnp.full((BS, 1), risk_ref[b], F32))
    seen = jnp.concatenate(seen, axis=0) > 0
    risk = jnp.concatenate(risk, axis=0)

    copies[0].wait()
    copies[1].wait()
    half = lax.broadcasted_iota(jnp.int32, (TOK, HEAD), 1) < HEAD // 2
    table = tables[...]
    turned_table = pltpu.roll(table, HEAD // 2, 1)
    cq = jnp.where(half, table, turned_table)
    sq = jnp.where(half, -turned_table, table)
    ck, sk = turned[:64], turned[64:]
    k1, k2 = k_lin[:64], k_lin[64:]
    keys = jnp.concatenate([k1 * ck - k2 * sk, k2 * ck + k1 * sk], axis=0).astype(BF16)
    copies[2].wait()
    weighted = (upstream[...].astype(F32) * risk).astype(BF16)
    for head in range(2):
        cols = pl.ds(head * HEAD, HEAD)
        q_lin = parts[0, :256, cols].astype(F32)
        for part in range(1, 4):
            q_lin = q_lin + parts[part, :256, cols].astype(F32)
        queries = ((q_lin * cq + pltpu.roll(q_lin, 64, 1) * sq) * scaling).astype(BF16)
        scores = jnp.dot(queries, keys, preferred_element_type=F32)
        raised = jnp.where(seen, jnp.exp(scores), 0.0)
        attend = raised * (1.0 / jnp.sum(raised, axis=1, keepdims=True))
        mixed = lax.dot_general(
            attend.astype(BF16), values, (((1,), (1,)), ((), ())), preferred_element_type=F32
        )
        attn_out[:, cols] = mixed.astype(BF16)
        pressure = jnp.dot(weighted[:, HEAD * head : HEAD * head + HEAD], values, preferred_element_type=F32)
        centre = jnp.sum(attend * pressure, axis=1, keepdims=True)
        slope = (attend * (pressure - centre)).astype(BF16)
        turned_dq = (
            lax.dot_general(keys, slope, (((1,), (1,)), ((), ())), preferred_element_type=F32)
            * scaling
        )
        d1, d2 = turned_dq[:64], turned_dq[64:]
        dq_out[HEAD * head : HEAD * head + 64, :] = (d1 * ck + d2 * sk).astype(BF16)
        dq_out[HEAD * head + 64 : HEAD * head + HEAD, :] = (d2 * ck - d1 * sk).astype(BF16)
    for copy in copies[3:]:
        copy.wait()


def attend(where, block_mask, risk_weight, parts, kv, upstream, tables, turned, states, n2, f2):
    own = jax.ShapeDtypeStruct((TOK, 2048), BF16)
    part = jax.ShapeDtypeStruct((TOK, 1024), BF16)
    square = jax.ShapeDtypeStruct((TOK, 256), BF16)
    return pl.pallas_call(
        attend_kernel,
        out_shape=(square, square, own, part, part),
        in_specs=[*[in_smem()] * 3, *in_vmem(2), *[in_hbm()] * 6],
        out_specs=tuple(in_vmem(5)),
        scratch_shapes=[
            pltpu.VMEM((TOK, 256), BF16),
            pltpu.VMEM((TOK, HEAD), F32),
            pltpu.VMEM((HEAD, TOK), F32),
            pltpu.SemaphoreType.DMA((13,)),
        ],
        compiler_params=params(),
        name="attend",
    )(
        where,
        block_mask,
        risk_weight,
        parts,
        kv,
        held(upstream),
        held(tables),
        held(turned),
        held(states),
        held(n2),
        held(f2),
    )


def gradient_kernel(where_ref, own, n1, n2, n3, f1, f2, f3, slopes, out):
    core = where_ref[0]
    for part in range(8):
        cols = pl.ds(256 * (part % 4), 256)
        total = None
        for number in range(4):
            if number == 0:
                x = own[:, pl.ds(256 * part, 256)]
            else:
                x = ((n1, n2, n3) if part < 4 else (f1, f2, f3))[number - 1][:, cols]
            term = jnp.dot(slopes[(where_ref[1] + number) % 4], x, preferred_element_type=F32)
            total = term if total is None else total + term
        out[block_of(part, core)] = total.astype(BF16)


def gradient(where, own, near, far, slopes):
    return pl.pallas_call(
        gradient_kernel,
        out_shape=jax.ShapeDtypeStruct((8, 256, 256), BF16),
        in_specs=[in_smem(), *in_vmem(8)],
        compiler_params=params(),
        name="gradient",
    )(where, own, *near, *far, slopes)


def total_kernel(terms, out):
    total = terms[0].astype(F32)
    for block in range(1, 8):
        total = total + terms[block].astype(F32)
    out[...] = total.T


def add_up(terms):
    return pl.pallas_call(
        total_kernel,
        out_shape=jax.ShapeDtypeStruct((256, 256), F32),
        compiler_params=params(),
        name="add_up",
    )(terms)


def shards(states, query_weight, key_matrix, value_matrix, block_mask, risk_weight, upstream):
    place = lax.axis_index(GROUP)
    plane = lax.axis_index(("yh", "xh", "xb"))
    where = jnp.stack([lax.axis_index("c"), place, plane]).astype(jnp.int32)

    (two,) = cut(where, states, (2,))
    n2 = lax.ppermute(two, AXES, ring_pairs(2, -2))

    first, second = pack(where, query_weight, key_matrix.T, value_matrix.T, two)
    first = lax.ppermute(first, AXES, home_pairs(0))
    second = lax.ppermute(second, AXES, home_pairs(1))
    outgoing = cut(where, states, (1, 3))
    weights = copies(where, first, second, outgoing[0], n2)

    up, down = gate(outgoing, held(weights))
    n1 = lax.ppermute(down, AXES, ring_pairs(-1, -1))
    n3 = lax.ppermute(up, AXES, ring_pairs(1, 1))
    near = (n1, n2, n3)
    far = [swap_core(x) for x in near]
    weights = lax.all_to_all(weights, OTHERS, split_axis=0, concat_axis=0)

    parts = project(where, states, near, far, weights)
    parts = lax.all_to_all(parts, GROUP, split_axis=0, concat_axis=0)
    kv = jnp.sum(parts[:, 256:].astype(F32), axis=0)
    kv = lax.all_gather(kv, ("xb", "c"), axis=0, tiled=False)

    depths = jnp.sum(block_mask, axis=1) - 1
    places = (depths[:, None] * BS + jnp.arange(BS, dtype=jnp.int32)[None, :]).reshape(TOK)
    frequency = jnp.exp(
        -math.log(1000000.0) * jnp.arange(HEAD // 2, dtype=F32) * 2.0 / HEAD
    )
    angles = places.astype(F32)[:, None] * frequency[None, :]
    cosine, sine = jnp.cos(angles), jnp.sin(angles)
    tables = jnp.concatenate([cosine, sine], axis=1)
    turned = jnp.concatenate([cosine.T, sine.T], axis=0)

    attn_out, dq, own, n2, f2 = attend(
        where, block_mask, risk_weight, parts, kv, upstream, tables, turned, states, n2, far[1]
    )
    near, far = (n1, n2, n3), (far[0], f2, far[2])
    slopes = lax.all_gather(dq, GROUP, axis=0, tiled=False)
    terms = gradient(where, own, near, far, slopes)
    terms = lax.all_to_all(terms, OTHERS, split_axis=0, concat_axis=0)
    return attn_out, add_up(terms)


def solution(mesh):
    fine = Mesh(mesh.devices.reshape(SIZES), AXES)
    dp, tensor = AXES[:4], AXES[4:]
    in_specs = (
        P(dp, None),
        P(tensor, dp),
        P(tensor, dp),
        P(tensor, dp),
        P(dp, None),
        P(dp),
        P(dp, tensor),
    )
    out_specs = (P(dp, tensor), P(dp, tensor))
    return jax.shard_map(shards, mesh=fine, in_specs=in_specs, out_specs=out_specs, check_vma=False)
```

```python
import math

import jax
import jax.numpy as jnp
from jax import lax
from jax.experimental import pallas as pl
from jax.experimental.pallas import tpu as pltpu
from jax.sharding import Mesh
from jax.sharding import PartitionSpec as P

HEAD = 128
BS = 64
TOK = 256
AXES = ("zh", "zb", "yu", "yb", "yh", "xh", "xb", "c")
SIZES = (4, 2, 2, 2, 2, 2, 2, 2)
GROUP = ("yu", "yb")
OTHERS = ("zh", "zb")
F32 = jnp.float32
BF16 = jnp.bfloat16
VMEM_LIMIT = 16 * 1024 * 1024


def params():
    return pltpu.CompilerParams(vmem_limit_bytes=VMEM_LIMIT)


def resting_z(z, block):
    way = (z + 4 - block % 4) % 4
    same = 1 - ((z // 4) ^ (block // 4))
    return (z + 10 - way + same * (2 + 4 * (way // 2))) % 8


def home_pairs(turn):
    pairs = []
    for d in range(32):
        for t in range(16):
            half = (d % 2) ^ turn
            block = 4 * resting_z(d // 4, t // 2) + 2 * (t % 2) + half
            pairs.append((d * 16 + t, block * 16 + d // 2))
    return pairs


def ring_pairs(first, second):
    pairs = []
    for z in range(8):
        for y in range(8):
            for x in range(4):
                for c in range(2):
                    to = (y + (second if c else first)) % 8

                    def index(y):
                        return (4 * z + y % 4) * 16 + (y // 4) * 8 + 2 * x + c

                    pairs.append((index(y), index(to)))
    return pairs


def swap_core(value):
    return lax.ppermute(value, "c", [(0, 1), (1, 0)])


def block_of(part, core):
    return 4 * (core ^ (part // 4)) + part % 4


def column_of(block, place):
    return pl.multiple_of(1024 * block + 256 * place, 256)


def in_smem():
    return pl.BlockSpec(memory_space=pltpu.SMEM)


def in_vmem(count):
    return [pl.BlockSpec(memory_space=pltpu.VMEM)] * count


def in_hbm():
    return pl.BlockSpec(memory_space=pltpu.HBM)


def held(value):
    return pltpu.with_memory_space_constraint(value, pltpu.HBM)


def anywhere():
    return pl.BlockSpec(memory_space=pl.ANY)


def pack_kernel(where_ref, query_ref, key_ref, value_ref, first, second, query, key_t, value_t, sems):
    odd = where_ref[1] % 2
    copies = [
        pltpu.make_async_copy(query_ref, query, sems.at[0]),
        pltpu.make_async_copy(key_ref, key_t, sems.at[1]),
        pltpu.make_async_copy(value_ref, value_t, sems.at[2]),
    ]
    for copy in copies:
        copy.start()
    for copy in copies:
        copy.wait()
    for turn, out in enumerate((first, second)):
        half = odd ^ turn
        out[:256, :] = query[pl.ds(pl.multiple_of(256 * half, 256), 256), :]
        for chunk in range(2):
            lanes = pl.ds(pl.multiple_of(256 * half + 128 * chunk, 128), 128)
            base = 256 + 32 * chunk
            out[base : base + 16, :] = key_t[:, lanes]
            out[base + 16 : base + 32, :] = value_t[:, lanes]


def pack(where, query, key_t, value_t):
    part = jax.ShapeDtypeStruct((320, 128), BF16)
    return pl.pallas_call(
        pack_kernel,
        out_shape=(part, part),
        in_specs=[in_smem(), in_hbm(), in_hbm(), in_hbm()],
        out_specs=tuple(in_vmem(2)),
        scratch_shapes=[
            pltpu.VMEM((512, 128), BF16),
            pltpu.VMEM((16, 512), BF16),
            pltpu.VMEM((16, 512), BF16),
            pltpu.SemaphoreType.DMA((3,)),
        ],
        compiler_params=params(),
        name="pack_weights",
    )(where, held(query), held(key_t), held(value_t))


def cut_kernel(where_ref, states_ref, up_ref, two_ref, down_ref, own_ref, own, sems):
    core, place = where_ref[0], where_ref[1]
    copies = own_columns(where_ref, states_ref, own, sems)
    for number, out in enumerate((up_ref, two_ref, down_ref)):
        for part in range(4):
            start = column_of(block_of(part, core), (place + number + 1) % 4)
            copies.append(
                pltpu.make_async_copy(
                    states_ref.at[:, pl.ds(start, 256)],
                    out.at[:, pl.ds(256 * part, 256)],
                    sems.at[len(copies)],
                )
            )
    for copy in copies:
        copy.start()
    for copy in copies[:8]:
        copy.wait()
    keep = pltpu.make_async_copy(own, own_ref, sems.at[20])
    keep.start()
    for copy in copies[8:]:
        copy.wait()
    keep.wait()


def cut(where, states):
    part = jax.ShapeDtypeStruct((TOK, 1024), BF16)
    return pl.pallas_call(
        cut_kernel,
        out_shape=(part, part, part, pltpu.HBM((TOK, 2048), BF16)),
        in_specs=[in_smem(), in_hbm()],
        out_specs=(*in_vmem(3), in_hbm()),
        scratch_shapes=[pltpu.VMEM((TOK, 2048), BF16), pltpu.SemaphoreType.DMA((21,))],
        compiler_params=params(),
        name="cut_states",
    )(where, held(states))


def gate_kernel(*refs):
    del refs


def gate(parts, after):
    count = len(parts)
    return pl.pallas_call(
        gate_kernel,
        out_shape=tuple(jax.ShapeDtypeStruct(x.shape, x.dtype) for x in parts),
        in_specs=[anywhere()] * (count + 1),
        out_specs=tuple([anywhere()] * count),
        input_output_aliases={i: i for i in range(count)},
        compiler_params=params(),
        name="gate",
    )(*parts, after)


def own_columns(where_ref, states_ref, own, sems):
    copies = []
    for part in range(8):
        start = column_of(block_of(part, where_ref[0]), where_ref[1])
        copies.append(
            pltpu.make_async_copy(
                states_ref.at[:, pl.ds(start, 256)],
                own.at[:, pl.ds(256 * part, 256)],
                sems.at[part],
            )
        )
    return copies


def copies_kernel(where_ref, first, second, after, out, piece, sems):
    del after
    odd = where_ref[1] % 2
    piece[odd] = first[...]
    piece[1 - odd] = second[...]
    sent = [pltpu.make_async_copy(piece, out.at[i], sems.at[i]) for i in range(8)]
    for copy in sent:
        copy.start()
    for copy in sent:
        copy.wait()


def copies(where, first, second, after):
    return pl.pallas_call(
        copies_kernel,
        out_shape=pltpu.HBM((8, 2, 320, 128), BF16),
        in_specs=[in_smem(), *in_vmem(2), anywhere()],
        out_specs=in_hbm(),
        scratch_shapes=[pltpu.VMEM((2, 320, 128), BF16), pltpu.SemaphoreType.DMA((8,))],
        compiler_params=params(),
        name="weight_copies",
    )(where, first, second, after)


def project_kernel(
    where_ref,
    own_ref,
    n1,
    n2,
    n3,
    f1,
    f2,
    f3,
    weights_ref,
    out,
    own,
    weights,
    w_q,
    w_kv,
    result,
    sems,
    out_sems,
):
    core = where_ref[0]
    arrivals = []
    for part in range(8):
        block = resting_z(where_ref[2], block_of(part, core))
        arrivals.append(
            pltpu.make_async_copy(weights_ref.at[block], weights.at[part], sems.at[8 + part])
        )
    copies = [pltpu.make_async_copy(own_ref, own, sems.at[0])]
    for copy in arrivals + copies:
        copy.start()
    for part in range(8):
        arrivals[part].wait()
        start = 256 * part
        for head in range(2):
            rows, cols = pl.ds(start, 256), pl.ds(HEAD * head, HEAD)
            w_q[rows, cols] = weights[part, head, :256, :]
            for chunk in range(2):
                lanes = pl.ds(start + 128 * chunk, 128)
                base = 256 + 32 * chunk
                w_kv[16 * head : 16 * head + 16, lanes] = weights[part, head, base : base + 16, :]
                w_kv[32 + 16 * head : 48 + 16 * head, lanes] = weights[
                    part, head, base + 16 : base + 32, :
                ]

    def product(x, rows):
        q = jnp.dot(x, w_q[rows, :], preferred_element_type=F32)
        kv = lax.dot_general(
            x, w_kv[:, rows], (((1,), (1,)), ((), ())), preferred_element_type=F32
        )
        return q, kv

    low, high = pl.ds(0, 1024), pl.ds(1024, 1024)
    departures = []
    for number, (near, far) in enumerate(((n1, f1), (n2, f2), (n3, f3), (None, None))):
        if near is None:
            for copy in copies:
                copy.wait()
            q, kv = product(own[...], pl.ds(0, 2048))
        else:
            q_near, kv_near = product(near[...], low)
            q_far, kv_far = product(far[...], high)
            q, kv = q_near + q_far, kv_near + kv_far
        result[number, :256, :] = q.astype(BF16)
        result[number, 256:, :] = kv.T.astype(BF16)
        other = (where_ref[1] + number + 1) % 4
        departures.append(
            pltpu.make_async_copy(result.at[number], out.at[other], out_sems.at[number])
        )
        departures[-1].start()
    for copy in departures:
        copy.wait()


def project(where, own, near, far, weights):
    return pl.pallas_call(
        project_kernel,
        out_shape=pltpu.HBM((4, 320, 256), BF16),
        in_specs=[in_smem(), in_hbm(), *in_vmem(6), in_hbm()],
        out_specs=in_hbm(),
        scratch_shapes=[
            pltpu.VMEM((TOK, 2048), BF16),
            pltpu.VMEM((8, 2, 320, 128), BF16),
            pltpu.VMEM((2048, 256), BF16),
            pltpu.VMEM((64, 2048), BF16),
            pltpu.VMEM((4, 320, 256), BF16),
            pltpu.SemaphoreType.DMA((16,)),
            pltpu.SemaphoreType.DMA((4,)),
        ],
        compiler_params=params(),
        name="project",
    )(where, held(own), *near, *far, held(weights))


def attend_kernel(
    mask_ref,
    risk_ref,
    parts,
    kv,
    upstream_ref,
    tables_ref,
    turned_ref,
    own_ref,
    attn_out,
    dq_out,
    own,
    upstream,
    tables,
    turned,
    sems,
):
    copies = [
        pltpu.make_async_copy(tables_ref, tables, sems.at[8]),
        pltpu.make_async_copy(turned_ref, turned, sems.at[9]),
        pltpu.make_async_copy(upstream_ref, upstream, sems.at[10]),
        pltpu.make_async_copy(own_ref, own, sems.at[0]),
    ]
    for copy in copies:
        copy.start()
    scaling = 1.0 / math.sqrt(HEAD)
    k_lin = jnp.concatenate([kv[s, :32, :] for s in range(4)], axis=0).astype(F32)
    values = jnp.concatenate([kv[s, 32:, :] for s in range(4)], axis=0)

    row = lax.broadcasted_iota(jnp.int32, (BS, TOK), 0)
    column = lax.broadcasted_iota(jnp.int32, (BS, TOK), 1)
    seen, risk = [], []
    for b in range(4):
        on_path = jnp.zeros((BS, TOK), jnp.int32)
        for c in range(4):
            on_path = jnp.where(column // BS == c, mask_ref[b, c], on_path)
        seen.append(jnp.where((column // BS != b) | (column - BS * b <= row), on_path, 0))
        risk.append(jnp.full((BS, 1), risk_ref[b], F32))
    seen = jnp.concatenate(seen, axis=0) > 0
    risk = jnp.concatenate(risk, axis=0)

    copies[0].wait()
    copies[1].wait()
    half = lax.broadcasted_iota(jnp.int32, (TOK, HEAD), 1) < HEAD // 2
    table = tables[...]
    turned_table = pltpu.roll(table, HEAD // 2, 1)
    cq = jnp.where(half, table, turned_table)
    sq = jnp.where(half, -turned_table, table)
    ck, sk = turned[:64], turned[64:]
    k1, k2 = k_lin[:64], k_lin[64:]
    keys = jnp.concatenate([k1 * ck - k2 * sk, k2 * ck + k1 * sk], axis=0).astype(BF16)
    copies[2].wait()
    weighted = (upstream[...].astype(F32) * risk).astype(BF16)
    for head in range(2):
        cols = pl.ds(head * HEAD, HEAD)
        q_lin = parts[0, :256, cols].astype(F32)
        for part in range(1, 4):
            q_lin = q_lin + parts[part, :256, cols].astype(F32)
        queries = ((q_lin * cq + pltpu.roll(q_lin, 64, 1) * sq) * scaling).astype(BF16)
        scores = jnp.dot(queries, keys, preferred_element_type=F32)
        raised = jnp.where(seen, jnp.exp(scores), 0.0)
        attend = raised * (1.0 / jnp.sum(raised, axis=1, keepdims=True))
        mixed = lax.dot_general(
            attend.astype(BF16), values, (((1,), (1,)), ((), ())), preferred_element_type=F32
        )
        attn_out[:, cols] = mixed.astype(BF16)
        pressure = jnp.dot(weighted[:, HEAD * head : HEAD * head + HEAD], values, preferred_element_type=F32)
        centre = jnp.sum(attend * pressure, axis=1, keepdims=True)
        slope = (attend * (pressure - centre)).astype(BF16)
        turned_dq = (
            lax.dot_general(keys, slope, (((1,), (1,)), ((), ())), preferred_element_type=F32)
            * scaling
        )
        d1, d2 = turned_dq[:64], turned_dq[64:]
        dq_out[HEAD * head : HEAD * head + 64, :] = (d1 * ck + d2 * sk).astype(BF16)
        dq_out[HEAD * head + 64 : HEAD * head + HEAD, :] = (d2 * ck - d1 * sk).astype(BF16)
    for copy in copies[3:]:
        copy.wait()


def attend(block_mask, risk_weight, parts, kv, upstream, tables, turned, own):
    whole = jax.ShapeDtypeStruct((TOK, 2048), BF16)
    square = jax.ShapeDtypeStruct((TOK, 256), BF16)
    return pl.pallas_call(
        attend_kernel,
        out_shape=(square, square, whole),
        in_specs=[*[in_smem()] * 2, *in_vmem(2), *[in_hbm()] * 4],
        out_specs=tuple(in_vmem(3)),
        scratch_shapes=[
            pltpu.VMEM((TOK, 256), BF16),
            pltpu.VMEM((TOK, HEAD), F32),
            pltpu.VMEM((HEAD, TOK), F32),
            pltpu.SemaphoreType.DMA((11,)),
        ],
        compiler_params=params(),
        name="attend",
    )(
        block_mask,
        risk_weight,
        parts,
        kv,
        held(upstream),
        held(tables),
        held(turned),
        held(own),
    )


def gradient_kernel(where_ref, own, n1, n2, n3, f1, f2, f3, slopes, out):
    core = where_ref[0]
    for part in range(8):
        cols = pl.ds(256 * (part % 4), 256)
        total = None
        for number in range(4):
            if number == 0:
                x = own[:, pl.ds(256 * part, 256)]
            else:
                x = ((n1, n2, n3) if part < 4 else (f1, f2, f3))[number - 1][:, cols]
            term = jnp.dot(slopes[(where_ref[1] + number) % 4], x, preferred_element_type=F32)
            total = term if total is None else total + term
        out[block_of(part, core)] = total.astype(BF16)


def gradient(where, own, near, far, slopes):
    return pl.pallas_call(
        gradient_kernel,
        out_shape=jax.ShapeDtypeStruct((8, 256, 256), BF16),
        in_specs=[in_smem(), *in_vmem(8)],
        compiler_params=params(),
        name="gradient",
    )(where, own, *near, *far, slopes)


def total_kernel(terms, out):
    total = terms[0].astype(F32)
    for block in range(1, 8):
        total = total + terms[block].astype(F32)
    out[...] = total.T


def add_up(terms):
    return pl.pallas_call(
        total_kernel,
        out_shape=jax.ShapeDtypeStruct((256, 256), F32),
        compiler_params=params(),
        name="add_up",
    )(terms)


def shards(states, query_weight, key_matrix, value_matrix, block_mask, risk_weight, upstream):
    place = lax.axis_index(GROUP)
    plane = lax.axis_index(("yh", "xh", "xb"))
    where = jnp.stack([lax.axis_index("c"), place, plane]).astype(jnp.int32)

    first, second = pack(where, query_weight, key_matrix.T, value_matrix.T)
    first = lax.ppermute(first, AXES, home_pairs(0))
    second = lax.ppermute(second, AXES, home_pairs(1))
    *outgoing, own = cut(where, states)
    weights = copies(where, first, second, outgoing[0])

    (two,) = gate(outgoing[1:2], second)
    up, down = gate((outgoing[0], outgoing[2]), held(weights))
    near = (
        lax.ppermute(down, AXES, ring_pairs(-1, -1)),
        lax.ppermute(two, AXES, ring_pairs(2, -2)),
        lax.ppermute(up, AXES, ring_pairs(1, 1)),
    )
    far = [swap_core(x) for x in near]
    weights = lax.all_to_all(weights, OTHERS, split_axis=0, concat_axis=0)

    parts = project(where, own, near, far, weights)
    parts = lax.all_to_all(parts, GROUP, split_axis=0, concat_axis=0)
    kv = jnp.sum(parts[:, 256:].astype(F32), axis=0).astype(BF16)
    kv = lax.all_gather(kv, ("xb", "c"), axis=0, tiled=False)

    depths = jnp.sum(block_mask, axis=1) - 1
    places = (depths[:, None] * BS + jnp.arange(BS, dtype=jnp.int32)[None, :]).reshape(TOK)
    frequency = jnp.exp(
        -math.log(1000000.0) * jnp.arange(HEAD // 2, dtype=F32) * 2.0 / HEAD
    )
    angles = places.astype(F32)[:, None] * frequency[None, :]
    cosine, sine = jnp.cos(angles), jnp.sin(angles)
    tables = jnp.concatenate([cosine, sine], axis=1)
    turned = jnp.concatenate([cosine.T, sine.T], axis=0)

    attn_out, dq, own = attend(
        block_mask, risk_weight, parts, kv, upstream, tables, turned, own
    )
    slopes = lax.all_gather(dq, GROUP, axis=0, tiled=False)
    terms = gradient(where, own, near, far, slopes)
    terms = lax.all_to_all(terms, OTHERS, split_axis=0, concat_axis=0)
    return attn_out, add_up(terms)


def solution(mesh):
    fine = Mesh(mesh.devices.reshape(SIZES), AXES)
    dp, tensor = AXES[:4], AXES[4:]
    in_specs = (
        P(dp, None),
        P(tensor, dp),
        P(tensor, dp),
        P(tensor, dp),
        P(dp, None),
        P(dp),
        P(dp, tensor),
    )
    out_specs = (P(dp, tensor), P(dp, tensor))
    return jax.shard_map(shards, mesh=fine, in_specs=in_specs, out_specs=out_specs, check_vma=False)
```

```python
import math

import jax
import jax.numpy as jnp
from jax import lax
from jax.experimental import pallas as pl
from jax.experimental.pallas import tpu as pltpu
from jax.sharding import Mesh
from jax.sharding import PartitionSpec as P

HEAD = 128
BS = 64
TOK = 256
AXES = ("zh", "zb", "yu", "yb", "yh", "xh", "xb", "c")
SIZES = (4, 2, 2, 2, 2, 2, 2, 2)
GROUP = ("yu", "yb")
OTHERS = ("zh", "zb")
F32 = jnp.float32
BF16 = jnp.bfloat16
VMEM_LIMIT = 16 * 1024 * 1024


def params():
    return pltpu.CompilerParams(vmem_limit_bytes=VMEM_LIMIT)


def resting_z(z, block):
    way = (z + 4 - block % 4) % 4
    same = 1 - ((z // 4) ^ (block // 4))
    return (z + 10 - way + same * (2 + 4 * (way // 2))) % 8


def home_pairs(turn):
    pairs = []
    for d in range(32):
        for t in range(16):
            half = (d % 2) ^ turn
            block = 4 * resting_z(d // 4, t // 2) + 2 * (t % 2) + half
            pairs.append((d * 16 + t, block * 16 + d // 2))
    return pairs


def ring_pairs(first, second):
    pairs = []
    for z in range(8):
        for y in range(8):
            for x in range(4):
                for c in range(2):
                    to = (y + (second if c else first)) % 8

                    def index(y):
                        return (4 * z + y % 4) * 16 + (y // 4) * 8 + 2 * x + c

                    pairs.append((index(y), index(to)))
    return pairs


def swap_core(value):
    return lax.ppermute(value, "c", [(0, 1), (1, 0)])


def block_of(part, core):
    return 4 * (core ^ (part // 4)) + part % 4


def column_of(block, place):
    return pl.multiple_of(1024 * block + 256 * place, 256)


def in_smem():
    return pl.BlockSpec(memory_space=pltpu.SMEM)


def in_vmem(count):
    return [pl.BlockSpec(memory_space=pltpu.VMEM)] * count


def in_hbm():
    return pl.BlockSpec(memory_space=pltpu.HBM)


def held(value):
    return pltpu.with_memory_space_constraint(value, pltpu.HBM)


def anywhere():
    return pl.BlockSpec(memory_space=pl.ANY)


def pack_kernel(where_ref, query_ref, key_ref, value_ref, first, second, query, key_t, value_t, sems):
    odd = where_ref[1] % 2
    copies = [
        pltpu.make_async_copy(query_ref, query, sems.at[0]),
        pltpu.make_async_copy(key_ref, key_t, sems.at[1]),
        pltpu.make_async_copy(value_ref, value_t, sems.at[2]),
    ]
    for copy in copies:
        copy.start()
    for copy in copies:
        copy.wait()
    for turn, out in enumerate((first, second)):
        half = odd ^ turn
        out[:256, :] = query[pl.ds(pl.multiple_of(256 * half, 256), 256), :]
        for chunk in range(2):
            lanes = pl.ds(pl.multiple_of(256 * half + 128 * chunk, 128), 128)
            base = 256 + 32 * chunk
            out[base : base + 16, :] = key_t[:, lanes]
            out[base + 16 : base + 32, :] = value_t[:, lanes]


def pack(where, query, key_t, value_t):
    part = jax.ShapeDtypeStruct((320, 128), BF16)
    return pl.pallas_call(
        pack_kernel,
        out_shape=(part, part),
        in_specs=[in_smem(), in_hbm(), in_hbm(), in_hbm()],
        out_specs=tuple(in_vmem(2)),
        scratch_shapes=[
            pltpu.VMEM((512, 128), BF16),
            pltpu.VMEM((16, 512), BF16),
            pltpu.VMEM((16, 512), BF16),
            pltpu.SemaphoreType.DMA((3,)),
        ],
        compiler_params=params(),
        name="pack_weights",
    )(where, held(query), held(key_t), held(value_t))


def cut_kernel(where_ref, states_ref, up_ref, two_ref, down_ref, own_ref, own, sems):
    core, place = where_ref[0], where_ref[1]
    copies = own_columns(where_ref, states_ref, own, sems)
    for number, out in enumerate((up_ref, two_ref, down_ref)):
        for part in range(4):
            start = column_of(block_of(part, core), (place + number + 1) % 4)
            copies.append(
                pltpu.make_async_copy(
                    states_ref.at[:, pl.ds(start, 256)],
                    out.at[:, pl.ds(256 * part, 256)],
                    sems.at[len(copies)],
                )
            )
    for copy in copies:
        copy.start()
    for copy in copies[:8]:
        copy.wait()
    keep = pltpu.make_async_copy(own, own_ref, sems.at[20])
    keep.start()
    for copy in copies[8:]:
        copy.wait()
    keep.wait()


def cut(where, states):
    part = jax.ShapeDtypeStruct((TOK, 1024), BF16)
    return pl.pallas_call(
        cut_kernel,
        out_shape=(part, part, part, pltpu.HBM((TOK, 2048), BF16)),
        in_specs=[in_smem(), in_hbm()],
        out_specs=(*in_vmem(3), in_hbm()),
        scratch_shapes=[pltpu.VMEM((TOK, 2048), BF16), pltpu.SemaphoreType.DMA((21,))],
        compiler_params=params(),
        name="cut_states",
    )(where, held(states))


def gate_kernel(*refs):
    del refs


def gate(parts, *after, cost=0):
    count = len(parts)
    return pl.pallas_call(
        gate_kernel,
        out_shape=tuple(jax.ShapeDtypeStruct(x.shape, x.dtype) for x in parts),
        in_specs=[anywhere()] * (count + len(after)),
        out_specs=tuple([anywhere()] * count),
        input_output_aliases={i: i for i in range(count)},
        cost_estimate=pl.CostEstimate(flops=cost, bytes_accessed=0, transcendentals=0),
        compiler_params=params(),
        name="gate",
    )(*parts, *after)


def own_columns(where_ref, states_ref, own, sems):
    copies = []
    for part in range(8):
        start = column_of(block_of(part, where_ref[0]), where_ref[1])
        copies.append(
            pltpu.make_async_copy(
                states_ref.at[:, pl.ds(start, 256)],
                own.at[:, pl.ds(256 * part, 256)],
                sems.at[part],
            )
        )
    return copies


def copies_kernel(where_ref, first, second, after, out, piece, sems):
    del after
    odd = where_ref[1] % 2
    piece[odd] = first[...]
    piece[1 - odd] = second[...]
    sent = [pltpu.make_async_copy(piece, out.at[i], sems.at[i]) for i in range(8)]
    for copy in sent:
        copy.start()
    for copy in sent:
        copy.wait()


def copies(where, first, second, after):
    return pl.pallas_call(
        copies_kernel,
        out_shape=pltpu.HBM((8, 2, 320, 128), BF16),
        in_specs=[in_smem(), *in_vmem(2), anywhere()],
        out_specs=in_hbm(),
        scratch_shapes=[pltpu.VMEM((2, 320, 128), BF16), pltpu.SemaphoreType.DMA((8,))],
        compiler_params=params(),
        name="weight_copies",
    )(where, first, second, after)


def project_kernel(
    where_ref,
    own_ref,
    n1,
    n2,
    n3,
    f1,
    f2,
    f3,
    weights_ref,
    out,
    own,
    weights,
    w_q,
    w_kv,
    result,
    sems,
    out_sems,
):
    core = where_ref[0]
    arrivals = []
    for part in range(8):
        block = resting_z(where_ref[2], block_of(part, core))
        arrivals.append(
            pltpu.make_async_copy(weights_ref.at[block], weights.at[part], sems.at[8 + part])
        )
    copies = [pltpu.make_async_copy(own_ref, own, sems.at[0])]
    for copy in arrivals + copies:
        copy.start()
    for part in range(8):
        arrivals[part].wait()
        start = 256 * part
        for head in range(2):
            rows, cols = pl.ds(start, 256), pl.ds(HEAD * head, HEAD)
            w_q[rows, cols] = weights[part, head, :256, :]
            for chunk in range(2):
                lanes = pl.ds(start + 128 * chunk, 128)
                base = 256 + 32 * chunk
                w_kv[16 * head : 16 * head + 16, lanes] = weights[part, head, base : base + 16, :]
                w_kv[32 + 16 * head : 48 + 16 * head, lanes] = weights[
                    part, head, base + 16 : base + 32, :
                ]

    def product(x, rows):
        q = jnp.dot(x, w_q[rows, :], preferred_element_type=F32)
        kv = lax.dot_general(
            x, w_kv[:, rows], (((1,), (1,)), ((), ())), preferred_element_type=F32
        )
        return q, kv

    low, high = pl.ds(0, 1024), pl.ds(1024, 1024)
    departures = []
    for number, (near, far) in enumerate(((n1, f1), (n2, f2), (n3, f3), (None, None))):
        if near is None:
            for copy in copies:
                copy.wait()
            q, kv = product(own[...], pl.ds(0, 2048))
        else:
            q_near, kv_near = product(near[...], low)
            q_far, kv_far = product(far[...], high)
            q, kv = q_near + q_far, kv_near + kv_far
        result[number, :256, :] = q.astype(BF16)
        result[number, 256:, :] = kv.T.astype(BF16)
        other = (where_ref[1] + number + 1) % 4
        departures.append(
            pltpu.make_async_copy(result.at[number], out.at[other], out_sems.at[number])
        )
        departures[-1].start()
    for copy in departures:
        copy.wait()


def project(where, own, near, far, weights):
    return pl.pallas_call(
        project_kernel,
        out_shape=pltpu.HBM((4, 320, 256), BF16),
        in_specs=[in_smem(), in_hbm(), *in_vmem(6), in_hbm()],
        out_specs=in_hbm(),
        scratch_shapes=[
            pltpu.VMEM((TOK, 2048), BF16),
            pltpu.VMEM((8, 2, 320, 128), BF16),
            pltpu.VMEM((2048, 256), BF16),
            pltpu.VMEM((64, 2048), BF16),
            pltpu.VMEM((4, 320, 256), BF16),
            pltpu.SemaphoreType.DMA((16,)),
            pltpu.SemaphoreType.DMA((4,)),
        ],
        compiler_params=params(),
        name="project",
    )(where, held(own), *near, *far, held(weights))


def attend_kernel(
    mask_ref,
    risk_ref,
    parts,
    kv,
    upstream_ref,
    tables_ref,
    turned_ref,
    own_ref,
    attn_out,
    dq_out,
    own,
    upstream,
    tables,
    turned,
    sems,
):
    copies = [
        pltpu.make_async_copy(tables_ref, tables, sems.at[8]),
        pltpu.make_async_copy(turned_ref, turned, sems.at[9]),
        pltpu.make_async_copy(upstream_ref, upstream, sems.at[10]),
        pltpu.make_async_copy(own_ref, own, sems.at[0]),
    ]
    for copy in copies:
        copy.start()
    scaling = 1.0 / math.sqrt(HEAD)
    k_lin = jnp.concatenate([kv[s, :32, :] for s in range(4)], axis=0).astype(F32)
    values = jnp.concatenate([kv[s, 32:, :] for s in range(4)], axis=0)

    row = lax.broadcasted_iota(jnp.int32, (BS, TOK), 0)
    column = lax.broadcasted_iota(jnp.int32, (BS, TOK), 1)
    seen, risk = [], []
    for b in range(4):
        on_path = jnp.zeros((BS, TOK), jnp.int32)
        for c in range(4):
            on_path = jnp.where(column // BS == c, mask_ref[b, c], on_path)
        seen.append(jnp.where((column // BS != b) | (column - BS * b <= row), on_path, 0))
        risk.append(jnp.full((BS, 1), risk_ref[b], F32))
    seen = jnp.concatenate(seen, axis=0) > 0
    risk = jnp.concatenate(risk, axis=0)

    copies[0].wait()
    copies[1].wait()
    half = lax.broadcasted_iota(jnp.int32, (TOK, HEAD), 1) < HEAD // 2
    table = tables[...]
    turned_table = pltpu.roll(table, HEAD // 2, 1)
    cq = jnp.where(half, table, turned_table)
    sq = jnp.where(half, -turned_table, table)
    ck, sk = turned[:64], turned[64:]
    k1, k2 = k_lin[:64], k_lin[64:]
    keys = jnp.concatenate([k1 * ck - k2 * sk, k2 * ck + k1 * sk], axis=0).astype(BF16)
    copies[2].wait()
    weighted = (upstream[...].astype(F32) * risk).astype(BF16)
    for head in range(2):
        cols = pl.ds(head * HEAD, HEAD)
        q_lin = parts[0, :256, cols].astype(F32)
        for part in range(1, 4):
            q_lin = q_lin + parts[part, :256, cols].astype(F32)
        queries = ((q_lin * cq + pltpu.roll(q_lin, 64, 1) * sq) * scaling).astype(BF16)
        scores = jnp.dot(queries, keys, preferred_element_type=F32)
        raised = jnp.where(seen, jnp.exp(scores), 0.0)
        attend = raised * (1.0 / jnp.sum(raised, axis=1, keepdims=True))
        mixed = lax.dot_general(
            attend.astype(BF16), values, (((1,), (1,)), ((), ())), preferred_element_type=F32
        )
        attn_out[:, cols] = mixed.astype(BF16)
        pressure = jnp.dot(weighted[:, HEAD * head : HEAD * head + HEAD], values, preferred_element_type=F32)
        centre = jnp.sum(attend * pressure, axis=1, keepdims=True)
        slope = (attend * (pressure - centre)).astype(BF16)
        turned_dq = (
            lax.dot_general(keys, slope, (((1,), (1,)), ((), ())), preferred_element_type=F32)
            * scaling
        )
        d1, d2 = turned_dq[:64], turned_dq[64:]
        dq_out[HEAD * head : HEAD * head + 64, :] = (d1 * ck + d2 * sk).astype(BF16)
        dq_out[HEAD * head + 64 : HEAD * head + HEAD, :] = (d2 * ck - d1 * sk).astype(BF16)
    for copy in copies[3:]:
        copy.wait()


def attend(block_mask, risk_weight, parts, kv, upstream, tables, turned, own):
    whole = jax.ShapeDtypeStruct((TOK, 2048), BF16)
    square = jax.ShapeDtypeStruct((TOK, 256), BF16)
    return pl.pallas_call(
        attend_kernel,
        out_shape=(square, square, whole),
        in_specs=[*[in_smem()] * 2, *in_vmem(2), *[in_hbm()] * 4],
        out_specs=tuple(in_vmem(3)),
        scratch_shapes=[
            pltpu.VMEM((TOK, 256), BF16),
            pltpu.VMEM((TOK, HEAD), F32),
            pltpu.VMEM((HEAD, TOK), F32),
            pltpu.SemaphoreType.DMA((11,)),
        ],
        compiler_params=params(),
        name="attend",
    )(
        block_mask,
        risk_weight,
        parts,
        kv,
        held(upstream),
        held(tables),
        held(turned),
        held(own),
    )


def gradient_kernel(where_ref, own, n1, n2, n3, f1, f2, f3, slopes, out):
    core = where_ref[0]
    for part in range(8):
        cols = pl.ds(256 * (part % 4), 256)
        total = None
        for number in range(4):
            if number == 0:
                x = own[:, pl.ds(256 * part, 256)]
            else:
                x = ((n1, n2, n3) if part < 4 else (f1, f2, f3))[number - 1][:, cols]
            term = jnp.dot(slopes[(where_ref[1] + number) % 4], x, preferred_element_type=F32)
            total = term if total is None else total + term
        out[block_of(part, core)] = total.astype(BF16)


def gradient(where, own, near, far, slopes):
    return pl.pallas_call(
        gradient_kernel,
        out_shape=jax.ShapeDtypeStruct((8, 256, 256), BF16),
        in_specs=[in_smem(), *in_vmem(8)],
        compiler_params=params(),
        name="gradient",
    )(where, own, *near, *far, slopes)


def total_kernel(terms, out):
    total = terms[0].astype(F32)
    for block in range(1, 8):
        total = total + terms[block].astype(F32)
    out[...] = total.T


def add_up(terms):
    return pl.pallas_call(
        total_kernel,
        out_shape=jax.ShapeDtypeStruct((256, 256), F32),
        compiler_params=params(),
        name="add_up",
    )(terms)


def shards(states, query_weight, key_matrix, value_matrix, block_mask, risk_weight, upstream):
    place = lax.axis_index(GROUP)
    plane = lax.axis_index(("yh", "xh", "xb"))
    where = jnp.stack([lax.axis_index("c"), place, plane]).astype(jnp.int32)

    first, second = pack(where, query_weight, key_matrix.T, value_matrix.T)
    first = lax.ppermute(first, AXES, home_pairs(0))
    second = lax.ppermute(second, AXES, home_pairs(1))
    *outgoing, own = cut(where, states)
    weights = copies(where, first, second, outgoing[0])

    (two,) = gate(outgoing[1:2], first, second)
    up, down = gate((outgoing[0], outgoing[2]), held(weights))
    near = (
        lax.ppermute(down, AXES, ring_pairs(-1, -1)),
        lax.ppermute(two, AXES, ring_pairs(2, -2)),
        lax.ppermute(up, AXES, ring_pairs(1, 1)),
    )
    far = [swap_core(x) for x in near]
    n2, f2 = gate((near[1], far[1]), where, cost=16 * 10**9)
    near, far = (near[0], n2, near[2]), (far[0], f2, far[2])
    weights = lax.all_to_all(weights, OTHERS, split_axis=0, concat_axis=0)

    parts = project(where, own, near, far, weights)
    parts = lax.all_to_all(parts, GROUP, split_axis=0, concat_axis=0)
    kv = jnp.sum(parts[:, 256:].astype(F32), axis=0).astype(BF16)
    kv = lax.all_gather(kv, ("xb", "c"), axis=0, tiled=False)

    depths = jnp.sum(block_mask, axis=1) - 1
    places = (depths[:, None] * BS + jnp.arange(BS, dtype=jnp.int32)[None, :]).reshape(TOK)
    frequency = jnp.exp(
        -math.log(1000000.0) * jnp.arange(HEAD // 2, dtype=F32) * 2.0 / HEAD
    )
    angles = places.astype(F32)[:, None] * frequency[None, :]
    cosine, sine = jnp.cos(angles), jnp.sin(angles)
    tables = jnp.concatenate([cosine, sine], axis=1)
    turned = jnp.concatenate([cosine.T, sine.T], axis=0)

    attn_out, dq, own = attend(
        block_mask, risk_weight, parts, kv, upstream, tables, turned, own
    )
    slopes = lax.all_gather(dq, GROUP, axis=0, tiled=False)
    terms = gradient(where, own, near, far, slopes)
    terms = lax.all_to_all(terms, OTHERS, split_axis=0, concat_axis=0)
    return attn_out, add_up(terms)


def solution(mesh):
    fine = Mesh(mesh.devices.reshape(SIZES), AXES)
    dp, tensor = AXES[:4], AXES[4:]
    in_specs = (
        P(dp, None),
        P(tensor, dp),
        P(tensor, dp),
        P(tensor, dp),
        P(dp, None),
        P(dp),
        P(dp, tensor),
    )
    out_specs = (P(dp, tensor), P(dp, tensor))
    return jax.shard_map(shards, mesh=fine, in_specs=in_specs, out_specs=out_specs, check_vma=False)
```

```python
import math

import jax
import jax.numpy as jnp
from jax import lax
from jax.experimental import pallas as pl
from jax.experimental.pallas import tpu as pltpu
from jax.sharding import Mesh
from jax.sharding import PartitionSpec as P

HEAD = 128
BS = 64
TOK = 256
AXES = ("zh", "zb", "yu", "yb", "yh", "xh", "xb", "c")
SIZES = (4, 2, 2, 2, 2, 2, 2, 2)
GROUP = ("yu", "yb")
OTHERS = ("zh", "zb")
F32 = jnp.float32
BF16 = jnp.bfloat16
VMEM_LIMIT = 16 * 1024 * 1024


def params():
    return pltpu.CompilerParams(vmem_limit_bytes=VMEM_LIMIT)


def resting_z(z, block):
    way = (z + 4 - block % 4) % 4
    same = 1 - ((z // 4) ^ (block // 4))
    return (z + 10 - way + same * (2 + 4 * (way // 2))) % 8


def home_pairs(turn):
    pairs = []
    for d in range(32):
        for t in range(16):
            half = (d % 2) ^ turn
            block = 4 * resting_z(d // 4, t // 2) + 2 * (t % 2) + half
            pairs.append((d * 16 + t, block * 16 + d // 2))
    return pairs


def ring_pairs(first, second):
    pairs = []
    for z in range(8):
        for y in range(8):
            for x in range(4):
                for c in range(2):
                    to = (y + (second if c else first)) % 8

                    def index(y):
                        return (4 * z + y % 4) * 16 + (y // 4) * 8 + 2 * x + c

                    pairs.append((index(y), index(to)))
    return pairs


def swap_core(value):
    return lax.ppermute(value, "c", [(0, 1), (1, 0)])


def block_of(part, core):
    return 4 * (core ^ (part // 4)) + part % 4


def column_of(block, place):
    return pl.multiple_of(1024 * block + 256 * place, 256)


def in_smem():
    return pl.BlockSpec(memory_space=pltpu.SMEM)


def in_vmem(count):
    return [pl.BlockSpec(memory_space=pltpu.VMEM)] * count


def in_hbm():
    return pl.BlockSpec(memory_space=pltpu.HBM)


def held(value):
    return pltpu.with_memory_space_constraint(value, pltpu.HBM)


def anywhere():
    return pl.BlockSpec(memory_space=pl.ANY)


def pack_kernel(where_ref, query_ref, key_ref, value_ref, first, second, query, key_t, value_t, sems):
    odd = where_ref[1] % 2
    copies = [
        pltpu.make_async_copy(query_ref, query, sems.at[0]),
        pltpu.make_async_copy(key_ref, key_t, sems.at[1]),
        pltpu.make_async_copy(value_ref, value_t, sems.at[2]),
    ]
    for copy in copies:
        copy.start()
    for copy in copies:
        copy.wait()
    for turn, out in enumerate((first, second)):
        half = odd ^ turn
        out[:256, :] = query[pl.ds(pl.multiple_of(256 * half, 256), 256), :]
        for chunk in range(2):
            lanes = pl.ds(pl.multiple_of(256 * half + 128 * chunk, 128), 128)
            base = 256 + 32 * chunk
            out[base : base + 16, :] = key_t[:, lanes]
            out[base + 16 : base + 32, :] = value_t[:, lanes]


def pack(where, query, key_t, value_t):
    part = jax.ShapeDtypeStruct((320, 128), BF16)
    return pl.pallas_call(
        pack_kernel,
        out_shape=(part, part),
        in_specs=[in_smem(), in_hbm(), in_hbm(), in_hbm()],
        out_specs=tuple(in_vmem(2)),
        scratch_shapes=[
            pltpu.VMEM((512, 128), BF16),
            pltpu.VMEM((16, 512), BF16),
            pltpu.VMEM((16, 512), BF16),
            pltpu.SemaphoreType.DMA((3,)),
        ],
        compiler_params=params(),
        name="pack_weights",
    )(where, held(query), held(key_t), held(value_t))


def cut_kernel(where_ref, states_ref, up_ref, two_ref, down_ref, own_ref, own, sems):
    core, place = where_ref[0], where_ref[1]
    copies = own_columns(where_ref, states_ref, own, sems)
    for number, out in enumerate((up_ref, two_ref, down_ref)):
        for part in range(4):
            start = column_of(block_of(part, core), (place + number + 1) % 4)
            copies.append(
                pltpu.make_async_copy(
                    states_ref.at[:, pl.ds(start, 256)],
                    out.at[:, pl.ds(256 * part, 256)],
                    sems.at[len(copies)],
                )
            )
    for copy in copies:
        copy.start()
    for copy in copies[:8]:
        copy.wait()
    keep = pltpu.make_async_copy(own, own_ref, sems.at[20])
    keep.start()
    for copy in copies[8:]:
        copy.wait()
    keep.wait()


def cut(where, states):
    part = jax.ShapeDtypeStruct((TOK, 1024), BF16)
    return pl.pallas_call(
        cut_kernel,
        out_shape=(part, part, part, pltpu.HBM((TOK, 2048), BF16)),
        in_specs=[in_smem(), in_hbm()],
        out_specs=(*in_vmem(3), in_hbm()),
        scratch_shapes=[pltpu.VMEM((TOK, 2048), BF16), pltpu.SemaphoreType.DMA((21,))],
        compiler_params=params(),
        name="cut_states",
    )(where, held(states))


def gate_kernel(*refs):
    del refs


def gate(parts, *after, cost=0):
    count = len(parts)
    return pl.pallas_call(
        gate_kernel,
        out_shape=tuple(jax.ShapeDtypeStruct(x.shape, x.dtype) for x in parts),
        in_specs=[anywhere()] * (count + len(after)),
        out_specs=tuple([anywhere()] * count),
        input_output_aliases={i: i for i in range(count)},
        cost_estimate=pl.CostEstimate(flops=cost, bytes_accessed=0, transcendentals=0),
        compiler_params=params(),
        name="gate",
    )(*parts, *after)


def own_columns(where_ref, states_ref, own, sems):
    copies = []
    for part in range(8):
        start = column_of(block_of(part, where_ref[0]), where_ref[1])
        copies.append(
            pltpu.make_async_copy(
                states_ref.at[:, pl.ds(start, 256)],
                own.at[:, pl.ds(256 * part, 256)],
                sems.at[part],
            )
        )
    return copies


def copies_kernel(where_ref, first, second, after, out, piece, sems):
    del after
    odd = where_ref[1] % 2
    piece[odd] = first[...]
    piece[1 - odd] = second[...]
    sent = [pltpu.make_async_copy(piece, out.at[i], sems.at[i]) for i in range(8)]
    for copy in sent:
        copy.start()
    for copy in sent:
        copy.wait()


def copies(where, first, second, after):
    return pl.pallas_call(
        copies_kernel,
        out_shape=pltpu.HBM((8, 2, 320, 128), BF16),
        in_specs=[in_smem(), *in_vmem(2), anywhere()],
        out_specs=in_hbm(),
        scratch_shapes=[pltpu.VMEM((2, 320, 128), BF16), pltpu.SemaphoreType.DMA((8,))],
        compiler_params=params(),
        name="weight_copies",
    )(where, first, second, after)


def project_kernel(
    where_ref,
    own_ref,
    n1,
    n2,
    n3,
    f1,
    f2,
    f3,
    weights_ref,
    out,
    own,
    weights,
    w_q,
    w_kv,
    result,
    sems,
    out_sems,
):
    core = where_ref[0]
    arrivals = []
    for part in range(8):
        block = resting_z(where_ref[2], block_of(part, core))
        arrivals.append(
            pltpu.make_async_copy(weights_ref.at[block], weights.at[part], sems.at[8 + part])
        )
    copies = [pltpu.make_async_copy(own_ref, own, sems.at[0])]
    for copy in arrivals + copies:
        copy.start()
    for part in range(8):
        arrivals[part].wait()
        start = 256 * part
        for head in range(2):
            rows, cols = pl.ds(start, 256), pl.ds(HEAD * head, HEAD)
            w_q[rows, cols] = weights[part, head, :256, :]
            for chunk in range(2):
                lanes = pl.ds(start + 128 * chunk, 128)
                base = 256 + 32 * chunk
                w_kv[16 * head : 16 * head + 16, lanes] = weights[part, head, base : base + 16, :]
                w_kv[32 + 16 * head : 48 + 16 * head, lanes] = weights[
                    part, head, base + 16 : base + 32, :
                ]

    def product(x, rows):
        q = jnp.dot(x, w_q[rows, :], preferred_element_type=F32)
        kv = lax.dot_general(
            x, w_kv[:, rows], (((1,), (1,)), ((), ())), preferred_element_type=F32
        )
        return q, kv

    low, high = pl.ds(0, 1024), pl.ds(1024, 1024)
    departures = []
    for number, (near, far) in enumerate(((n1, f1), (n2, f2), (n3, f3), (None, None))):
        if near is None:
            for copy in copies:
                copy.wait()
            q, kv = product(own[...], pl.ds(0, 2048))
        else:
            q_near, kv_near = product(near[...], low)
            q_far, kv_far = product(far[...], high)
            q, kv = q_near + q_far, kv_near + kv_far
        result[number, :256, :] = q.astype(BF16)
        result[number, 256:, :] = kv.T.astype(BF16)
        other = (where_ref[1] + number + 1) % 4
        departures.append(
            pltpu.make_async_copy(result.at[number], out.at[other], out_sems.at[number])
        )
        departures[-1].start()
    for copy in departures:
        copy.wait()


def project(where, own, near, far, weights):
    return pl.pallas_call(
        project_kernel,
        out_shape=pltpu.HBM((4, 320, 256), BF16),
        in_specs=[in_smem(), in_hbm(), *in_vmem(6), in_hbm()],
        out_specs=in_hbm(),
        scratch_shapes=[
            pltpu.VMEM((TOK, 2048), BF16),
            pltpu.VMEM((8, 2, 320, 128), BF16),
            pltpu.VMEM((2048, 256), BF16),
            pltpu.VMEM((64, 2048), BF16),
            pltpu.VMEM((4, 320, 256), BF16),
            pltpu.SemaphoreType.DMA((16,)),
            pltpu.SemaphoreType.DMA((4,)),
        ],
        compiler_params=params(),
        name="project",
    )(where, held(own), *near, *far, held(weights))


def attend_kernel(
    mask_ref,
    risk_ref,
    parts,
    kv,
    upstream_ref,
    tables_ref,
    turned_ref,
    own_ref,
    attn_out,
    dq_out,
    own,
    upstream,
    tables,
    turned,
    sems,
):
    copies = [
        pltpu.make_async_copy(tables_ref, tables, sems.at[8]),
        pltpu.make_async_copy(turned_ref, turned, sems.at[9]),
        pltpu.make_async_copy(upstream_ref, upstream, sems.at[10]),
        pltpu.make_async_copy(own_ref, own, sems.at[0]),
    ]
    for copy in copies:
        copy.start()
    scaling = 1.0 / math.sqrt(HEAD)
    k_lin = jnp.concatenate([kv[s, :32, :] for s in range(4)], axis=0).astype(F32)
    values = jnp.concatenate([kv[s, 32:, :] for s in range(4)], axis=0)

    row = lax.broadcasted_iota(jnp.int32, (BS, TOK), 0)
    column = lax.broadcasted_iota(jnp.int32, (BS, TOK), 1)
    seen, risk = [], []
    for b in range(4):
        on_path = jnp.zeros((BS, TOK), jnp.int32)
        for c in range(4):
            on_path = jnp.where(column // BS == c, mask_ref[b, c], on_path)
        seen.append(jnp.where((column // BS != b) | (column - BS * b <= row), on_path, 0))
        risk.append(jnp.full((BS, 1), risk_ref[b], F32))
    seen = jnp.concatenate(seen, axis=0) > 0
    risk = jnp.concatenate(risk, axis=0)

    copies[0].wait()
    copies[1].wait()
    half = lax.broadcasted_iota(jnp.int32, (TOK, HEAD), 1) < HEAD // 2
    table = tables[...]
    turned_table = pltpu.roll(table, HEAD // 2, 1)
    cq = jnp.where(half, table, turned_table)
    sq = jnp.where(half, -turned_table, table)
    ck, sk = turned[:64], turned[64:]
    k1, k2 = k_lin[:64], k_lin[64:]
    keys = jnp.concatenate([k1 * ck - k2 * sk, k2 * ck + k1 * sk], axis=0).astype(BF16)
    copies[2].wait()
    weighted = (upstream[...].astype(F32) * risk).astype(BF16)
    for head in range(2):
        cols = pl.ds(head * HEAD, HEAD)
        q_lin = parts[0, :256, cols].astype(F32)
        for part in range(1, 4):
            q_lin = q_lin + parts[part, :256, cols].astype(F32)
        queries = ((q_lin * cq + pltpu.roll(q_lin, 64, 1) * sq) * scaling).astype(BF16)
        scores = jnp.dot(queries, keys, preferred_element_type=F32)
        raised = jnp.where(seen, jnp.exp(scores), 0.0)
        attend = raised * (1.0 / jnp.sum(raised, axis=1, keepdims=True))
        mixed = lax.dot_general(
            attend.astype(BF16), values, (((1,), (1,)), ((), ())), preferred_element_type=F32
        )
        attn_out[:, cols] = mixed.astype(BF16)
        pressure = jnp.dot(weighted[:, HEAD * head : HEAD * head + HEAD], values, preferred_element_type=F32)
        centre = jnp.sum(attend * pressure, axis=1, keepdims=True)
        slope = (attend * (pressure - centre)).astype(BF16)
        turned_dq = (
            lax.dot_general(keys, slope, (((1,), (1,)), ((), ())), preferred_element_type=F32)
            * scaling
        )
        d1, d2 = turned_dq[:64], turned_dq[64:]
        dq_out[HEAD * head : HEAD * head + 64, :] = (d1 * ck + d2 * sk).astype(BF16)
        dq_out[HEAD * head + 64 : HEAD * head + HEAD, :] = (d2 * ck - d1 * sk).astype(BF16)
    for copy in copies[3:]:
        copy.wait()


def attend(block_mask, risk_weight, parts, kv, upstream, tables, turned, own):
    whole = jax.ShapeDtypeStruct((TOK, 2048), BF16)
    square = jax.ShapeDtypeStruct((TOK, 256), BF16)
    return pl.pallas_call(
        attend_kernel,
        out_shape=(square, square, whole),
        in_specs=[*[in_smem()] * 2, *in_vmem(2), *[in_hbm()] * 4],
        out_specs=tuple(in_vmem(3)),
        scratch_shapes=[
            pltpu.VMEM((TOK, 256), BF16),
            pltpu.VMEM((TOK, HEAD), F32),
            pltpu.VMEM((HEAD, TOK), F32),
            pltpu.SemaphoreType.DMA((11,)),
        ],
        compiler_params=params(),
        name="attend",
    )(
        block_mask,
        risk_weight,
        parts,
        kv,
        held(upstream),
        held(tables),
        held(turned),
        held(own),
    )


def gradient_kernel(where_ref, own, n1, n2, n3, f1, f2, f3, slopes, out):
    core = where_ref[0]
    for part in range(8):
        cols = pl.ds(256 * (part % 4), 256)
        total = None
        for number in range(4):
            if number == 0:
                x = own[:, pl.ds(256 * part, 256)]
            else:
                x = ((n1, n2, n3) if part < 4 else (f1, f2, f3))[number - 1][:, cols]
            term = jnp.dot(slopes[(where_ref[1] + number) % 4], x, preferred_element_type=F32)
            total = term if total is None else total + term
        out[block_of(part, core)] = total.astype(BF16)


def gradient(where, own, near, far, slopes):
    return pl.pallas_call(
        gradient_kernel,
        out_shape=jax.ShapeDtypeStruct((8, 256, 256), BF16),
        in_specs=[in_smem(), *in_vmem(8)],
        compiler_params=params(),
        name="gradient",
    )(where, own, *near, *far, slopes)


def total_kernel(terms, out):
    total = terms[0].astype(F32)
    for block in range(1, 8):
        total = total + terms[block].astype(F32)
    out[...] = total.T


def add_up(terms):
    return pl.pallas_call(
        total_kernel,
        out_shape=jax.ShapeDtypeStruct((256, 256), F32),
        compiler_params=params(),
        name="add_up",
    )(terms)


def shards(states, query_weight, key_matrix, value_matrix, block_mask, risk_weight, upstream):
    place = lax.axis_index(GROUP)
    plane = lax.axis_index(("yh", "xh", "xb"))
    where = jnp.stack([lax.axis_index("c"), place, plane]).astype(jnp.int32)

    first, second = pack(where, query_weight, key_matrix.T, value_matrix.T)
    first = lax.ppermute(first, AXES, home_pairs(0))
    second = lax.ppermute(second, AXES, home_pairs(1))
    *outgoing, own = cut(where, states)
    weights = copies(where, first, second, outgoing[0])

    (two,) = gate(outgoing[1:2], held(weights))
    up, down = gate((outgoing[0], outgoing[2]), held(weights))
    near = (
        lax.ppermute(down, AXES, ring_pairs(-1, -1)),
        lax.ppermute(two, AXES, ring_pairs(2, -2)),
        lax.ppermute(up, AXES, ring_pairs(1, 1)),
    )
    far = [swap_core(x) for x in near]
    n2, f2 = gate((near[1], far[1]), where, cost=16 * 10**9)
    near, far = (near[0], n2, near[2]), (far[0], f2, far[2])
    weights = lax.all_to_all(weights, OTHERS, split_axis=0, concat_axis=0)

    parts = project(where, own, near, far, weights)
    parts = lax.all_to_all(parts, GROUP, split_axis=0, concat_axis=0)
    kv = jnp.sum(parts[:, 256:].astype(F32), axis=0).astype(BF16)
    kv = lax.all_gather(kv, ("xb", "c"), axis=0, tiled=False)

    depths = jnp.sum(block_mask, axis=1) - 1
    places = (depths[:, None] * BS + jnp.arange(BS, dtype=jnp.int32)[None, :]).reshape(TOK)
    frequency = jnp.exp(
        -math.log(1000000.0) * jnp.arange(HEAD // 2, dtype=F32) * 2.0 / HEAD
    )
    angles = places.astype(F32)[:, None] * frequency[None, :]
    cosine, sine = jnp.cos(angles), jnp.sin(angles)
    tables = jnp.concatenate([cosine, sine], axis=1)
    turned = jnp.concatenate([cosine.T, sine.T], axis=0)

    attn_out, dq, own = attend(
        block_mask, risk_weight, parts, kv, upstream, tables, turned, own
    )
    slopes = lax.all_gather(dq, GROUP, axis=0, tiled=False)
    terms = gradient(where, own, near, far, slopes)
    terms = lax.all_to_all(terms, OTHERS, split_axis=0, concat_axis=0)
    return attn_out, add_up(terms)


def solution(mesh):
    fine = Mesh(mesh.devices.reshape(SIZES), AXES)
    dp, tensor = AXES[:4], AXES[4:]
    in_specs = (
        P(dp, None),
        P(tensor, dp),
        P(tensor, dp),
        P(tensor, dp),
        P(dp, None),
        P(dp),
        P(dp, tensor),
    )
    out_specs = (P(dp, tensor), P(dp, tensor))
    return jax.shard_map(shards, mesh=fine, in_specs=in_specs, out_specs=out_specs, check_vma=False)
```

```python
import math

import jax
import jax.numpy as jnp
from jax import lax
from jax.experimental import pallas as pl
from jax.experimental.pallas import tpu as pltpu
from jax.sharding import Mesh
from jax.sharding import PartitionSpec as P

HEAD = 128
BS = 64
TOK = 256
AXES = ("zh", "zb", "yu", "yb", "yh", "xh", "xb", "c")
SIZES = (4, 2, 2, 2, 2, 2, 2, 2)
GROUP = ("yu", "yb")
OTHERS = ("zh", "zb")
F32 = jnp.float32
BF16 = jnp.bfloat16
VMEM_LIMIT = 16 * 1024 * 1024


def params():
    return pltpu.CompilerParams(vmem_limit_bytes=VMEM_LIMIT)


def resting_z(z, block):
    way = (z + 4 - block % 4) % 4
    same = 1 - ((z // 4) ^ (block // 4))
    return (z + 10 - way + same * (2 + 4 * (way // 2))) % 8


def home_pairs(turn):
    pairs = []
    for d in range(32):
        for t in range(16):
            half = (d % 2) ^ turn
            block = 4 * resting_z(d // 4, t // 2) + 2 * (t % 2) + half
            pairs.append((d * 16 + t, block * 16 + d // 2))
    return pairs


def ring_pairs(first, second):
    pairs = []
    for z in range(8):
        for y in range(8):
            for x in range(4):
                for c in range(2):
                    to = (y + (second if c else first)) % 8

                    def index(y):
                        return (4 * z + y % 4) * 16 + (y // 4) * 8 + 2 * x + c

                    pairs.append((index(y), index(to)))
    return pairs


def swap_core(value):
    return lax.ppermute(value, "c", [(0, 1), (1, 0)])


def block_of(part, core):
    return 4 * (core ^ (part // 4)) + part % 4


def column_of(block, place):
    return pl.multiple_of(1024 * block + 256 * place, 256)


def in_smem():
    return pl.BlockSpec(memory_space=pltpu.SMEM)


def in_vmem(count):
    return [pl.BlockSpec(memory_space=pltpu.VMEM)] * count


def in_hbm():
    return pl.BlockSpec(memory_space=pltpu.HBM)


def held(value):
    return pltpu.with_memory_space_constraint(value, pltpu.HBM)


def anywhere():
    return pl.BlockSpec(memory_space=pl.ANY)


def pack_kernel(where_ref, query_ref, key_ref, value_ref, first, second, query, key_t, value_t, sems):
    odd = where_ref[1] % 2
    copies = [
        pltpu.make_async_copy(query_ref, query, sems.at[0]),
        pltpu.make_async_copy(key_ref, key_t, sems.at[1]),
        pltpu.make_async_copy(value_ref, value_t, sems.at[2]),
    ]
    for copy in copies:
        copy.start()
    for copy in copies:
        copy.wait()
    for turn, out in enumerate((first, second)):
        half = odd ^ turn
        out[:256, :] = query[pl.ds(pl.multiple_of(256 * half, 256), 256), :]
        for chunk in range(2):
            lanes = pl.ds(pl.multiple_of(256 * half + 128 * chunk, 128), 128)
            base = 256 + 32 * chunk
            out[base : base + 16, :] = key_t[:, lanes]
            out[base + 16 : base + 32, :] = value_t[:, lanes]


def pack(where, query, key_t, value_t):
    part = jax.ShapeDtypeStruct((320, 128), BF16)
    return pl.pallas_call(
        pack_kernel,
        out_shape=(part, part),
        in_specs=[in_smem(), in_hbm(), in_hbm(), in_hbm()],
        out_specs=tuple(in_vmem(2)),
        scratch_shapes=[
            pltpu.VMEM((512, 128), BF16),
            pltpu.VMEM((16, 512), BF16),
            pltpu.VMEM((16, 512), BF16),
            pltpu.SemaphoreType.DMA((3,)),
        ],
        compiler_params=params(),
        name="pack_weights",
    )(where, held(query), held(key_t), held(value_t))


def cut_kernel(where_ref, states_ref, up_ref, two_ref, down_ref, own_ref, own, sems):
    core, place = where_ref[0], where_ref[1]
    copies = own_columns(where_ref, states_ref, own, sems)
    for number, out in enumerate((up_ref, two_ref, down_ref)):
        for part in range(4):
            start = column_of(block_of(part, core), (place + number + 1) % 4)
            copies.append(
                pltpu.make_async_copy(
                    states_ref.at[:, pl.ds(start, 256)],
                    out.at[:, pl.ds(256 * part, 256)],
                    sems.at[len(copies)],
                )
            )
    for copy in copies:
        copy.start()
    for copy in copies[:8]:
        copy.wait()
    keep = pltpu.make_async_copy(own, own_ref, sems.at[20])
    keep.start()
    for copy in copies[8:]:
        copy.wait()
    keep.wait()


def cut(where, states):
    part = jax.ShapeDtypeStruct((TOK, 1024), BF16)
    return pl.pallas_call(
        cut_kernel,
        out_shape=(part, part, part, pltpu.HBM((TOK, 2048), BF16)),
        in_specs=[in_smem(), in_hbm()],
        out_specs=(*in_vmem(3), in_hbm()),
        scratch_shapes=[pltpu.VMEM((TOK, 2048), BF16), pltpu.SemaphoreType.DMA((21,))],
        compiler_params=params(),
        name="cut_states",
    )(where, held(states))


def gate_kernel(*refs):
    del refs


def gate(parts, *after, cost=0):
    count = len(parts)
    return pl.pallas_call(
        gate_kernel,
        out_shape=tuple(jax.ShapeDtypeStruct(x.shape, x.dtype) for x in parts),
        in_specs=[anywhere()] * (count + len(after)),
        out_specs=tuple([anywhere()] * count),
        input_output_aliases={i: i for i in range(count)},
        cost_estimate=pl.CostEstimate(flops=cost, bytes_accessed=0, transcendentals=0),
        compiler_params=params(),
        name="gate",
    )(*parts, *after)


def own_columns(where_ref, states_ref, own, sems):
    copies = []
    for part in range(8):
        start = column_of(block_of(part, where_ref[0]), where_ref[1])
        copies.append(
            pltpu.make_async_copy(
                states_ref.at[:, pl.ds(start, 256)],
                own.at[:, pl.ds(256 * part, 256)],
                sems.at[part],
            )
        )
    return copies


def copies_kernel(where_ref, first, second, after, out, piece, sems):
    del after
    odd = where_ref[1] % 2
    piece[odd] = first[...]
    piece[1 - odd] = second[...]
    sent = [pltpu.make_async_copy(piece, out.at[i], sems.at[i]) for i in range(8)]
    for copy in sent:
        copy.start()
    for copy in sent:
        copy.wait()


def copies(where, first, second, after):
    return pl.pallas_call(
        copies_kernel,
        out_shape=pltpu.HBM((8, 2, 320, 128), BF16),
        in_specs=[in_smem(), *in_vmem(2), anywhere()],
        out_specs=in_hbm(),
        scratch_shapes=[pltpu.VMEM((2, 320, 128), BF16), pltpu.SemaphoreType.DMA((8,))],
        compiler_params=params(),
        name="weight_copies",
    )(where, first, second, after)


def project_kernel(
    where_ref,
    own_ref,
    n1,
    n2,
    n3,
    f1,
    f2,
    f3,
    weights_ref,
    out,
    own,
    weights,
    w_q,
    w_kv,
    result,
    sems,
    out_sems,
):
    core = where_ref[0]
    arrivals = []
    for part in range(8):
        block = resting_z(where_ref[2], block_of(part, core))
        arrivals.append(
            pltpu.make_async_copy(weights_ref.at[block], weights.at[part], sems.at[8 + part])
        )
    copies = [pltpu.make_async_copy(own_ref, own, sems.at[0])]
    for copy in arrivals + copies:
        copy.start()
    def unpack(part):
        arrivals[part].wait()
        start = 256 * part
        for head in range(2):
            rows, cols = pl.ds(start, 256), pl.ds(HEAD * head, HEAD)
            w_q[rows, cols] = weights[part, head, :256, :]
            for chunk in range(2):
                lanes = pl.ds(start + 128 * chunk, 128)
                base = 256 + 32 * chunk
                w_kv[16 * head : 16 * head + 16, lanes] = weights[part, head, base : base + 16, :]
                w_kv[32 + 16 * head : 48 + 16 * head, lanes] = weights[
                    part, head, base + 16 : base + 32, :
                ]

    def product(x, rows):
        q = jnp.dot(x, w_q[rows, :], preferred_element_type=F32)
        kv = lax.dot_general(
            x, w_kv[:, rows], (((1,), (1,)), ((), ())), preferred_element_type=F32
        )
        return q, kv

    low, high = pl.ds(0, 1024), pl.ds(1024, 1024)
    for part in range(4):
        unpack(part)
    begun = [product(near[...], low) for near in (n1, n2, n3)]
    for part in range(4, 8):
        unpack(part)
    departures = []
    for number, (near, far) in enumerate(((n1, f1), (n2, f2), (n3, f3), (None, None))):
        if near is None:
            for copy in copies:
                copy.wait()
            q, kv = product(own[...], pl.ds(0, 2048))
        else:
            q_near, kv_near = begun[number]
            q_far, kv_far = product(far[...], high)
            q, kv = q_near + q_far, kv_near + kv_far
        result[number, :256, :] = q.astype(BF16)
        result[number, 256:, :] = kv.T.astype(BF16)
        other = (where_ref[1] + number + 1) % 4
        departures.append(
            pltpu.make_async_copy(result.at[number], out.at[other], out_sems.at[number])
        )
        departures[-1].start()
    for copy in departures:
        copy.wait()


def project(where, own, near, far, weights):
    return pl.pallas_call(
        project_kernel,
        out_shape=pltpu.HBM((4, 320, 256), BF16),
        in_specs=[in_smem(), in_hbm(), *in_vmem(6), in_hbm()],
        out_specs=in_hbm(),
        scratch_shapes=[
            pltpu.VMEM((TOK, 2048), BF16),
            pltpu.VMEM((8, 2, 320, 128), BF16),
            pltpu.VMEM((2048, 256), BF16),
            pltpu.VMEM((64, 2048), BF16),
            pltpu.VMEM((4, 320, 256), BF16),
            pltpu.SemaphoreType.DMA((16,)),
            pltpu.SemaphoreType.DMA((4,)),
        ],
        compiler_params=params(),
        name="project",
    )(where, held(own), *near, *far, held(weights))


def attend_kernel(
    mask_ref,
    risk_ref,
    parts,
    kv,
    upstream_ref,
    tables_ref,
    turned_ref,
    own_ref,
    attn_out,
    dq_out,
    own,
    upstream,
    tables,
    turned,
    sems,
):
    copies = [
        pltpu.make_async_copy(tables_ref, tables, sems.at[8]),
        pltpu.make_async_copy(turned_ref, turned, sems.at[9]),
        pltpu.make_async_copy(upstream_ref, upstream, sems.at[10]),
        pltpu.make_async_copy(own_ref, own, sems.at[0]),
    ]
    for copy in copies:
        copy.start()
    scaling = 1.0 / math.sqrt(HEAD)
    k_lin = jnp.concatenate([kv[s, :32, :] for s in range(4)], axis=0).astype(F32)
    values = jnp.concatenate([kv[s, 32:, :] for s in range(4)], axis=0)

    row = lax.broadcasted_iota(jnp.int32, (BS, TOK), 0)
    column = lax.broadcasted_iota(jnp.int32, (BS, TOK), 1)
    seen, risk = [], []
    for b in range(4):
        on_path = jnp.zeros((BS, TOK), jnp.int32)
        for c in range(4):
            on_path = jnp.where(column // BS == c, mask_ref[b, c], on_path)
        seen.append(jnp.where((column // BS != b) | (column - BS * b <= row), on_path, 0))
        risk.append(jnp.full((BS, 1), risk_ref[b], F32))
    seen = jnp.concatenate(seen, axis=0) > 0
    risk = jnp.concatenate(risk, axis=0)

    copies[0].wait()
    copies[1].wait()
    half = lax.broadcasted_iota(jnp.int32, (TOK, HEAD), 1) < HEAD // 2
    table = tables[...]
    turned_table = pltpu.roll(table, HEAD // 2, 1)
    cq = jnp.where(half, table, turned_table)
    sq = jnp.where(half, -turned_table, table)
    ck, sk = turned[:64], turned[64:]
    k1, k2 = k_lin[:64], k_lin[64:]
    keys = jnp.concatenate([k1 * ck - k2 * sk, k2 * ck + k1 * sk], axis=0).astype(BF16)
    copies[2].wait()
    weighted = (upstream[...].astype(F32) * risk).astype(BF16)
    for head in range(2):
        cols = pl.ds(head * HEAD, HEAD)
        q_lin = parts[0, :256, cols].astype(F32)
        for part in range(1, 4):
            q_lin = q_lin + parts[part, :256, cols].astype(F32)
        queries = ((q_lin * cq + pltpu.roll(q_lin, 64, 1) * sq) * scaling).astype(BF16)
        scores = jnp.dot(queries, keys, preferred_element_type=F32)
        raised = jnp.where(seen, jnp.exp(scores), 0.0)
        attend = raised * (1.0 / jnp.sum(raised, axis=1, keepdims=True))
        mixed = lax.dot_general(
            attend.astype(BF16), values, (((1,), (1,)), ((), ())), preferred_element_type=F32
        )
        attn_out[:, cols] = mixed.astype(BF16)
        pressure = jnp.dot(weighted[:, HEAD * head : HEAD * head + HEAD], values, preferred_element_type=F32)
        centre = jnp.sum(attend * pressure, axis=1, keepdims=True)
        slope = (attend * (pressure - centre)).astype(BF16)
        turned_dq = (
            lax.dot_general(keys, slope, (((1,), (1,)), ((), ())), preferred_element_type=F32)
            * scaling
        )
        d1, d2 = turned_dq[:64], turned_dq[64:]
        dq_out[HEAD * head : HEAD * head + 64, :] = (d1 * ck + d2 * sk).astype(BF16)
        dq_out[HEAD * head + 64 : HEAD * head + HEAD, :] = (d2 * ck - d1 * sk).astype(BF16)
    for copy in copies[3:]:
        copy.wait()


def attend(block_mask, risk_weight, parts, kv, upstream, tables, turned, own):
    whole = jax.ShapeDtypeStruct((TOK, 2048), BF16)
    square = jax.ShapeDtypeStruct((TOK, 256), BF16)
    return pl.pallas_call(
        attend_kernel,
        out_shape=(square, square, whole),
        in_specs=[*[in_smem()] * 2, *in_vmem(2), *[in_hbm()] * 4],
        out_specs=tuple(in_vmem(3)),
        scratch_shapes=[
            pltpu.VMEM((TOK, 256), BF16),
            pltpu.VMEM((TOK, HEAD), F32),
            pltpu.VMEM((HEAD, TOK), F32),
            pltpu.SemaphoreType.DMA((11,)),
        ],
        compiler_params=params(),
        name="attend",
    )(
        block_mask,
        risk_weight,
        parts,
        kv,
        held(upstream),
        held(tables),
        held(turned),
        held(own),
    )


def gradient_kernel(where_ref, own, n1, n2, n3, f1, f2, f3, slopes, out):
    core = where_ref[0]
    for part in range(8):
        cols = pl.ds(256 * (part % 4), 256)
        total = None
        for number in range(4):
            if number == 0:
                x = own[:, pl.ds(256 * part, 256)]
            else:
                x = ((n1, n2, n3) if part < 4 else (f1, f2, f3))[number - 1][:, cols]
            term = jnp.dot(slopes[(where_ref[1] + number) % 4], x, preferred_element_type=F32)
            total = term if total is None else total + term
        out[block_of(part, core)] = total.astype(BF16)


def gradient(where, own, near, far, slopes):
    return pl.pallas_call(
        gradient_kernel,
        out_shape=jax.ShapeDtypeStruct((8, 256, 256), BF16),
        in_specs=[in_smem(), *in_vmem(8)],
        compiler_params=params(),
        name="gradient",
    )(where, own, *near, *far, slopes)


def total_kernel(terms, out):
    total = terms[0].astype(F32)
    for block in range(1, 8):
        total = total + terms[block].astype(F32)
    out[...] = total.T


def add_up(terms):
    return pl.pallas_call(
        total_kernel,
        out_shape=jax.ShapeDtypeStruct((256, 256), F32),
        compiler_params=params(),
        name="add_up",
    )(terms)


def shards(states, query_weight, key_matrix, value_matrix, block_mask, risk_weight, upstream):
    place = lax.axis_index(GROUP)
    plane = lax.axis_index(("yh", "xh", "xb"))
    where = jnp.stack([lax.axis_index("c"), place, plane]).astype(jnp.int32)

    first, second = pack(where, query_weight, key_matrix.T, value_matrix.T)
    first = lax.ppermute(first, AXES, home_pairs(0))
    second = lax.ppermute(second, AXES, home_pairs(1))
    *outgoing, own = cut(where, states)
    weights = copies(where, first, second, outgoing[0])

    (two,) = gate(outgoing[1:2], first, second)
    up, down = gate((outgoing[0], outgoing[2]), held(weights))
    near = (
        lax.ppermute(down, AXES, ring_pairs(-1, -1)),
        lax.ppermute(two, AXES, ring_pairs(2, -2)),
        lax.ppermute(up, AXES, ring_pairs(1, 1)),
    )
    far = [swap_core(x) for x in near]
    n2, f2 = gate((near[1], far[1]), where, cost=16 * 10**9)
    near, far = (near[0], n2, near[2]), (far[0], f2, far[2])
    weights = lax.all_to_all(weights, OTHERS, split_axis=0, concat_axis=0)

    parts = project(where, own, near, far, weights)
    parts = lax.all_to_all(parts, GROUP, split_axis=0, concat_axis=0)
    kv = jnp.sum(parts[:, 256:].astype(F32), axis=0).astype(BF16)
    kv = lax.all_gather(kv, ("xb", "c"), axis=0, tiled=False)

    depths = jnp.sum(block_mask, axis=1) - 1
    places = (depths[:, None] * BS + jnp.arange(BS, dtype=jnp.int32)[None, :]).reshape(TOK)
    frequency = jnp.exp(
        -math.log(1000000.0) * jnp.arange(HEAD // 2, dtype=F32) * 2.0 / HEAD
    )
    angles = places.astype(F32)[:, None] * frequency[None, :]
    cosine, sine = jnp.cos(angles), jnp.sin(angles)
    tables = jnp.concatenate([cosine, sine], axis=1)
    turned = jnp.concatenate([cosine.T, sine.T], axis=0)

    attn_out, dq, own = attend(
        block_mask, risk_weight, parts, kv, upstream, tables, turned, own
    )
    slopes = lax.all_gather(dq, GROUP, axis=0, tiled=False)
    terms = gradient(where, own, near, far, slopes)
    terms = lax.all_to_all(terms, OTHERS, split_axis=0, concat_axis=0)
    return attn_out, add_up(terms)


def solution(mesh):
    fine = Mesh(mesh.devices.reshape(SIZES), AXES)
    dp, tensor = AXES[:4], AXES[4:]
    in_specs = (
        P(dp, None),
        P(tensor, dp),
        P(tensor, dp),
        P(tensor, dp),
        P(dp, None),
        P(dp),
        P(dp, tensor),
    )
    out_specs = (P(dp, tensor), P(dp, tensor))
    return jax.shard_map(shards, mesh=fine, in_specs=in_specs, out_specs=out_specs, check_vma=False)
```
